32 devices in a mesh: sector: 8 (over y, x, core), dof: 4 (over z).
Axes of the slice: x: 2, y: 2, z: 4, core: 2. Of those that a mesh axis runs over, the one named last changes fastest.
Arguments:
- rhs: float32 [8, 4096, 128], P('sector', 'dof')
- diagonal: float32 [8, 4096], P('sector', 'dof'), may hold values from 4 to 8
- coupling: bfloat16 [8, 4096, 2048], P('sector', 'dof'), may hold values from -0.125 to 0.125
- springs: float32 [8, 3072], P('sector', 'dof'), may hold values from 1 to 4
- precond: bfloat16 [4096, 4096], P('dof')
- hub_inverse: bfloat16 [3072, 3072], P('dof')
Outputs:
- solution: float32 [8, 4096, 128], P('sector', 'dof')
- residual: float32 [8, 4096, 128], P('sector', 'dof')
The draws below stay inside these ranges and needn't reach their ends.
All inputs are finite; a program needn't handle non-finite values.
Results may differ from the reference program's by a relative error of at most 0.0056.
Values may be sent and summed in bfloat16 or wider, within the bound.
No kernel may reach another device: no remote copies, remote signals or barrier semaphores. Data moves between devices by JAX's collectives and lax.ppermute only.
A program may use at most 64 MiB of HBM per device.

```python
import math
import jax
import jax.numpy as jnp
from jax import lax

B = 4096
R = 128
ITERS = 3
SECTORS = 8
HUB = 3072
N_DOF = 4


def draw_rhs(key, part):
    first, second = jax.random.split(jax.random.fold_in(key, 11), 2)
    shared = jax.random.normal(first, (B, R), jnp.float32)
    own = jax.random.normal(second, (SECTORS, B, R), jnp.float32)
    return 0.7 * shared[None] + 0.7 * own


def dominant(key, order, scale):
    first, second = jax.random.split(key)
    spread = jax.random.normal(first, (order, order), jnp.float32)
    lead = 1.0 + 0.5 * jax.random.uniform(second, (order,), jnp.float32)
    return scale * (jnp.eye(order, dtype=jnp.float32) * lead[None, :] + 0.3 * spread / order ** 0.5)


def draw_precond(key, part):
    return dominant(jax.random.fold_in(key, 23), B, 1.0 / 6.0).astype(jnp.bfloat16)


def draw_hub_inverse(key, part):
    return dominant(jax.random.fold_in(key, 37), HUB, 1.0 / SECTORS).astype(jnp.bfloat16)


def steps_of(stream_key, extent, shards, least, top_value):
    factor_of = 1.0
    for axis_at, blocks in shards:
        steps = jax.random.uniform(jax.random.fold_in(jax.random.fold_in(stream_key, 6), axis_at), (blocks,), jnp.float32, least / len(shards), top_value / len(shards))
        factor_of = factor_of * jnp.repeat(jnp.exp(steps), extent[axis_at] // blocks).reshape((-1,) + (1,) * (len(extent) - 1 - axis_at))
    return factor_of


def noise(stream_key, shape, width, bound, cuts=(), held_as=jnp.bfloat16):
    array = width * jax.random.normal(stream_key, shape, jnp.float32)
    if cuts:
        array = array * steps_of(stream_key, shape, cuts, -0.22, 0.18)
    return jnp.clip(array, -bound, bound).astype(held_as)


def setup_inputs(seed: int = 0) -> dict:
    streams_of = jax.random.split(jax.random.key(seed), 7)
    return {
        "rhs": draw_rhs(jax.random.fold_in(streams_of[6], 71), 0),
        "diagonal": jnp.clip(4.0 + 4.0 * jax.random.uniform(streams_of[1], (SECTORS, B), jnp.float32) ** steps_of(streams_of[1], (SECTORS, B), ((0, 8), (1, 4)), -0.2, 0.2), 4.0, 8.0),
        "coupling": noise(streams_of[2], (SECTORS, B, B // 2), (B // 2) ** -0.5, 0.125, ((0, 8), (1, 4))),
        "springs": jnp.clip(jnp.exp(math.log(4.0) - 1.3862944 * jax.random.uniform(streams_of[3], (SECTORS, HUB), jnp.float32) ** steps_of(streams_of[3], (SECTORS, HUB), ((0, 8), (1, 4)), -0.2, 0.2)), 1.0, 4.0),
        "precond": draw_precond(jax.random.fold_in(streams_of[6], 71), 0),
        "hub_inverse": draw_hub_inverse(jax.random.fold_in(streams_of[6], 71), 0),
    }


def reference(rhs, diagonal, coupling, springs, precond, hub_inverse):
    rows_dev = B // N_DOF
    quarter = rows_dev // 4

    def apply_pre(field):
        field_low = field.astype(jnp.bfloat16)
        return lax.map(lambda block: jnp.dot(precond, block, preferred_element_type=jnp.float32), field_low)

    def apply_op(field):
        split = field.reshape(SECTORS, N_DOF, rows_dev, R)
        split_low = split.astype(jnp.bfloat16)
        prev_right = jnp.roll(split_low[:, :, quarter:2 * quarter], 1, axis=0)
        next_left = jnp.roll(split_low[:, :, :quarter], -1, axis=0)
        inter = jnp.concatenate([prev_right, next_left], axis=2).reshape(SECTORS, B // 2, R)
        couple = lax.map(lambda pair: jnp.dot(pair[0], pair[1], preferred_element_type=jnp.float32), (coupling, inter))
        spring_rows = springs.reshape(SECTORS, N_DOF, 3 * quarter)[..., None]
        attached = split[:, :, :3 * quarter]
        load = jnp.sum(spring_rows * attached, axis=0).reshape(HUB, R).astype(jnp.bfloat16)
        hub = jnp.dot(hub_inverse, load, preferred_element_type=jnp.float32).reshape(N_DOF, 3 * quarter, R)
        hub_term = spring_rows * (attached - hub[None])
        hub_term = jnp.concatenate([hub_term, jnp.zeros((SECTORS, N_DOF, quarter, R), jnp.float32)], axis=2)
        return diagonal[..., None] * field + couple + hub_term.reshape(SECTORS, B, R)

    solution = jnp.zeros_like(rhs)
    residual = rhs
    for step in range(ITERS):
        precon = apply_pre(residual)
        image = apply_op(precon)
        upper = jnp.sum(image * residual, axis=(0, 1))
        lower = jnp.sum(image * image, axis=(0, 1))
        alpha = upper / (lower + 1e-6)
        solution = solution + alpha * precon
        residual = residual - alpha * image
    return solution, residual
```

```python
import jax
import jax.numpy as jnp
from jax import lax
from jax.sharding import PartitionSpec as P

ITERS = 3


def from_ahead(cells, axis, distance):
    count = lax.axis_size(axis)
    return lax.ppermute(cells, axis, [((i + distance) % count, i) for i in range(count)])


def all_pieces(cells, axis):
    return [cells] + [from_ahead(cells, axis, d) for d in range(1, lax.axis_size(axis))]


def in_order(pieces, axis):
    count = len(pieces)
    stacked = jnp.stack(pieces + pieces[:-1])
    start = (count - lax.axis_index(axis)) % count
    placed = lax.dynamic_slice_in_dim(stacked, start, count, axis=0)
    return placed


def gathered(cells, axis):
    placed = in_order(all_pieces(cells, axis), axis)
    return placed.reshape((-1,) + cells.shape[1:])


def scattered_sum(cells, axis):
    count = lax.axis_size(axis)
    part = cells.shape[0] // count
    me = lax.axis_index(axis)
    total = None
    for d in range(count):
        target = (me + d) % count
        piece = lax.dynamic_slice_in_dim(cells, target * part, part, axis=0)
        if d:
            piece = from_ahead(piece, axis, count - d)
        piece = piece.astype(jnp.float32)
        total = piece if total is None else total + piece
    return total


def summed(cells, axis):
    return sum(all_pieces(cells, axis)[1:], cells)


def beside_faces(own_faces, quarter):
    sectors, parts = lax.axis_size("sector"), lax.axis_size("dof")
    both = []
    for step, cells in ((-1, own_faces[quarter:]), (1, own_faces[:quarter])):
        pieces = []
        for d in range(parts):
            perm = [
                (((s + step) % sectors) * parts + (z + d) % parts, s * parts + z)
                for s in range(sectors)
                for z in range(parts)
            ]
            pieces.append(lax.ppermute(cells, ("sector", "dof"), perm))
        both.append(in_order(pieces, "dof"))
    return jnp.stack(both, axis=1)


def body(rhs, diagonal, coupling, springs, precond, hub_inverse):
    residual = rhs[0]
    diag_rows = diagonal[0][:, None]
    couple_rows = coupling[0]
    spring_rows = springs[0][:, None]
    rows_dev, loads = residual.shape
    quarter = rows_dev // 4
    solution = jnp.zeros_like(residual)

    def precondition(field):
        return jnp.dot(
            precond,
            gathered(field.astype(jnp.bfloat16), "dof"),
            preferred_element_type=jnp.float32,
        )

    precon = precondition(residual)
    for step in range(ITERS):
        own_faces = precon[: 2 * quarter].astype(jnp.bfloat16)
        needed = beside_faces(own_faces, quarter).reshape(-1, loads)
        attached = precon[: 3 * quarter]
        load = (spring_rows * attached).astype(jnp.bfloat16).T
        load = scattered_sum(load, "sector").astype(jnp.bfloat16)
        load = in_order(all_pieces(load, "dof"), "dof")
        load = load.transpose(0, 2, 1).reshape(-1, load.shape[1])
        hub = jnp.dot(hub_inverse, load, preferred_element_type=jnp.float32)
        hub = gathered(hub.T, "sector").T
        couple = jnp.dot(couple_rows, needed, preferred_element_type=jnp.float32)
        hub_term = jnp.concatenate(
            [spring_rows * (attached - hub), jnp.zeros((quarter, loads), jnp.float32)], axis=0
        )
        image = diag_rows * precon + couple + hub_term
        sums = jnp.stack([jnp.sum(image * residual, axis=0), jnp.sum(image * image, axis=0)])
        sums = summed(summed(sums, "sector"), "dof")
        alpha = sums[0] / (sums[1] + 1e-06)
        solution = solution + alpha * precon
        residual = residual - alpha * image
        if step < ITERS - 1:
            precon = precon - alpha * precondition(image)
    return (solution[None], residual[None])


def solution(mesh):
    placed = (
        P("sector", "dof", None),
        P("sector", "dof"),
        P("sector", "dof", None),
        P("sector", "dof"),
        P("dof", None),
        P("dof", None),
    )
    return jax.shard_map(
        body,
        mesh=mesh,
        in_specs=placed,
        out_specs=(P("sector", "dof", None), P("sector", "dof", None)),
        check_vma=False,
    )
```

```python
import jax
import jax.numpy as jnp
from jax import lax
from jax.sharding import PartitionSpec as P

ITERS = 3


def gathered(cells, axis):
    return lax.all_gather(cells, axis, axis=0, tiled=True)


def scattered_sum(cells, axis):
    count = lax.axis_size(axis)
    parts = cells.reshape((count, -1) + cells.shape[1:])
    parts = lax.all_to_all(parts, axis, split_axis=0, concat_axis=0)
    return jnp.sum(parts.astype(jnp.float32), axis=0)


def summed(cells, axes):
    count = lax.axis_size(axes)
    parts = jnp.broadcast_to(cells[None], (count,) + cells.shape)
    return jnp.sum(lax.all_to_all(parts, axes, split_axis=0, concat_axis=0), axis=0)


def beside_faces(own_faces, quarter):
    sectors = lax.axis_size("sector")
    before = lax.ppermute(
        own_faces[quarter:], "sector", [(s, (s + 1) % sectors) for s in range(sectors)]
    )
    after = lax.ppermute(
        own_faces[:quarter], "sector", [((s + 1) % sectors, s) for s in range(sectors)]
    )
    return gathered(jnp.concatenate([before, after]), "dof")


def body(rhs, diagonal, coupling, springs, precond, hub_inverse):
    residual = rhs[0]
    diag_rows = diagonal[0][:, None]
    couple_rows = coupling[0]
    spring_rows = springs[0][:, None]
    rows_dev, loads = residual.shape
    quarter = rows_dev // 4
    solution = jnp.zeros_like(residual)

    def precondition(field):
        return jnp.dot(
            precond,
            gathered(field.astype(jnp.bfloat16), "dof"),
            preferred_element_type=jnp.float32,
        )

    precon = precondition(residual)
    for step in range(ITERS):
        own_faces = precon[: 2 * quarter].astype(jnp.bfloat16)
        needed = beside_faces(own_faces, quarter)
        attached = precon[: 3 * quarter]
        load = (spring_rows * attached).astype(jnp.bfloat16).T
        load = scattered_sum(load, "sector").astype(jnp.bfloat16)
        load = lax.all_gather(load, "dof", axis=0)
        load = load.transpose(0, 2, 1).reshape(-1, load.shape[1])
        hub = jnp.dot(hub_inverse, load, preferred_element_type=jnp.float32)
        hub = gathered(hub.T, "sector").T
        couple = jnp.dot(couple_rows, needed, preferred_element_type=jnp.float32)
        hub_term = jnp.concatenate(
            [spring_rows * (attached - hub), jnp.zeros((quarter, loads), jnp.float32)], axis=0
        )
        image = diag_rows * precon + couple + hub_term
        sums = jnp.stack([jnp.sum(image * residual, axis=0), jnp.sum(image * image, axis=0)])
        sums = summed(sums, ("sector", "dof"))
        alpha = sums[0] / (sums[1] + 1e-06)
        solution = solution + alpha * precon
        residual = residual - alpha * image
        if step < ITERS - 1:
            precon = precon - alpha * precondition(image)
    return (solution[None], residual[None])


def solution(mesh):
    placed = (
        P("sector", "dof", None),
        P("sector", "dof"),
        P("sector", "dof", None),
        P("sector", "dof"),
        P("dof", None),
        P("dof", None),
    )
    return jax.shard_map(
        body,
        mesh=mesh,
        in_specs=placed,
        out_specs=(P("sector", "dof", None), P("sector", "dof", None)),
        check_vma=False,
    )
```

```python
import jax
import jax.numpy as jnp
from jax import lax
from jax.sharding import PartitionSpec as P

ITERS = 3


def gathered(cells, axis):
    return lax.all_gather(cells, axis, axis=0, tiled=True)


def scattered_sum(cells, axis):
    count = lax.axis_size(axis)
    parts = cells.reshape((count, -1) + cells.shape[1:])
    parts = lax.all_to_all(parts, axis, split_axis=0, concat_axis=0)
    return jnp.sum(parts.astype(jnp.float32), axis=0)


def every_piece(cells, axes):
    count = lax.axis_size(axes)
    parts = jnp.broadcast_to(cells[None], (count,) + cells.shape)
    return lax.all_to_all(parts, axes, split_axis=0, concat_axis=0)


def beside_faces(own_faces, quarter):
    sectors = lax.axis_size("sector")
    before = lax.ppermute(
        own_faces[quarter:], "sector", [(s, (s + 1) % sectors) for s in range(sectors)]
    )
    after = lax.ppermute(
        own_faces[:quarter], "sector", [((s + 1) % sectors, s) for s in range(sectors)]
    )
    sides = every_piece(jnp.concatenate([before, after]), "dof")
    return sides.reshape(-1, own_faces.shape[1])


def body(rhs, diagonal, coupling, springs, precond, hub_inverse):
    residual = rhs[0]
    diag_rows = diagonal[0][:, None]
    couple_rows = coupling[0]
    spring_rows = springs[0][:, None]
    rows_dev, loads = residual.shape
    quarter = rows_dev // 4
    solution = jnp.zeros_like(residual)

    def precondition(field):
        return jnp.dot(
            precond,
            gathered(field.astype(jnp.bfloat16), "dof"),
            preferred_element_type=jnp.float32,
        )

    precon = precondition(residual)
    for step in range(ITERS):
        own_faces = precon[: 2 * quarter].astype(jnp.bfloat16)
        needed = beside_faces(own_faces, quarter)
        attached = precon[: 3 * quarter]
        load = (spring_rows * attached).astype(jnp.bfloat16).T
        load = scattered_sum(load, "sector").astype(jnp.bfloat16)
        load = every_piece(load, "dof")
        load = load.transpose(0, 2, 1).reshape(-1, load.shape[1])
        hub = jnp.dot(hub_inverse, load, preferred_element_type=jnp.float32)
        hub = every_piece(hub.T, "sector").reshape(loads, -1).T
        couple = jnp.dot(couple_rows, needed, preferred_element_type=jnp.float32)
        hub_term = jnp.concatenate(
            [spring_rows * (attached - hub), jnp.zeros((quarter, loads), jnp.float32)], axis=0
        )
        image = diag_rows * precon + couple + hub_term
        sums = jnp.stack([jnp.sum(image * residual, axis=0), jnp.sum(image * image, axis=0)])
        sums = jnp.sum(every_piece(sums, ("sector", "dof")), axis=0)
        alpha = sums[0] / (sums[1] + 1e-06)
        solution = solution + alpha * precon
        residual = residual - alpha * image
        if step < ITERS - 1:
            precon = precon - alpha * precondition(image)
    return (solution[None], residual[None])


def solution(mesh):
    placed = (
        P("sector", "dof", None),
        P("sector", "dof"),
        P("sector", "dof", None),
        P("sector", "dof"),
        P("dof", None),
        P("dof", None),
    )
    return jax.shard_map(
        body,
        mesh=mesh,
        in_specs=placed,
        out_specs=(P("sector", "dof", None), P("sector", "dof", None)),
        check_vma=False,
    )
```

```python
import functools

import jax
import jax.numpy as jnp
from jax import lax
from jax.experimental import pallas as pl
from jax.experimental.pallas import tpu as pltpu
from jax.sharding import PartitionSpec as P

ITERS = 3
VMEM_LIMIT = 32 * 1024 * 1024


def every_piece(cells, axes):
    count = lax.axis_size(axes)
    parts = jnp.broadcast_to(cells[None], (count,) + cells.shape)
    return lax.all_to_all(parts, axes, split_axis=0, concat_axis=0)


def product_kernel(first, matrix_ref, field_ref, *refs):
    if first:
        (out_ref,) = refs
    else:
        before_ref, sums_ref, out_ref = refs
    step = pl.program_id(0)
    product = jnp.dot(matrix_ref[...], field_ref[...], preferred_element_type=jnp.float32)

    @pl.when(step == 0)
    def _():
        out_ref[...] = product

    @pl.when(step > 0)
    def _():
        out_ref[...] += product

    if not first:

        @pl.when(step == pl.num_programs(0) - 1)
        def _():
            sums = jnp.sum(sums_ref[...], axis=0)
            alpha = sums[0:1] / (sums[1:2] + 1e-06)
            out_ref[...] = before_ref[...] - alpha * out_ref[...]


def preconditioned(matrix, field, before=None, sums=None):
    rows, depth = matrix.shape
    loads = field.shape[1]
    block = min(512, depth)
    first = before is None
    extra = [] if first else [before, sums]
    extra_specs = [pl.BlockSpec(a.shape, functools.partial(lambda n, k: (0,) * n, a.ndim)) for a in extra]
    return pl.pallas_call(
        functools.partial(product_kernel, first),
        grid=(depth // block,),
        in_specs=[
            pl.BlockSpec((rows, block), lambda k: (0, k)),
            pl.BlockSpec((block, loads), lambda k: (k, 0)),
        ]
        + extra_specs,
        out_specs=pl.BlockSpec((rows, loads), lambda k: (0, 0)),
        out_shape=jax.ShapeDtypeStruct((rows, loads), jnp.float32),
        compiler_params=pltpu.CompilerParams(vmem_limit_bytes=VMEM_LIMIT),
        cost_estimate=pl.CostEstimate(
            flops=2 * rows * depth * loads,
            bytes_accessed=2 * depth * (rows + loads) + 8 * rows * loads,
            transcendentals=0,
        ),
    )(matrix, field, *extra)


def send_kernel(precon_ref, springs_ref, before_ref, after_ref, faces_ref, load_ref):
    quarter = before_ref.shape[0]
    faces_ref[:quarter] = before_ref[...]
    faces_ref[quarter : 2 * quarter] = after_ref[...]
    faces_ref[2 * quarter :] = jnp.zeros_like(faces_ref[2 * quarter :])
    attached = precon_ref[: 3 * quarter]
    load_ref[...] = (attached.T * springs_ref[...]).astype(load_ref.dtype)


def faces_and_load(precon, springs, before, after):
    rows, loads = precon.shape
    return pl.pallas_call(
        send_kernel,
        out_shape=(
            jax.ShapeDtypeStruct((rows, loads), jnp.bfloat16),
            jax.ShapeDtypeStruct((loads, springs.shape[1]), jnp.bfloat16),
        ),
        compiler_params=pltpu.CompilerParams(vmem_limit_bytes=VMEM_LIMIT),
    )(precon, springs, before, after)


def hub_kernel(matrix_ref, load_ref, out_ref, total_ref):
    step = pl.program_id(0)
    product = lax.dot_general(
        load_ref[0], matrix_ref[...], (((1,), (1,)), ((), ())), preferred_element_type=jnp.float32
    )

    @pl.when(step == 0)
    def _():
        total_ref[...] = product

    @pl.when(step > 0)
    def _():
        total_ref[...] += product

    @pl.when(step == pl.num_programs(0) - 1)
    def _():
        out_ref[...] = jnp.broadcast_to(total_ref[...][None], out_ref.shape)


def hub_copies(matrix, load, count):
    parts, cases, depth = load.shape
    rows = matrix.shape[0]
    if depth % 128 or cases % 16:
        load = load.transpose(1, 0, 2).reshape(cases, -1)
        hub = lax.dot_general(
            load, matrix, (((1,), (1,)), ((), ())), preferred_element_type=jnp.float32
        )
        return jnp.broadcast_to(hub[None], (count,) + hub.shape)
    return pl.pallas_call(
        hub_kernel,
        grid=(parts,),
        in_specs=[
            pl.BlockSpec((rows, depth), lambda k: (0, k)),
            pl.BlockSpec((1, cases, depth), lambda k: (k, 0, 0)),
        ],
        out_specs=pl.BlockSpec((count, cases, rows), lambda k: (0, 0, 0)),
        out_shape=jax.ShapeDtypeStruct((count, cases, rows), jnp.float32),
        scratch_shapes=[pltpu.VMEM((cases, rows), jnp.float32)],
        compiler_params=pltpu.CompilerParams(vmem_limit_bytes=VMEM_LIMIT),
        cost_estimate=pl.CostEstimate(
            flops=2 * rows * depth * parts * cases,
            bytes_accessed=2 * rows * depth * parts,
            transcendentals=0,
        ),
    )(matrix, load)


def body(rhs, diagonal, coupling, springs, precond, hub_inverse):
    residual = rhs[0]
    diag_rows = diagonal[0][:, None]
    couple_rows = coupling[0]
    spring_rows = springs[0][:, None]
    rows_dev, loads = residual.shape
    quarter = rows_dev // 4
    sectors = lax.axis_size("sector")
    onward = [(s, (s + 1) % sectors) for s in range(sectors)]
    backward = [((s + 1) % sectors, s) for s in range(sectors)]
    solution = jnp.zeros_like(residual)

    def gathered(field):
        return lax.all_gather(field.astype(jnp.bfloat16), "dof", axis=0)

    precon = preconditioned(precond, gathered(residual).reshape(-1, loads))
    for step in range(ITERS):
        own_faces = precon[: 2 * quarter].astype(jnp.bfloat16)
        before = lax.ppermute(own_faces[quarter:], "sector", onward)
        after = lax.ppermute(own_faces[:quarter], "sector", backward)
        faces, load = faces_and_load(precon, springs, before, after)
        needed = gathered(faces)[:, : 2 * quarter].reshape(-1, loads)

        load = load.reshape(sectors, loads // sectors, -1)
        load = lax.all_to_all(load, "sector", split_axis=0, concat_axis=0)
        load = jnp.sum(load.astype(jnp.float32), axis=0).astype(jnp.bfloat16)
        hub = hub_copies(hub_inverse, every_piece(load, "dof"), sectors)
        hub = lax.all_to_all(hub, "sector", split_axis=0, concat_axis=0)
        hub = hub.reshape(loads, -1).T

        couple = jnp.dot(couple_rows, needed, preferred_element_type=jnp.float32)
        attached = precon[: 3 * quarter]
        hub_term = jnp.concatenate(
            [spring_rows * (attached - hub), jnp.zeros((quarter, loads), jnp.float32)], axis=0
        )
        image = diag_rows * precon + couple + hub_term
        sums = jnp.stack([jnp.sum(image * residual, axis=0), jnp.sum(image * image, axis=0)])
        sums = every_piece(sums, ("sector", "dof"))
        total = jnp.sum(sums, axis=0)
        alpha = total[0] / (total[1] + 1e-06)
        solution = solution + alpha * precon
        residual = residual - alpha * image
        if step < ITERS - 1:
            precon = preconditioned(precond, gathered(image).reshape(-1, loads), precon, sums)
    return (solution[None], residual[None])


def solution(mesh):
    placed = (
        P("sector", "dof", None),
        P("sector", "dof"),
        P("sector", "dof", None),
        P("sector", "dof"),
        P("dof", None),
        P("dof", None),
    )
    return jax.shard_map(
        body,
        mesh=mesh,
        in_specs=placed,
        out_specs=(P("sector", "dof", None), P("sector", "dof", None)),
        check_vma=False,
    )
```

```python
import functools

import jax
import jax.numpy as jnp
from jax import lax
from jax.experimental import pallas as pl
from jax.experimental.pallas import tpu as pltpu
from jax.sharding import PartitionSpec as P

ITERS = 3
LANES = 128
VMEM_LIMIT = 30 * 1024 * 1024
WHOLE = pl.BlockSpec(memory_space=pltpu.VMEM)
UNREAD = pl.BlockSpec(memory_space=pl.ANY)
f32 = jnp.float32
bf16 = jnp.bfloat16


def call(kernel, outs, operands, unread=0, scratch=(), flops=0, traffic=0):
    count = len(operands)
    return pl.pallas_call(
        kernel,
        in_specs=[WHOLE] * (count - unread) + [UNREAD] * unread,
        out_specs=jax.tree.map(lambda _: WHOLE, outs),
        out_shape=outs,
        scratch_shapes=list(scratch),
        compiler_params=pltpu.CompilerParams(vmem_limit_bytes=VMEM_LIMIT),
        cost_estimate=pl.CostEstimate(flops=flops, bytes_accessed=traffic, transcendentals=0),
    )(*operands)


def shape(*dims, dtype=f32):
    return jax.ShapeDtypeStruct(dims, dtype)


def product_kernel(matrix_ref, tops_ref, ends_ref, *refs):
    before_ref, sums_ref, out_ref = refs if len(refs) == 3 else (None, None, refs[0])
    parts, top, _ = tops_ref.shape
    end = ends_ref.shape[1]
    out_ref[...] = jnp.zeros_like(out_ref)

    @pl.loop(0, parts)
    def _(part):
        start = pl.multiple_of(part * (top + end), LANES)
        out_ref[...] += jnp.dot(
            matrix_ref[:, pl.ds(start, top)], tops_ref[part], preferred_element_type=f32
        ) + jnp.dot(
            matrix_ref[:, pl.ds(pl.multiple_of(start + top, LANES), end)],
            ends_ref[part],
            preferred_element_type=f32,
        )

    if before_ref is not None:
        sums = jnp.sum(sums_ref[...], axis=0)
        alpha = sums[0:1] / (sums[1:2] + 1e-06)
        out_ref[...] = before_ref[...] - alpha * out_ref[...]


def preconditioned(matrix, tops, ends, *before_and_sums):
    rows, depth = matrix.shape
    loads = tops.shape[2]
    return call(
        product_kernel,
        shape(rows, loads),
        (matrix, tops, ends, *before_and_sums),
        flops=2 * rows * depth * loads,
        traffic=2 * depth * (rows + loads),
    )


def send_kernel(precon_ref, springs_ref, load_ref, right_ref, left_ref):
    sectors, height, _ = load_ref.shape
    cases = precon_ref.shape[1] // sectors
    quarter = right_ref.shape[0]
    left_ref[...] = precon_ref[:quarter].astype(bf16)
    right_ref[...] = precon_ref[quarter : 2 * quarter].astype(bf16)
    for at in range(height // cases):
        rows = precon_ref[at * LANES : (at + 1) * LANES]
        turned = (rows.T * springs_ref[:, at * LANES : (at + 1) * LANES]).astype(bf16)
        for s in range(sectors):
            load_ref[s, at * cases : (at + 1) * cases] = turned[s * cases : (s + 1) * cases]


def pack_kernel(before_ref, after_ref, parts_ref, out_ref):
    quarter = before_ref.shape[0]
    out_ref[:quarter] = before_ref[...]
    out_ref[quarter : 2 * quarter] = after_ref[...]
    out_ref[2 * quarter :] = jnp.sum(parts_ref[...].astype(f32), axis=0).astype(bf16)


def hub_kernel(cases, matrix_ref, pieces_ref, out_ref):
    parts = pieces_ref.shape[0]
    height = out_ref.shape[1]
    chunks = height // cases
    depth = chunks * LANES
    first = pieces_ref.shape[1] - height
    total = None
    for part in range(parts):
        load = jnp.concatenate(
            [pieces_ref[part, first + c * cases : first + (c + 1) * cases] for c in range(chunks)],
            axis=1,
        )
        product = lax.dot_general(
            load,
            matrix_ref[:, part * depth : (part + 1) * depth],
            (((1,), (1,)), ((), ())),
            preferred_element_type=f32,
        )
        total = product if total is None else total + product
    total = total.astype(bf16)
    for c in range(chunks):
        block = total[:, c * LANES : (c + 1) * LANES]
        for s in range(out_ref.shape[0]):
            out_ref[s, c * cases : (c + 1) * cases] = block


def base_kernel(matrix_ref, pieces_ref, precon_ref, stiffness_ref, base_ref, end_ref):
    parts = pieces_ref.shape[0]
    depth = matrix_ref.shape[1] // parts
    base_ref[...] = stiffness_ref[...] * precon_ref[...]

    @pl.loop(0, parts)
    def _(part):
        start = pl.multiple_of(part * depth, LANES)
        base_ref[...] += jnp.dot(
            matrix_ref[:, pl.ds(start, depth)], pieces_ref[part, :depth], preferred_element_type=f32
        )

    end = end_ref.shape[0]
    end_ref[...] = base_ref[base_ref.shape[0] - end :].astype(bf16)


def image_kernel(base_ref, hubs_ref, springs_ref, residual_ref, _, image_ref, top_ref, sums_ref):
    sectors, height, _ = hubs_ref.shape
    attached, loads = top_ref.shape
    chunks = attached // LANES
    cases = height // chunks
    for c in range(chunks):
        at = slice(c * LANES, (c + 1) * LANES)
        hub = jnp.concatenate([hubs_ref[s, c * cases : (c + 1) * cases] for s in range(sectors)], axis=0)
        pull = (hub.astype(f32) * springs_ref[:, at]).T
        image = base_ref[at] - pull
        image_ref[at] = image
        top_ref[at] = image.astype(bf16)
    image_ref[attached:] = base_ref[attached:]
    image = image_ref[...]
    upper = jnp.sum(image * residual_ref[...], axis=0, keepdims=True)
    lower = jnp.sum(image * image, axis=0, keepdims=True)
    sums = jnp.concatenate([upper, lower], axis=0)
    sums_ref[...] = jnp.broadcast_to(sums[None], sums_ref.shape)


def exchange(blocks, axes):
    return lax.all_to_all(blocks, axes, split_axis=0, concat_axis=0)


def gathered(field):
    return lax.all_gather(field, "dof", axis=0)


def around(sectors):
    onward = [(s, (s + 1) % sectors) for s in range(sectors)]
    return onward, [(b, a) for a, b in onward]


def alpha_of(sums):
    total = jnp.sum(sums, axis=0)
    return total[0] / (total[1] + 1e-06)


def round_kernel(field_ref, _, out_ref):
    out_ref[...] = field_ref[...].astype(bf16)


def tiled_body(rhs, diagonal, coupling, springs, precond, hub_inverse):
    residual = rhs[0]
    rows, loads = residual.shape
    attached = springs.shape[1]
    quarter = rows - attached
    sectors, parts = lax.axis_size("sector"), lax.axis_size("dof")
    cases = loads // sectors
    height = attached // LANES * cases
    onward, backward = around(sectors)

    stiffness = diagonal[0] + jnp.pad(springs[0], (0, quarter))
    stiffness = jnp.broadcast_to(stiffness[:, None], (rows, loads))
    solution = jnp.zeros_like(residual)

    ends = gathered(residual[attached:].astype(bf16))
    top = call(round_kernel, shape(attached, loads, dtype=bf16), (residual[:attached], ends), unread=1)
    precon = preconditioned(precond, gathered(top), ends)
    for step in range(ITERS):
        load, right, left = call(
            send_kernel,
            (
                shape(sectors, height, LANES, dtype=bf16),
                shape(quarter, loads, dtype=bf16),
                shape(quarter, loads, dtype=bf16),
            ),
            (precon, springs),
        )
        before = lax.ppermute(right, "sector", onward)
        after = lax.ppermute(left, "sector", backward)
        packed = call(
            pack_kernel,
            shape(2 * quarter + height, loads, dtype=bf16),
            (before, after, exchange(load, "sector")),
        )
        pieces = gathered(packed)
        hub = call(
            functools.partial(hub_kernel, cases),
            shape(sectors, height, LANES, dtype=bf16),
            (hub_inverse, pieces),
            flops=2 * hub_inverse.size * cases,
            traffic=2 * hub_inverse.size,
        )
        hubs = exchange(hub, "sector")
        base, end = call(
            base_kernel,
            (shape(rows, loads), shape(quarter, loads, dtype=bf16)),
            (coupling[0], pieces, precon, stiffness),
            flops=2 * coupling.size * loads,
            traffic=2 * coupling.size,
        )
        last = step == ITERS - 1
        ends = end if last else gathered(end)
        image, top, sums = call(
            image_kernel,
            (
                shape(rows, loads),
                shape(attached, loads, dtype=bf16),
                shape(sectors * parts, 2, loads),
            ),
            (base, hubs, springs, residual, ends),
            unread=1,
        )
        sums = exchange(sums, ("sector", "dof"))
        alpha = alpha_of(sums)
        solution = solution + alpha * precon
        residual = residual - alpha * image
        if not last:
            precon = preconditioned(precond, gathered(top), ends, precon, sums)
    return (solution[None], residual[None])


def plain_body(rhs, diagonal, coupling, springs, precond, hub_inverse):
    residual = rhs[0]
    spring_rows = springs[0][:, None]
    rows, loads = residual.shape
    quarter = rows // 4
    sectors = lax.axis_size("sector")
    onward, backward = around(sectors)
    solution = jnp.zeros_like(residual)

    def whole(field):
        return gathered(field.astype(bf16)).reshape(-1, loads)

    def copies(cells, axes):
        count = lax.axis_size(axes)
        return exchange(jnp.broadcast_to(cells[None], (count,) + cells.shape), axes)

    precon = jnp.dot(precond, whole(residual), preferred_element_type=f32)
    for step in range(ITERS):
        faces = precon[: 2 * quarter].astype(bf16)
        before = lax.ppermute(faces[quarter:], "sector", onward)
        after = lax.ppermute(faces[:quarter], "sector", backward)
        couple = jnp.dot(
            coupling[0], whole(jnp.concatenate([before, after])), preferred_element_type=f32
        )
        attached = precon[: 3 * quarter]
        load = (spring_rows * attached).T.reshape(sectors, loads // sectors, -1)
        load = jnp.sum(exchange(load, "sector"), axis=0).astype(bf16)
        load = copies(load, "dof").transpose(0, 2, 1).reshape(hub_inverse.shape[1], -1)
        hub = jnp.dot(hub_inverse, load, preferred_element_type=f32)
        hub = copies(hub.T, "sector").reshape(loads, -1).T
        pull = jnp.pad(spring_rows * (attached - hub), ((0, quarter), (0, 0)))
        image = diagonal[0][:, None] * precon + couple + pull
        sums = jnp.stack([jnp.sum(image * residual, axis=0), jnp.sum(image * image, axis=0)])
        alpha = alpha_of(copies(sums, ("sector", "dof")))
        solution = solution + alpha * precon
        residual = residual - alpha * image
        if step < ITERS - 1:
            change = jnp.dot(precond, whole(image), preferred_element_type=f32)
            precon = precon - alpha * change
    return (solution[None], residual[None])


def body(rhs, *rest):
    rows, loads = rhs.shape[1:]
    cases = loads // lax.axis_size("sector")
    tiled = loads == LANES and (rows // 4) % LANES == 0 and cases % 16 == 0
    return (tiled_body if tiled else plain_body)(rhs, *rest)


def solution(mesh):
    placed = (
        P("sector", "dof", None),
        P("sector", "dof"),
        P("sector", "dof", None),
        P("sector", "dof"),
        P("dof", None),
        P("dof", None),
    )
    return jax.shard_map(
        body,
        mesh=mesh,
        in_specs=placed,
        out_specs=(P("sector", "dof", None), P("sector", "dof", None)),
        check_vma=False,
    )
```

```python
import functools

import jax
import jax.numpy as jnp
from jax import lax
from jax.experimental import pallas as pl
from jax.experimental.pallas import tpu as pltpu
from jax.sharding import PartitionSpec as P

ITERS = 3
LANES = 128
MIB = 1024 * 1024
WHOLE = pl.BlockSpec(memory_space=pltpu.VMEM)
UNREAD = pl.BlockSpec(memory_space=pl.ANY)
f32 = jnp.float32
bf16 = jnp.bfloat16


def shape(*dims, dtype=f32):
    return jax.ShapeDtypeStruct(dims, dtype)


def call(kernel, outs, operands, streamed=False, unread=0, flops=0):
    matrix = operands[0]
    specs = [WHOLE] * (len(operands) - unread) + [UNREAD] * unread
    scratch = []
    if streamed:
        specs[0] = pl.BlockSpec(memory_space=pltpu.HBM)
        scratch = [pltpu.VMEM(matrix.shape, matrix.dtype), pltpu.SemaphoreType.DMA((streamed,))]
    return pl.pallas_call(
        kernel,
        in_specs=specs,
        out_specs=jax.tree.map(lambda _: WHOLE, outs),
        out_shape=outs,
        scratch_shapes=scratch,
        compiler_params=pltpu.CompilerParams(vmem_limit_bytes=(60 if streamed else 16) * MIB),
        cost_estimate=pl.CostEstimate(
            flops=flops, bytes_accessed=sum(x.size * x.dtype.itemsize for x in operands), transcendentals=0
        ),
    )(*operands)


def columns(parts, width, source, buffer, sems):
    copies = []
    for part in range(parts):
        at = (slice(None), pl.ds(part * width, width))
        copy = pltpu.make_async_copy(source.at[at], buffer.at[at], sems.at[part])
        copy.start()
        copies.append((copy, at))

    def block(part):
        copy, at = copies[part]
        copy.wait()
        return buffer[at]

    return block


def product_kernel(change, matrix_ref, springs_ref, *refs):
    *refs, out_ref, load_ref, right_ref, left_ref, buffer, sems = refs
    field_refs = refs[:-2] if change else refs
    parts = field_refs[0].shape[0]
    count = len(field_refs)
    block = columns(parts * count, field_refs[0].shape[1], matrix_ref, buffer, sems)
    for part in range(parts):
        for at, ref in enumerate(field_refs):
            product = jnp.dot(block(part * count + at), ref[part], preferred_element_type=f32)
            if part + at == 0:
                out_ref[...] = product
            else:
                out_ref[...] += product
    if change:
        before_ref, alpha_ref = refs[-2:]
        out_ref[...] = before_ref[...] - alpha_ref[0:1] * out_ref[...]

    sectors, height, _ = load_ref.shape
    cases = out_ref.shape[1] // sectors
    quarter = right_ref.shape[0]
    left_ref[...] = out_ref[:quarter].astype(bf16)
    right_ref[...] = out_ref[quarter : 2 * quarter].astype(bf16)
    for at in range(height // cases):
        rows = slice(at * LANES, (at + 1) * LANES)
        turned = out_ref[rows].T * springs_ref[:, rows]
        for s in range(sectors):
            load_ref[s, at * cases : (at + 1) * cases] = turned[s * cases : (s + 1) * cases]


def preconditioned(sectors, matrix, springs, fields, *before_and_alpha):
    rows, depth = matrix.shape
    parts, _, loads = fields[0].shape
    attached = springs.shape[1]
    height = attached // LANES * (loads // sectors)
    face = shape(rows - attached, loads, dtype=bf16)
    return call(
        functools.partial(product_kernel, bool(before_and_alpha)),
        (shape(rows, loads), shape(sectors, height, LANES), face, face),
        (matrix, springs, *fields, *before_and_alpha),
        streamed=parts * len(fields),
        flops=2 * rows * depth * loads,
    )


def pack_kernel(before_ref, after_ref, parts_ref, out_ref):
    quarter = before_ref.shape[0]
    out_ref[:quarter] = before_ref[...]
    out_ref[quarter : 2 * quarter] = after_ref[...]
    out_ref[2 * quarter :] = jnp.sum(parts_ref[...], axis=0).astype(bf16)


def hub_kernel(cases, matrix_ref, pieces_ref, out_ref, buffer, sems):
    parts = pieces_ref.shape[0]
    height = out_ref.shape[1]
    chunks = height // cases
    depth = chunks * LANES
    first = pieces_ref.shape[1] - height
    matrix_block = columns(parts, depth, matrix_ref, buffer, sems)
    total = None
    for part in range(parts):
        load = jnp.concatenate(
            [pieces_ref[part, first + c * cases : first + (c + 1) * cases] for c in range(chunks)],
            axis=1,
        )
        product = lax.dot_general(
            load,
            matrix_block(part),
            (((1,), (1,)), ((), ())),
            preferred_element_type=f32,
        )
        total = product if total is None else total + product
    for c in range(chunks):
        block = total[:, c * LANES : (c + 1) * LANES]
        for s in range(out_ref.shape[0]):
            out_ref[s, c * cases : (c + 1) * cases] = block


def base_kernel(matrix_ref, pieces_ref, precon_ref, stiffness_ref, base_ref, buffer, sems):
    parts = pieces_ref.shape[0]
    depth = matrix_ref.shape[1] // parts
    block = columns(parts, depth, matrix_ref, buffer, sems)
    base_ref[...] = stiffness_ref[...] * precon_ref[...]
    for part in range(parts):
        base_ref[...] += jnp.dot(block(part), pieces_ref[part, :depth], preferred_element_type=f32)


def image_kernel(base_ref, hubs_ref, springs_ref, residual_ref, image_ref, low_ref, sums_ref):
    sectors, height, _ = hubs_ref.shape
    attached = springs_ref.shape[1]
    chunks = attached // LANES
    cases = height // chunks
    for c in range(chunks):
        at = slice(c * LANES, (c + 1) * LANES)
        hub = jnp.concatenate([hubs_ref[s, c * cases : (c + 1) * cases] for s in range(sectors)], axis=0)
        image_ref[at] = base_ref[at] - (hub * springs_ref[:, at]).T
    image_ref[attached:] = base_ref[attached:]
    image = image_ref[...]
    low_ref[...] = image.astype(bf16)
    upper = jnp.sum(image * residual_ref[...], axis=0, keepdims=True)
    lower = jnp.sum(image * image, axis=0, keepdims=True)
    sums = jnp.concatenate([upper, lower], axis=0)
    sums_ref[...] = jnp.broadcast_to(sums[None], sums_ref.shape)


def step_kernel(sums_ref, precon_ref, image_ref, solution_ref, residual_ref, alpha_ref, newer_ref, left_ref):
    sums = jnp.sum(sums_ref[...], axis=0)
    alpha = sums[0:1] / (sums[1:2] + 1e-06)
    alpha_ref[...] = jnp.broadcast_to(alpha, alpha_ref.shape)
    newer_ref[...] = solution_ref[...] + alpha * precon_ref[...]
    left_ref[...] = residual_ref[...] - alpha * image_ref[...]


def halves_kernel(field_ref, upper_ref, lower_ref):
    half = upper_ref.shape[0]
    upper_ref[...] = field_ref[0, :half].astype(bf16)
    lower_ref[...] = field_ref[0, half:].astype(bf16)


def after_kernel(field_ref, _, out_ref):
    out_ref[...] = field_ref[...]


def exchange(blocks, axes):
    return lax.all_to_all(blocks, axes, split_axis=0, concat_axis=0)


def gathered(field):
    return lax.all_gather(field, "dof", axis=0)


def around(sectors):
    onward = [(s, (s + 1) % sectors) for s in range(sectors)]
    return onward, [(b, a) for a, b in onward]


def alpha_of(sums):
    total = jnp.sum(sums, axis=0)
    return total[0] / (total[1] + 1e-06)


def tiled_body(rhs, diagonal, coupling, springs, precond, hub_inverse):
    residual = rhs[0]
    rows, loads = residual.shape
    attached = springs.shape[1]
    quarter = rows - attached
    sectors, parts = lax.axis_size("sector"), lax.axis_size("dof")
    cases = loads // sectors
    height = attached // LANES * cases
    onward, backward = around(sectors)

    stiffness = diagonal[0] + jnp.pad(springs[0], (0, quarter))
    stiffness = jnp.broadcast_to(stiffness[:, None], (rows, loads))
    solution = jnp.zeros_like(residual)

    half = shape(rows // 2, loads, dtype=bf16)
    upper, lower = call(halves_kernel, (half, half), (rhs,))
    upper = gathered(upper)
    lower = gathered(call(after_kernel, half, (lower, upper), unread=1))
    precon, load, right, left = preconditioned(sectors, precond, springs, (upper, lower))
    for step in range(ITERS):
        before = lax.ppermute(right, "sector", onward)
        after = lax.ppermute(left, "sector", backward)
        packed = call(
            pack_kernel,
            shape(2 * quarter + height, loads, dtype=bf16),
            (before, after, exchange(load, "sector")),
        )
        pieces = gathered(packed)
        hub = call(
            functools.partial(hub_kernel, cases),
            shape(sectors, height, LANES),
            (hub_inverse, pieces),
            streamed=parts,
            flops=2 * hub_inverse.size * cases,
        )
        hubs = exchange(hub, "sector")
        base = call(
            base_kernel,
            shape(rows, loads),
            (coupling[0], pieces, precon, stiffness),
            streamed=parts,
            flops=2 * coupling.size * loads,
        )
        image, low, sums = call(
            image_kernel,
            (shape(rows, loads), shape(rows, loads, dtype=bf16), shape(sectors * parts, 2, loads)),
            (base, hubs, springs, residual),
        )
        sums = exchange(sums, ("sector", "dof"))
        alpha, solution, residual = call(
            step_kernel,
            (shape(8, loads), shape(rows, loads), shape(rows, loads)),
            (sums, precon, image, solution, residual),
        )
        if step < ITERS - 1:
            precon, load, right, left = preconditioned(
                sectors, precond, springs, (gathered(low),), precon, alpha
            )
    return (solution[None], residual[None])


def plain_body(rhs, diagonal, coupling, springs, precond, hub_inverse):
    residual = rhs[0]
    spring_rows = springs[0][:, None]
    rows, loads = residual.shape
    quarter = rows // 4
    sectors = lax.axis_size("sector")
    onward, backward = around(sectors)
    solution = jnp.zeros_like(residual)

    def whole(field):
        return gathered(field.astype(bf16)).reshape(-1, loads)

    def copies(cells, axes):
        count = lax.axis_size(axes)
        return exchange(jnp.broadcast_to(cells[None], (count,) + cells.shape), axes)

    precon = jnp.dot(precond, whole(residual), preferred_element_type=f32)
    for step in range(ITERS):
        faces = precon[: 2 * quarter].astype(bf16)
        before = lax.ppermute(faces[quarter:], "sector", onward)
        after = lax.ppermute(faces[:quarter], "sector", backward)
        couple = jnp.dot(
            coupling[0], whole(jnp.concatenate([before, after])), preferred_element_type=f32
        )
        attached = precon[: 3 * quarter]
        load = (spring_rows * attached).T.reshape(sectors, loads // sectors, -1)
        load = jnp.sum(exchange(load, "sector"), axis=0).astype(bf16)
        load = copies(load, "dof").transpose(0, 2, 1).reshape(hub_inverse.shape[1], -1)
        hub = jnp.dot(hub_inverse, load, preferred_element_type=f32)
        hub = copies(hub.T, "sector").reshape(loads, -1).T
        pull = jnp.pad(spring_rows * (attached - hub), ((0, quarter), (0, 0)))
        image = diagonal[0][:, None] * precon + couple + pull
        sums = jnp.stack([jnp.sum(image * residual, axis=0), jnp.sum(image * image, axis=0)])
        alpha = alpha_of(copies(sums, ("sector", "dof")))
        solution = solution + alpha * precon
        residual = residual - alpha * image
        if step < ITERS - 1:
            change = jnp.dot(precond, whole(image), preferred_element_type=f32)
            precon = precon - alpha * change
    return (solution[None], residual[None])


def body(rhs, *rest):
    rows, loads = rhs.shape[1:]
    cases = loads // lax.axis_size("sector")
    tiled = loads == LANES and (rows // 4) % LANES == 0 and cases % 16 == 0
    return (tiled_body if tiled else plain_body)(rhs, *rest)


def solution(mesh):
    placed = (
        P("sector", "dof", None),
        P("sector", "dof"),
        P("sector", "dof", None),
        P("sector", "dof"),
        P("dof", None),
        P("dof", None),
    )
    return jax.shard_map(
        body,
        mesh=mesh,
        in_specs=placed,
        out_specs=(P("sector", "dof", None), P("sector", "dof", None)),
        check_vma=False,
    )
```

```python
import functools

import jax
import jax.numpy as jnp
from jax import lax
from jax.experimental import pallas as pl
from jax.experimental.pallas import tpu as pltpu
from jax.sharding import PartitionSpec as P

ITERS = 3
LANES = 128
MIB = 1024 * 1024
IN_FLIGHT = 3
SUM_ROWS = 8
WHOLE = pl.BlockSpec(memory_space=pltpu.VMEM)
f32 = jnp.float32
bf16 = jnp.bfloat16


def shape(*dims, dtype=f32):
    return jax.ShapeDtypeStruct(dims, dtype)


def call(kernel, outs, operands, parts=0, flops=0):
    matrix = operands[0]
    specs = [WHOLE] * len(operands)
    scratch = []
    if parts:
        specs[0] = pl.BlockSpec(memory_space=pltpu.HBM)
        scratch = [pltpu.VMEM(matrix.shape, matrix.dtype), pltpu.SemaphoreType.DMA((parts,))]
    return pl.pallas_call(
        kernel,
        in_specs=specs,
        out_specs=jax.tree.map(lambda _: WHOLE, outs),
        out_shape=outs,
        scratch_shapes=scratch,
        compiler_params=pltpu.CompilerParams(vmem_limit_bytes=(60 if parts else 16) * MIB),
        cost_estimate=pl.CostEstimate(
            flops=flops, bytes_accessed=sum(x.size * x.dtype.itemsize for x in operands), transcendentals=0
        ),
    )(*operands)


def columns(widths, source, buffer, sems):
    copies = []
    start = 0
    for at, width in enumerate(widths):
        block = (slice(None), pl.ds(start, width))
        copies.append((pltpu.make_async_copy(source.at[block], buffer.at[block], sems.at[at]), block))
        start += width
    for copy, _ in copies[:IN_FLIGHT]:
        copy.start()

    def block(at):
        copy, columns_at = copies[at]
        copy.wait()
        if at + IN_FLIGHT < len(copies):
            copies[at + IN_FLIGHT][0].start()
        return buffer[columns_at]

    return block


def product_kernel(matrix_ref, springs_ref, sums_ref, *refs):
    *field_refs, out_ref, load_ref, right_ref, left_ref, buffer, sems = refs
    count = len(field_refs)
    parts = field_refs[0].shape[0]
    block = columns([ref.shape[1] for ref in field_refs] * parts, matrix_ref, buffer, sems)
    for at in range(parts * count):
        field = field_refs[at % count][at // count]
        product = jnp.dot(block(at), field, preferred_element_type=f32)
        if at == 0:
            out_ref[...] = product
        else:
            out_ref[...] += product

    sectors, height, _ = load_ref.shape
    cases = out_ref.shape[1] // sectors
    quarter = right_ref.shape[0]
    left_ref[...] = out_ref[:quarter].astype(bf16)
    right_ref[...] = out_ref[quarter : 2 * quarter].astype(bf16)
    for at in range((height - SUM_ROWS) // cases):
        rows = slice(at * LANES, (at + 1) * LANES)
        turned = out_ref[rows].T * springs_ref[:, rows]
        for s in range(sectors):
            load_ref[s, at * cases : (at + 1) * cases] = turned[s * cases : (s + 1) * cases]
    for s in range(sectors):
        load_ref[s, height - SUM_ROWS :] = sums_ref[...]


def pack_kernel(before_ref, after_ref, parts_ref, out_ref):
    quarter = before_ref.shape[0]
    height = parts_ref.shape[1] - SUM_ROWS
    out_ref[:quarter] = before_ref[...]
    out_ref[quarter : 2 * quarter] = after_ref[...]
    total = jnp.sum(parts_ref[...], axis=0)
    out_ref[2 * quarter : 2 * quarter + height] = total[:height].astype(bf16)
    rest = total[height:]
    terms = []
    for _ in range(3):
        term = rest.astype(bf16)
        terms.append(term.astype(f32))
        rest = rest - terms[-1]
    terms.append(jnp.zeros_like(rest))
    out_ref[2 * quarter + height :] = jnp.concatenate(terms, axis=0).astype(bf16)


def alpha_from(sums):
    return sums[0:1] / (sums[1:2] + 1e-06)


def hub_kernel(cases, matrix_ref, pieces_ref, out_ref, buffer, sems):
    parts = pieces_ref.shape[0]
    height = out_ref.shape[1]
    chunks = height // cases
    depth = chunks * LANES
    first = pieces_ref.shape[1] - 4 * SUM_ROWS - height
    block = columns([depth] * parts, matrix_ref, buffer, sems)
    total = None
    for part in range(parts):
        load = jnp.concatenate(
            [pieces_ref[part, first + c * cases : first + (c + 1) * cases] for c in range(chunks)],
            axis=1,
        )
        product = lax.dot_general(
            load, block(part), (((1,), (1,)), ((), ())), preferred_element_type=f32
        )
        total = product if total is None else total + product
    for c in range(chunks):
        for s in range(out_ref.shape[0]):
            out_ref[s, c * cases : (c + 1) * cases] = total[:, c * LANES : (c + 1) * LANES]


def base_kernel(first, matrix_ref, pieces_ref, product_ref, stiffness_ref, *refs):
    if first:
        base_ref, ends_ref, factor_ref, buffer, sems = refs
    else:
        image_ref, residual_ref, precon_ref, solution_ref, *refs = refs
        base_ref, ends_ref, factor_ref, left_ref, newer_ref, better_ref, buffer, sems = refs
    parts = pieces_ref.shape[0]
    depth = matrix_ref.shape[1] // parts
    block = columns([depth] * parts, matrix_ref, buffer, sems)
    base_ref[...] = stiffness_ref[...] * product_ref[...]
    for part in range(parts):
        base_ref[...] += jnp.dot(block(part), pieces_ref[part, :depth], preferred_element_type=f32)
    if first:
        factor_ref[...] = jnp.ones_like(factor_ref)
    else:
        sums = None
        height = pieces_ref.shape[1]
        for part in range(parts):
            terms = pieces_ref[part, height - 4 * SUM_ROWS :].astype(f32)
            terms = terms[:SUM_ROWS] + terms[SUM_ROWS : 2 * SUM_ROWS] + terms[2 * SUM_ROWS : 3 * SUM_ROWS]
            sums = terms if sums is None else sums + terms
        alpha = alpha_from(sums)
        factor_ref[...] = jnp.broadcast_to(-alpha, factor_ref.shape)
        base_ref[...] = image_ref[...] - alpha * base_ref[...]
        left_ref[...] = residual_ref[...] - alpha * image_ref[...]
        better_ref[...] = solution_ref[...] + alpha * precon_ref[...]
        newer_ref[...] = precon_ref[...] - alpha * product_ref[...]
    end = base_ref[base_ref.shape[0] - ends_ref.shape[1] :].astype(bf16)
    ends_ref[...] = jnp.broadcast_to(end[None], ends_ref.shape)


def image_kernel(base_ref, hubs_ref, springs_ref, factor_ref, residual_ref, image_ref, top_ref, sums_ref):
    sectors, height, _ = hubs_ref.shape
    attached = top_ref.shape[0]
    chunks = attached // LANES
    cases = height // chunks
    factor = factor_ref[0:1]
    for c in range(chunks):
        at = slice(c * LANES, (c + 1) * LANES)
        hub = jnp.concatenate([hubs_ref[s, c * cases : (c + 1) * cases] for s in range(sectors)], axis=0)
        image = base_ref[at] - factor * (hub * springs_ref[:, at]).T
        image_ref[at] = image
        top_ref[at] = image.astype(bf16)
    image_ref[attached:] = base_ref[attached:]
    image = image_ref[...]
    upper = jnp.sum(image * residual_ref[...], axis=0, keepdims=True)
    lower = jnp.sum(image * image, axis=0, keepdims=True)
    rest = jnp.zeros((SUM_ROWS - 2, image.shape[1]), f32)
    sums = jnp.concatenate([upper, lower, rest], axis=0)
    sums_ref[...] = jnp.broadcast_to(sums[None], sums_ref.shape)


def last_kernel(sums_ref, precon_ref, image_ref, solution_ref, residual_ref, newer_ref, left_ref):
    alpha = alpha_from(jnp.sum(sums_ref[...], axis=0))
    newer_ref[0] = solution_ref[...] + alpha * precon_ref[...]
    left_ref[0] = residual_ref[...] - alpha * image_ref[...]


def round_kernel(field_ref, top_ref, ends_ref):
    attached = top_ref.shape[0]
    top_ref[...] = field_ref[0, :attached].astype(bf16)
    end = field_ref[0, attached:].astype(bf16)
    ends_ref[...] = jnp.broadcast_to(end[None], ends_ref.shape)


def exchange(blocks, axes):
    return lax.all_to_all(blocks, axes, split_axis=0, concat_axis=0)


def gathered(field):
    return lax.all_gather(field, "dof", axis=0)


def around(sectors):
    onward = [(s, (s + 1) % sectors) for s in range(sectors)]
    return onward, [(b, a) for a, b in onward]


def alpha_of(sums):
    return alpha_from(jnp.sum(sums, axis=0))[0]


def tiled_body(rhs, diagonal, coupling, springs, precond, hub_inverse):
    residual = rhs[0]
    rows, loads = residual.shape
    attached = springs.shape[1]
    quarter = rows - attached
    sectors, parts = lax.axis_size("sector"), lax.axis_size("dof")
    cases = loads // sectors
    height = attached // LANES * cases
    onward, backward = around(sectors)
    full, face = shape(rows, loads), shape(quarter, loads, dtype=bf16)
    top_shape, ends_shape = shape(attached, loads, dtype=bf16), shape(parts, quarter, loads, dtype=bf16)

    stiffness = diagonal[0] + jnp.pad(springs[0], (0, quarter))
    stiffness = jnp.broadcast_to(stiffness[:, None], (rows, loads))
    solution = jnp.zeros_like(residual)
    image = precon = None
    sums = jnp.zeros((1, SUM_ROWS, loads), f32)

    top, ends = call(round_kernel, (top_shape, ends_shape), (rhs,))
    for step in range(ITERS):
        first, last = step == 0, step == ITERS - 1
        product, load, right, left = call(
            product_kernel,
            (full, shape(sectors, height + SUM_ROWS, LANES), face, face),
            (precond, springs, sums[0], gathered(top), exchange(ends, "dof")),
            parts=2 * parts,
            flops=2 * precond.size * loads,
        )
        before = lax.ppermute(right, "sector", onward)
        after = lax.ppermute(left, "sector", backward)
        packed = call(
            pack_kernel,
            shape(2 * quarter + height + 4 * SUM_ROWS, loads, dtype=bf16),
            (before, after, exchange(load, "sector")),
        )
        pieces = gathered(packed)
        hub = call(
            functools.partial(hub_kernel, cases),
            shape(sectors, height, LANES),
            (hub_inverse, pieces),
            parts=parts,
            flops=2 * hub_inverse.size * cases,
        )
        hubs = exchange(hub, "sector")
        state = () if first else (image, residual, precon, solution)
        base, ends, factor, *state = call(
            functools.partial(base_kernel, first),
            (full, ends_shape, shape(SUM_ROWS, loads)) + (() if first else (full, full, full)),
            (coupling[0], pieces, product, stiffness, *state),
            parts=parts,
            flops=2 * coupling.size * loads,
        )
        if first:
            precon = product
        else:
            residual, precon, solution = state
        image, top, sums = call(
            image_kernel,
            (full, top_shape, shape(sectors * parts if last else 1, SUM_ROWS, loads)),
            (base, hubs, springs, factor, residual),
        )
    out = shape(1, rows, loads)
    return call(
        last_kernel, (out, out), (exchange(sums, ("sector", "dof")), precon, image, solution, residual)
    )


def plain_body(rhs, diagonal, coupling, springs, precond, hub_inverse):
    residual = rhs[0]
    spring_rows = springs[0][:, None]
    rows, loads = residual.shape
    quarter = rows // 4
    sectors = lax.axis_size("sector")
    onward, backward = around(sectors)
    solution = jnp.zeros_like(residual)

    def whole(field):
        return gathered(field.astype(bf16)).reshape(-1, loads)

    def copies(cells, axes):
        count = lax.axis_size(axes)
        return exchange(jnp.broadcast_to(cells[None], (count,) + cells.shape), axes)

    precon = jnp.dot(precond, whole(residual), preferred_element_type=f32)
    for step in range(ITERS):
        faces = precon[: 2 * quarter].astype(bf16)
        before = lax.ppermute(faces[quarter:], "sector", onward)
        after = lax.ppermute(faces[:quarter], "sector", backward)
        couple = jnp.dot(
            coupling[0], whole(jnp.concatenate([before, after])), preferred_element_type=f32
        )
        attached = precon[: 3 * quarter]
        load = (spring_rows * attached).T.reshape(sectors, loads // sectors, -1)
        load = jnp.sum(exchange(load, "sector"), axis=0).astype(bf16)
        load = copies(load, "dof").transpose(0, 2, 1).reshape(hub_inverse.shape[1], -1)
        hub = jnp.dot(hub_inverse, load, preferred_element_type=f32)
        hub = copies(hub.T, "sector").reshape(loads, -1).T
        pull = jnp.pad(spring_rows * (attached - hub), ((0, quarter), (0, 0)))
        image = diagonal[0][:, None] * precon + couple + pull
        sums = jnp.stack([jnp.sum(image * residual, axis=0), jnp.sum(image * image, axis=0)])
        alpha = alpha_of(copies(sums, ("sector", "dof")))
        solution = solution + alpha * precon
        residual = residual - alpha * image
        if step < ITERS - 1:
            change = jnp.dot(precond, whole(image), preferred_element_type=f32)
            precon = precon - alpha * change
    return (solution[None], residual[None])


def body(rhs, *rest):
    rows, loads = rhs.shape[1:]
    cases = loads // lax.axis_size("sector")
    tiled = loads == LANES and (rows // 4) % LANES == 0 and cases % 16 == 0
    return (tiled_body if tiled else plain_body)(rhs, *rest)


def solution(mesh):
    placed = (
        P("sector", "dof", None),
        P("sector", "dof"),
        P("sector", "dof", None),
        P("sector", "dof"),
        P("dof", None),
        P("dof", None),
    )
    return jax.shard_map(
        body,
        mesh=mesh,
        in_specs=placed,
        out_specs=(P("sector", "dof", None), P("sector", "dof", None)),
        check_vma=False,
    )
```

```python
import functools

import jax
import jax.numpy as jnp
from jax import lax
from jax.experimental import pallas as pl
from jax.experimental.pallas import tpu as pltpu
from jax.sharding import PartitionSpec as P

ITERS = 3
LANES = 128
MIB = 1024 * 1024
IN_FLIGHT = 2
SUM_ROWS = 8
WHOLE = pl.BlockSpec(memory_space=pltpu.VMEM)
f32 = jnp.float32
bf16 = jnp.bfloat16


def shape(*dims, dtype=f32):
    return jax.ShapeDtypeStruct(dims, dtype)


def call(kernel, outs, operands, parts=0, flops=0, small=False):
    matrix = operands[0]
    specs = [WHOLE] * len(operands)
    scratch = []
    if parts:
        specs[0] = pl.BlockSpec(memory_space=pltpu.HBM)
        scratch = [pltpu.VMEM(matrix.shape, matrix.dtype), pltpu.SemaphoreType.DMA((parts,))]
    return pl.pallas_call(
        kernel,
        in_specs=specs,
        out_specs=jax.tree.map(lambda _: WHOLE, outs),
        out_shape=outs,
        scratch_shapes=scratch,
        compiler_params=pltpu.CompilerParams(vmem_limit_bytes=(16 if small else 60) * MIB),
        cost_estimate=pl.CostEstimate(
            flops=flops, bytes_accessed=sum(x.size * x.dtype.itemsize for x in operands), transcendentals=0
        ),
    )(*operands)


def row_blocks(source, buffer, sems):
    count = sems.shape[0]
    height = source.shape[0] // count
    blocks = [pl.ds(at * height, height) for at in range(count)]
    copies = [
        pltpu.make_async_copy(source.at[rows], buffer.at[rows], sems.at[at])
        for at, rows in enumerate(blocks)
    ]
    for copy in copies[:IN_FLIGHT]:
        copy.start()
    for at in range(count):
        copies[at].wait()
        if at + IN_FLIGHT < count:
            copies[at + IN_FLIGHT].start()
        yield slice(at * height, (at + 1) * height)


def product_kernel(summed, matrix_ref, springs_ref, *refs):
    *refs, out_ref, load_ref, right_ref, left_ref, buffer, sems = refs
    tops_ref, ends_ref = refs[-2:]
    parts, top, _ = tops_ref.shape
    end = ends_ref.shape[1]
    for rows in row_blocks(matrix_ref, buffer, sems):
        total = None
        for part in range(parts):
            start = part * (top + end)
            for width, field in ((top, tops_ref[part]), (end, ends_ref[part])):
                product = jnp.dot(
                    buffer[rows, start : start + width], field, preferred_element_type=f32
                )
                total = product if total is None else total + product
                start += width
        out_ref[rows] = total

    sectors, height, _ = load_ref.shape
    cases = out_ref.shape[1] // sectors
    quarter = right_ref.shape[0]
    left_ref[...] = out_ref[:quarter].astype(bf16)
    right_ref[...] = out_ref[quarter : 2 * quarter].astype(bf16)
    for at in range((height - SUM_ROWS) // cases):
        rows = slice(at * LANES, (at + 1) * LANES)
        turned = out_ref[rows].T * springs_ref[:, rows]
        for s in range(sectors):
            load_ref[s, at * cases : (at + 1) * cases] = turned[s * cases : (s + 1) * cases]
    for s in range(sectors):
        load_ref[s, height - SUM_ROWS :] = refs[0][...] if summed else jnp.zeros((SUM_ROWS, LANES), f32)


def pack_kernel(before_ref, after_ref, parts_ref, out_ref):
    quarter = before_ref.shape[0]
    height = parts_ref.shape[1] - SUM_ROWS
    out_ref[:quarter] = before_ref[...]
    out_ref[quarter : 2 * quarter] = after_ref[...]
    total = jnp.sum(parts_ref[...], axis=0)
    out_ref[2 * quarter : 2 * quarter + height] = total[:height].astype(bf16)
    rest = total[height:]
    terms = []
    for _ in range(3):
        term = rest.astype(bf16)
        terms.append(term.astype(f32))
        rest = rest - terms[-1]
    terms.append(jnp.zeros_like(rest))
    out_ref[2 * quarter + height :] = jnp.concatenate(terms, axis=0).astype(bf16)


def alpha_from(sums):
    return sums[0:1] / (sums[1:2] + 1e-06)


def hub_kernel(cases, matrix_ref, pieces_ref, out_ref, buffer, sems):
    parts = pieces_ref.shape[0]
    height = out_ref.shape[1]
    chunks = height // cases
    first = pieces_ref.shape[1] - 4 * SUM_ROWS - height
    load = jnp.concatenate(
        [
            pieces_ref[part, first + c * cases : first + (c + 1) * cases]
            for part in range(parts)
            for c in range(chunks)
        ],
        axis=1,
    )
    for rows in row_blocks(matrix_ref, buffer, sems):
        hub = lax.dot_general(
            load, buffer[rows], (((1,), (1,)), ((), ())), preferred_element_type=f32
        )
        for c in range(rows.start // LANES, rows.stop // LANES):
            at = c * LANES - rows.start
            for s in range(out_ref.shape[0]):
                out_ref[s, c * cases : (c + 1) * cases] = hub[:, at : at + LANES]


def base_kernel(first, matrix_ref, pieces_ref, product_ref, stiffness_ref, *refs):
    if first:
        base_ref, ends_ref, factor_ref, buffer, sems = refs
    else:
        *refs, base_ref, ends_ref, factor_ref, left_ref, newer_ref, better_ref, buffer, sems = refs
        image_ref, residual_ref, precon_ref = refs[:3]
    parts = pieces_ref.shape[0]
    depth = matrix_ref.shape[1] // parts
    for rows in row_blocks(matrix_ref, buffer, sems):
        total = stiffness_ref[rows] * product_ref[rows]
        for part in range(parts):
            total += jnp.dot(
                buffer[rows, part * depth : (part + 1) * depth],
                pieces_ref[part, :depth],
                preferred_element_type=f32,
            )
        base_ref[rows] = total
    if first:
        factor_ref[...] = jnp.ones_like(factor_ref)
    else:
        sums = None
        height = pieces_ref.shape[1]
        for part in range(parts):
            terms = pieces_ref[part, height - 4 * SUM_ROWS :].astype(f32)
            terms = terms[:SUM_ROWS] + terms[SUM_ROWS : 2 * SUM_ROWS] + terms[2 * SUM_ROWS : 3 * SUM_ROWS]
            sums = terms if sums is None else sums + terms
        alpha = alpha_from(sums)
        factor_ref[...] = jnp.broadcast_to(-alpha, factor_ref.shape)
        base_ref[...] = image_ref[...] - alpha * base_ref[...]
        left_ref[...] = residual_ref[...] - alpha * image_ref[...]
        gain = alpha * precon_ref[...]
        better_ref[...] = refs[3][...] + gain if len(refs) > 3 else gain
        newer_ref[...] = precon_ref[...] - alpha * product_ref[...]
    end = base_ref[base_ref.shape[0] - ends_ref.shape[1] :].astype(bf16)
    ends_ref[...] = jnp.broadcast_to(end[None], ends_ref.shape)


def image_kernel(base_ref, hubs_ref, springs_ref, factor_ref, residual_ref, image_ref, top_ref, sums_ref):
    sectors, height, _ = hubs_ref.shape
    attached = top_ref.shape[0]
    chunks = attached // LANES
    cases = height // chunks
    factor = factor_ref[0:1]
    for c in range(chunks):
        at = slice(c * LANES, (c + 1) * LANES)
        hub = jnp.concatenate([hubs_ref[s, c * cases : (c + 1) * cases] for s in range(sectors)], axis=0)
        image = base_ref[at] - factor * (hub * springs_ref[:, at]).T
        image_ref[at] = image
        top_ref[at] = image.astype(bf16)
    image_ref[attached:] = base_ref[attached:]
    image = image_ref[...]
    upper = jnp.sum(image * residual_ref[...], axis=0, keepdims=True)
    lower = jnp.sum(image * image, axis=0, keepdims=True)
    rest = jnp.zeros((SUM_ROWS - 2, image.shape[1]), f32)
    sums = jnp.concatenate([upper, lower, rest], axis=0)
    sums_ref[...] = jnp.broadcast_to(sums, sums_ref.shape)


def last_kernel(sums_ref, image_ref, residual_ref, precon_ref, solution_ref, newer_ref, left_ref):
    alpha = alpha_from(jnp.sum(sums_ref[...], axis=0))
    newer_ref[0] = solution_ref[...] + alpha * precon_ref[...]
    left_ref[0] = residual_ref[...] - alpha * image_ref[...]


def round_kernel(field_ref, top_ref, ends_ref):
    attached = top_ref.shape[0]
    top_ref[...] = field_ref[0, :attached].astype(bf16)
    end = field_ref[0, attached:].astype(bf16)
    ends_ref[...] = jnp.broadcast_to(end[None], ends_ref.shape)


def exchange(blocks, axes):
    return lax.all_to_all(blocks, axes, split_axis=0, concat_axis=0)


def gathered(field):
    return lax.all_gather(field, "dof", axis=0)


def around(sectors):
    onward = [(s, (s + 1) % sectors) for s in range(sectors)]
    return onward, [(b, a) for a, b in onward]


def alpha_of(sums):
    return alpha_from(jnp.sum(sums, axis=0))[0]


def tiled_body(rhs, diagonal, coupling, springs, precond, hub_inverse):
    residual = rhs[0]
    rows, loads = residual.shape
    attached = springs.shape[1]
    quarter = rows - attached
    sectors, parts = lax.axis_size("sector"), lax.axis_size("dof")
    cases = loads // sectors
    height = attached // LANES * cases
    onward, backward = around(sectors)
    full, face = shape(rows, loads), shape(quarter, loads, dtype=bf16)
    top_shape, ends_shape = shape(attached, loads, dtype=bf16), shape(parts, quarter, loads, dtype=bf16)

    stiffness = diagonal[0] + jnp.pad(springs[0], (0, quarter))
    stiffness = jnp.broadcast_to(stiffness[:, None], (rows, loads))
    state = sums = ()

    top, ends = call(round_kernel, (top_shape, ends_shape), (rhs,))
    for step in range(ITERS):
        first, last = step == 0, step == ITERS - 1
        product, load, right, left = call(
            functools.partial(product_kernel, not first),
            (full, shape(sectors, height + SUM_ROWS, LANES), face, face),
            (precond, springs, *sums, gathered(top), exchange(ends, "dof")),
            parts=rows // (2 * LANES),
            flops=2 * precond.size * loads,
        )
        before = lax.ppermute(right, "sector", onward)
        after = lax.ppermute(left, "sector", backward)
        packed = call(
            pack_kernel,
            shape(2 * quarter + height + 4 * SUM_ROWS, loads, dtype=bf16),
            (before, after, exchange(load, "sector")),
            small=True,
        )
        pieces = gathered(packed)
        hub = call(
            functools.partial(hub_kernel, cases),
            shape(sectors, height, LANES),
            (hub_inverse, pieces),
            parts=attached // LANES // 2 if attached % (2 * LANES) == 0 else attached // LANES,
            flops=2 * hub_inverse.size * cases,
        )
        hubs = exchange(hub, "sector")
        base, ends, factor, *state = call(
            functools.partial(base_kernel, first),
            (full, ends_shape, shape(SUM_ROWS, loads)) + (() if first else (full, full, full)),
            (coupling[0], pieces, product, stiffness, *state),
            parts=rows // (2 * LANES),
            flops=2 * coupling.size * loads,
        )
        residual, precon, *solution = (residual, product) if first else state
        image, top, sums = call(
            image_kernel,
            (
                full,
                top_shape,
                shape(sectors * parts, SUM_ROWS, loads) if last else shape(SUM_ROWS, loads),
            ),
            (base, hubs, springs, factor, residual),
        )
        state = (image, residual, precon, *solution)
        sums = (sums,)
    out = shape(1, rows, loads)
    return call(last_kernel, (out, out), (exchange(*sums, ("sector", "dof")), *state))


def plain_body(rhs, diagonal, coupling, springs, precond, hub_inverse):
    residual = rhs[0]
    spring_rows = springs[0][:, None]
    rows, loads = residual.shape
    quarter = rows // 4
    sectors = lax.axis_size("sector")
    onward, backward = around(sectors)
    solution = jnp.zeros_like(residual)

    def whole(field):
        return gathered(field.astype(bf16)).reshape(-1, loads)

    def copies(cells, axes):
        count = lax.axis_size(axes)
        return exchange(jnp.broadcast_to(cells[None], (count,) + cells.shape), axes)

    precon = jnp.dot(precond, whole(residual), preferred_element_type=f32)
    for step in range(ITERS):
        faces = precon[: 2 * quarter].astype(bf16)
        before = lax.ppermute(faces[quarter:], "sector", onward)
        after = lax.ppermute(faces[:quarter], "sector", backward)
        couple = jnp.dot(
            coupling[0], whole(jnp.concatenate([before, after])), preferred_element_type=f32
        )
        attached = precon[: 3 * quarter]
        load = (spring_rows * attached).T.reshape(sectors, loads // sectors, -1)
        load = jnp.sum(exchange(load, "sector"), axis=0).astype(bf16)
        load = copies(load, "dof").transpose(0, 2, 1).reshape(hub_inverse.shape[1], -1)
        hub = jnp.dot(hub_inverse, load, preferred_element_type=f32)
        hub = copies(hub.T, "sector").reshape(loads, -1).T
        pull = jnp.pad(spring_rows * (attached - hub), ((0, quarter), (0, 0)))
        image = diagonal[0][:, None] * precon + couple + pull
        sums = jnp.stack([jnp.sum(image * residual, axis=0), jnp.sum(image * image, axis=0)])
        alpha = alpha_of(copies(sums, ("sector", "dof")))
        solution = solution + alpha * precon
        residual = residual - alpha * image
        if step < ITERS - 1:
            change = jnp.dot(precond, whole(image), preferred_element_type=f32)
            precon = precon - alpha * change
    return (solution[None], residual[None])


def body(rhs, *rest):
    rows, loads = rhs.shape[1:]
    cases = loads // lax.axis_size("sector")
    tiled = loads == LANES and (rows // 4) % LANES == 0 and cases % 16 == 0
    return (tiled_body if tiled else plain_body)(rhs, *rest)


def solution(mesh):
    placed = (
        P("sector", "dof", None),
        P("sector", "dof"),
        P("sector", "dof", None),
        P("sector", "dof"),
        P("dof", None),
        P("dof", None),
    )
    return jax.shard_map(
        body,
        mesh=mesh,
        in_specs=placed,
        out_specs=(P("sector", "dof", None), P("sector", "dof", None)),
        check_vma=False,
    )
```

```python
import functools

import jax
import jax.numpy as jnp
from jax import lax
from jax.experimental import pallas as pl
from jax.experimental.pallas import tpu as pltpu
from jax.sharding import PartitionSpec as P

ITERS = 3
LANES = 128
MIB = 1024 * 1024
IN_FLIGHT = 8
PIECE_ROWS = 64
BLOCK_ROWS = 256
SUM_ROWS = 8
WHOLE = pl.BlockSpec(memory_space=pltpu.VMEM)
f32 = jnp.float32
bf16 = jnp.bfloat16


def shape(*dims, dtype=f32):
    return jax.ShapeDtypeStruct(dims, dtype)


def call(kernel, outs, operands, streamed=False, flops=0, small=False):
    matrix = operands[0]
    specs = [WHOLE] * len(operands)
    scratch = []
    if streamed:
        specs[0] = pl.BlockSpec(memory_space=pltpu.HBM)
        scratch = [pltpu.VMEM(matrix.shape, matrix.dtype), pltpu.SemaphoreType.DMA((matrix.shape[0] // PIECE_ROWS,))]
    return pl.pallas_call(
        kernel,
        in_specs=specs,
        out_specs=jax.tree.map(lambda _: WHOLE, outs),
        out_shape=outs,
        scratch_shapes=scratch,
        compiler_params=pltpu.CompilerParams(vmem_limit_bytes=(16 if small else 60) * MIB),
        cost_estimate=pl.CostEstimate(
            flops=flops, bytes_accessed=sum(x.size * x.dtype.itemsize for x in operands), transcendentals=0
        ),
    )(*operands)


def row_blocks(source, buffer, sems):
    count = sems.shape[0]
    height = source.shape[0] // count
    pieces = [pl.ds(at * height, height) for at in range(count)]
    copies = [
        pltpu.make_async_copy(source.at[rows], buffer.at[rows], sems.at[at])
        for at, rows in enumerate(pieces)
    ]
    for copy in copies[:IN_FLIGHT]:
        copy.start()
    for at in range(count):
        copies[at].wait()
        if at + IN_FLIGHT < count:
            copies[at + IN_FLIGHT].start()
        stop = (at + 1) * height
        if stop % BLOCK_ROWS == 0:
            yield slice(stop - BLOCK_ROWS, stop)


def product_kernel(matrix_ref, tops_ref, ends_ref, out_ref, right_ref, left_ref, buffer, sems):
    parts, top, _ = tops_ref.shape
    end = ends_ref.shape[1]
    for rows in row_blocks(matrix_ref, buffer, sems):
        total = None
        for part in range(parts):
            start = part * (top + end)
            for width, field in ((top, tops_ref[part]), (end, ends_ref[part])):
                product = jnp.dot(
                    buffer[rows, start : start + width], field, preferred_element_type=f32
                )
                total = product if total is None else total + product
                start += width
        out_ref[rows] = total
    quarter = right_ref.shape[0]
    left_ref[...] = out_ref[:quarter].astype(bf16)
    right_ref[...] = out_ref[quarter : 2 * quarter].astype(bf16)


def load_kernel(product_ref, springs_ref, *refs):
    load_ref = refs[-1]
    sectors, height, loads = load_ref.shape
    cases = loads // sectors
    for at in range((height - SUM_ROWS) // cases):
        rows = slice(at * LANES, (at + 1) * LANES)
        turned = product_ref[rows].T * springs_ref[:, rows]
        for s in range(sectors):
            load_ref[s, at * cases : (at + 1) * cases] = turned[s * cases : (s + 1) * cases]
    for s in range(sectors):
        load_ref[s, height - SUM_ROWS :] = refs[0][...] if refs[1:] else jnp.zeros((SUM_ROWS, LANES), f32)


def pack_kernel(before_ref, after_ref, parts_ref, out_ref):
    quarter = before_ref.shape[0]
    height = parts_ref.shape[1] - SUM_ROWS
    out_ref[:quarter] = before_ref[...]
    out_ref[quarter : 2 * quarter] = after_ref[...]
    total = jnp.sum(parts_ref[...], axis=0)
    out_ref[2 * quarter : 2 * quarter + height] = total[:height].astype(bf16)
    rest = total[height:]
    terms = []
    for _ in range(3):
        term = rest.astype(bf16)
        terms.append(term.astype(f32))
        rest = rest - terms[-1]
    terms.append(jnp.zeros_like(rest))
    out_ref[2 * quarter + height :] = jnp.concatenate(terms, axis=0).astype(bf16)


def alpha_from(sums):
    return sums[0:1] / (sums[1:2] + 1e-06)


def hub_kernel(cases, matrix_ref, pieces_ref, out_ref, buffer, sems):
    parts = pieces_ref.shape[0]
    height = out_ref.shape[1]
    chunks = height // cases
    first = pieces_ref.shape[1] - 4 * SUM_ROWS - height
    load = jnp.concatenate(
        [
            pieces_ref[part, first + c * cases : first + (c + 1) * cases]
            for part in range(parts)
            for c in range(chunks)
        ],
        axis=1,
    )
    for rows in row_blocks(matrix_ref, buffer, sems):
        hub = lax.dot_general(
            load, buffer[rows], (((1,), (1,)), ((), ())), preferred_element_type=f32
        )
        for c in range(rows.start // LANES, rows.stop // LANES):
            at = c * LANES - rows.start
            for s in range(out_ref.shape[0]):
                out_ref[s, c * cases : (c + 1) * cases] = hub[:, at : at + LANES]


def base_kernel(first, matrix_ref, pieces_ref, product_ref, stiffness_ref, *refs):
    if first:
        base_ref, ends_ref, factor_ref, buffer, sems = refs
    else:
        *refs, base_ref, ends_ref, factor_ref, left_ref, newer_ref, better_ref, buffer, sems = refs
        image_ref, residual_ref, precon_ref = refs[:3]
    parts = pieces_ref.shape[0]
    depth = matrix_ref.shape[1] // parts
    for rows in row_blocks(matrix_ref, buffer, sems):
        total = stiffness_ref[rows] * product_ref[rows]
        for part in range(parts):
            total += jnp.dot(
                buffer[rows, part * depth : (part + 1) * depth],
                pieces_ref[part, :depth],
                preferred_element_type=f32,
            )
        base_ref[rows] = total
    if first:
        factor_ref[...] = jnp.ones_like(factor_ref)
    else:
        sums = None
        height = pieces_ref.shape[1]
        for part in range(parts):
            terms = pieces_ref[part, height - 4 * SUM_ROWS :].astype(f32)
            terms = terms[:SUM_ROWS] + terms[SUM_ROWS : 2 * SUM_ROWS] + terms[2 * SUM_ROWS : 3 * SUM_ROWS]
            sums = terms if sums is None else sums + terms
        alpha = alpha_from(sums)
        factor_ref[...] = jnp.broadcast_to(-alpha, factor_ref.shape)
        base_ref[...] = image_ref[...] - alpha * base_ref[...]
        left_ref[...] = residual_ref[...] - alpha * image_ref[...]
        gain = alpha * precon_ref[...]
        better_ref[...] = refs[3][...] + gain if len(refs) > 3 else gain
        newer_ref[...] = precon_ref[...] - alpha * product_ref[...]
    end = base_ref[base_ref.shape[0] - ends_ref.shape[1] :].astype(bf16)
    ends_ref[...] = jnp.broadcast_to(end[None], ends_ref.shape)


def image_kernel(base_ref, hubs_ref, springs_ref, factor_ref, residual_ref, image_ref, top_ref, sums_ref):
    sectors, height, _ = hubs_ref.shape
    attached = top_ref.shape[0]
    chunks = attached // LANES
    cases = height // chunks
    factor = factor_ref[0:1]
    for c in range(chunks):
        at = slice(c * LANES, (c + 1) * LANES)
        hub = jnp.concatenate([hubs_ref[s, c * cases : (c + 1) * cases] for s in range(sectors)], axis=0)
        image = base_ref[at] - factor * (hub * springs_ref[:, at]).T
        image_ref[at] = image
        top_ref[at] = image.astype(bf16)
    image_ref[attached:] = base_ref[attached:]
    image = image_ref[...]
    upper = jnp.sum(image * residual_ref[...], axis=0, keepdims=True)
    lower = jnp.sum(image * image, axis=0, keepdims=True)
    rest = jnp.zeros((SUM_ROWS - 2, image.shape[1]), f32)
    sums = jnp.concatenate([upper, lower, rest], axis=0)
    sums_ref[...] = jnp.broadcast_to(sums, sums_ref.shape)


def last_kernel(sums_ref, image_ref, residual_ref, precon_ref, solution_ref, newer_ref, left_ref):
    alpha = alpha_from(jnp.sum(sums_ref[...], axis=0))
    newer_ref[0] = solution_ref[...] + alpha * precon_ref[...]
    left_ref[0] = residual_ref[...] - alpha * image_ref[...]


def round_kernel(field_ref, top_ref, ends_ref):
    attached = top_ref.shape[0]
    top_ref[...] = field_ref[0, :attached].astype(bf16)
    end = field_ref[0, attached:].astype(bf16)
    ends_ref[...] = jnp.broadcast_to(end[None], ends_ref.shape)


def exchange(blocks, axes):
    return lax.all_to_all(blocks, axes, split_axis=0, concat_axis=0)


def gathered(field):
    return lax.all_gather(field, "dof", axis=0)


def around(sectors):
    onward = [(s, (s + 1) % sectors) for s in range(sectors)]
    return onward, [(b, a) for a, b in onward]


def alpha_of(sums):
    return alpha_from(jnp.sum(sums, axis=0))[0]


def tiled_body(rhs, diagonal, coupling, springs, precond, hub_inverse):
    residual = rhs[0]
    rows, loads = residual.shape
    attached = springs.shape[1]
    quarter = rows - attached
    sectors, parts = lax.axis_size("sector"), lax.axis_size("dof")
    cases = loads // sectors
    height = attached // LANES * cases
    onward, backward = around(sectors)
    full, face = shape(rows, loads), shape(quarter, loads, dtype=bf16)
    top_shape, ends_shape = shape(attached, loads, dtype=bf16), shape(parts, quarter, loads, dtype=bf16)

    stiffness = diagonal[0] + jnp.pad(springs[0], (0, quarter))
    stiffness = jnp.broadcast_to(stiffness[:, None], (rows, loads))
    state = sums = ()

    top, ends = call(round_kernel, (top_shape, ends_shape), (rhs,))
    for step in range(ITERS):
        first, last = step == 0, step == ITERS - 1
        product, right, left = call(
            product_kernel,
            (full, face, face),
            (precond, gathered(top), exchange(ends, "dof")),
            streamed=True,
            flops=2 * precond.size * loads,
        )
        before = lax.ppermute(right, "sector", onward)
        after = lax.ppermute(left, "sector", backward)
        load = call(
            load_kernel, shape(sectors, height + SUM_ROWS, LANES), (product, springs, *sums), small=True
        )
        packed = call(
            pack_kernel,
            shape(2 * quarter + height + 4 * SUM_ROWS, loads, dtype=bf16),
            (before, after, exchange(load, "sector")),
            small=True,
        )
        pieces = gathered(packed)
        hub = call(
            functools.partial(hub_kernel, cases),
            shape(sectors, height, LANES),
            (hub_inverse, pieces),
            streamed=True,
            flops=2 * hub_inverse.size * cases,
        )
        hubs = exchange(hub, "sector")
        base, ends, factor, *state = call(
            functools.partial(base_kernel, first),
            (full, ends_shape, shape(SUM_ROWS, loads)) + (() if first else (full, full, full)),
            (coupling[0], pieces, product, stiffness, *state),
            streamed=True,
            flops=2 * coupling.size * loads,
        )
        residual, precon, *solution = (residual, product) if first else state
        image, top, sums = call(
            image_kernel,
            (
                full,
                top_shape,
                shape(sectors * parts, SUM_ROWS, loads) if last else shape(SUM_ROWS, loads),
            ),
            (base, hubs, springs, factor, residual),
        )
        state = (image, residual, precon, *solution)
        sums = (sums,)
    out = shape(1, rows, loads)
    return call(last_kernel, (out, out), (exchange(*sums, ("sector", "dof")), *state))


def plain_body(rhs, diagonal, coupling, springs, precond, hub_inverse):
    residual = rhs[0]
    spring_rows = springs[0][:, None]
    rows, loads = residual.shape
    quarter = rows // 4
    sectors = lax.axis_size("sector")
    onward, backward = around(sectors)
    solution = jnp.zeros_like(residual)

    def whole(field):
        return gathered(field.astype(bf16)).reshape(-1, loads)

    def copies(cells, axes):
        count = lax.axis_size(axes)
        return exchange(jnp.broadcast_to(cells[None], (count,) + cells.shape), axes)

    precon = jnp.dot(precond, whole(residual), preferred_element_type=f32)
    for step in range(ITERS):
        faces = precon[: 2 * quarter].astype(bf16)
        before = lax.ppermute(faces[quarter:], "sector", onward)
        after = lax.ppermute(faces[:quarter], "sector", backward)
        couple = jnp.dot(
            coupling[0], whole(jnp.concatenate([before, after])), preferred_element_type=f32
        )
        attached = precon[: 3 * quarter]
        load = (spring_rows * attached).T.reshape(sectors, loads // sectors, -1)
        load = jnp.sum(exchange(load, "sector"), axis=0).astype(bf16)
        load = copies(load, "dof").transpose(0, 2, 1).reshape(hub_inverse.shape[1], -1)
        hub = jnp.dot(hub_inverse, load, preferred_element_type=f32)
        hub = copies(hub.T, "sector").reshape(loads, -1).T
        pull = jnp.pad(spring_rows * (attached - hub), ((0, quarter), (0, 0)))
        image = diagonal[0][:, None] * precon + couple + pull
        sums = jnp.stack([jnp.sum(image * residual, axis=0), jnp.sum(image * image, axis=0)])
        alpha = alpha_of(copies(sums, ("sector", "dof")))
        solution = solution + alpha * precon
        residual = residual - alpha * image
        if step < ITERS - 1:
            change = jnp.dot(precond, whole(image), preferred_element_type=f32)
            precon = precon - alpha * change
    return (solution[None], residual[None])


def body(rhs, *rest):
    rows, loads = rhs.shape[1:]
    cases = loads // lax.axis_size("sector")
    tiled = loads == LANES and (rows // 4) % BLOCK_ROWS == 0 and cases % 16 == 0
    return (tiled_body if tiled else plain_body)(rhs, *rest)


def solution(mesh):
    placed = (
        P("sector", "dof", None),
        P("sector", "dof"),
        P("sector", "dof", None),
        P("sector", "dof"),
        P("dof", None),
        P("dof", None),
    )
    return jax.shard_map(
        body,
        mesh=mesh,
        in_specs=placed,
        out_specs=(P("sector", "dof", None), P("sector", "dof", None)),
        check_vma=False,
    )
```

```python
import functools

import jax
import jax.numpy as jnp
from jax import lax
from jax.experimental import pallas as pl
from jax.experimental.pallas import tpu as pltpu
from jax.sharding import PartitionSpec as P

ITERS = 3
LANES = 128
MIB = 1024 * 1024
SUM_ROWS = 8
f32 = jnp.float32
bf16 = jnp.bfloat16


def shape(*dims, dtype=f32):
    return jax.ShapeDtypeStruct(dims, dtype)


def call(kernel, outs, operands, parted=(), steps=1, scratch=(), flops=0, small=False):
    specs = []
    for at, operand in enumerate(operands):
        block, dim = list(operand.shape), operand.ndim
        if at not in parted:
            specs.append(pl.BlockSpec(block, lambda k, dim=dim: (0,) * dim))
        elif dim == 2:
            specs.append(pl.BlockSpec([block[0], block[1] // steps], lambda k: (0, k)))
        else:
            specs.append(pl.BlockSpec([1] + block[1:], lambda k: (k, 0, 0)))
    out_specs = jax.tree.map(
        lambda out: pl.BlockSpec(out.shape, lambda k, dim=len(out.shape): (0,) * dim), outs
    )
    return pl.pallas_call(
        kernel,
        grid=(steps,),
        in_specs=specs,
        out_specs=out_specs,
        out_shape=outs,
        scratch_shapes=list(scratch),
        compiler_params=pltpu.CompilerParams(vmem_limit_bytes=(16 if small else 60) * MIB),
        cost_estimate=pl.CostEstimate(
            flops=flops, bytes_accessed=sum(x.size * x.dtype.itemsize for x in operands), transcendentals=0
        ),
    )(*operands)


def add_product(ref, product):
    first = pl.program_id(0) == 0

    @pl.when(first)
    def _():
        ref[...] = product

    @pl.when(jnp.logical_not(first))
    def _():
        ref[...] += product


def at_end(run):
    pl.when(pl.program_id(0) == pl.num_programs(0) - 1)(run)


def product_kernel(summed, matrix_ref, tops_ref, ends_ref, springs_ref, *refs):
    *refs, out_ref, load_ref, right_ref, left_ref = refs
    top = tops_ref.shape[1]
    add_product(
        out_ref,
        jnp.dot(matrix_ref[:, :top], tops_ref[0], preferred_element_type=f32)
        + jnp.dot(matrix_ref[:, top:], ends_ref[0], preferred_element_type=f32),
    )

    @at_end
    def _():
        sectors, height, _ = load_ref.shape
        cases = out_ref.shape[1] // sectors
        quarter = right_ref.shape[0]
        left_ref[...] = out_ref[:quarter].astype(bf16)
        right_ref[...] = out_ref[quarter : 2 * quarter].astype(bf16)
        for at in range((height - SUM_ROWS) // cases):
            rows = slice(at * LANES, (at + 1) * LANES)
            turned = out_ref[rows].T * springs_ref[:, rows]
            for s in range(sectors):
                load_ref[s, at * cases : (at + 1) * cases] = turned[s * cases : (s + 1) * cases]
        for s in range(sectors):
            load_ref[s, height - SUM_ROWS :] = refs[0][...] if summed else jnp.zeros((SUM_ROWS, LANES), f32)


def pack_kernel(before_ref, after_ref, parts_ref, out_ref):
    quarter = before_ref.shape[0]
    height = parts_ref.shape[1] - SUM_ROWS
    out_ref[:quarter] = before_ref[...]
    out_ref[quarter : 2 * quarter] = after_ref[...]
    total = jnp.sum(parts_ref[...], axis=0)
    out_ref[2 * quarter : 2 * quarter + height] = total[:height].astype(bf16)
    rest = total[height:]
    terms = []
    for _ in range(3):
        term = rest.astype(bf16)
        terms.append(term.astype(f32))
        rest = rest - terms[-1]
    terms.append(jnp.zeros_like(rest))
    out_ref[2 * quarter + height :] = jnp.concatenate(terms, axis=0).astype(bf16)


def alpha_from(sums):
    return sums[0:1] / (sums[1:2] + 1e-06)


def hub_kernel(cases, matrix_ref, pieces_ref, out_ref, total_ref):
    height = out_ref.shape[1]
    chunks = height // cases
    first = pieces_ref.shape[1] - 4 * SUM_ROWS - height
    load = jnp.concatenate(
        [pieces_ref[0, first + c * cases : first + (c + 1) * cases] for c in range(chunks)], axis=1
    )
    add_product(
        total_ref,
        lax.dot_general(
            load, matrix_ref[...], (((1,), (1,)), ((), ())), preferred_element_type=f32
        ),
    )

    @at_end
    def _():
        for c in range(chunks):
            block = total_ref[:, c * LANES : (c + 1) * LANES]
            for s in range(out_ref.shape[0]):
                out_ref[s, c * cases : (c + 1) * cases] = block


def base_kernel(first, matrix_ref, pieces_ref, product_ref, stiffness_ref, *refs):
    if first:
        base_ref, ends_ref, factor_ref, sums_ref = refs
    else:
        *refs, base_ref, ends_ref, factor_ref, left_ref, newer_ref, better_ref, sums_ref = refs
        image_ref, residual_ref, precon_ref = refs[:3]
    depth = matrix_ref.shape[1]
    add_product(
        base_ref, jnp.dot(matrix_ref[...], pieces_ref[0, :depth], preferred_element_type=f32)
    )
    terms = pieces_ref[0, pieces_ref.shape[1] - 4 * SUM_ROWS :].astype(f32)
    add_product(
        sums_ref, terms[:SUM_ROWS] + terms[SUM_ROWS : 2 * SUM_ROWS] + terms[2 * SUM_ROWS : 3 * SUM_ROWS]
    )

    @at_end
    def _():
        base = base_ref[...] + stiffness_ref[...] * product_ref[...]
        if first:
            factor_ref[...] = jnp.ones_like(factor_ref)
        else:
            alpha = alpha_from(sums_ref[...])
            factor_ref[...] = jnp.broadcast_to(-alpha, factor_ref.shape)
            base = image_ref[...] - alpha * base
            left_ref[...] = residual_ref[...] - alpha * image_ref[...]
            gain = alpha * precon_ref[...]
            better_ref[...] = refs[3][...] + gain if len(refs) > 3 else gain
            newer_ref[...] = precon_ref[...] - alpha * product_ref[...]
        base_ref[...] = base
        end = base[base.shape[0] - ends_ref.shape[1] :].astype(bf16)
        ends_ref[...] = jnp.broadcast_to(end[None], ends_ref.shape)


def image_kernel(base_ref, hubs_ref, springs_ref, factor_ref, residual_ref, image_ref, top_ref, sums_ref):
    sectors, height, _ = hubs_ref.shape
    attached = top_ref.shape[0]
    chunks = attached // LANES
    cases = height // chunks
    factor = factor_ref[0:1]
    for c in range(chunks):
        at = slice(c * LANES, (c + 1) * LANES)
        hub = jnp.concatenate([hubs_ref[s, c * cases : (c + 1) * cases] for s in range(sectors)], axis=0)
        image = base_ref[at] - factor * (hub * springs_ref[:, at]).T
        image_ref[at] = image
        top_ref[at] = image.astype(bf16)
    image_ref[attached:] = base_ref[attached:]
    image = image_ref[...]
    upper = jnp.sum(image * residual_ref[...], axis=0, keepdims=True)
    lower = jnp.sum(image * image, axis=0, keepdims=True)
    rest = jnp.zeros((SUM_ROWS - 2, image.shape[1]), f32)
    sums = jnp.concatenate([upper, lower, rest], axis=0)
    sums_ref[...] = jnp.broadcast_to(sums, sums_ref.shape)


def last_kernel(sums_ref, image_ref, residual_ref, precon_ref, solution_ref, newer_ref, left_ref):
    alpha = alpha_from(jnp.sum(sums_ref[...], axis=0))
    newer_ref[0] = solution_ref[...] + alpha * precon_ref[...]
    left_ref[0] = residual_ref[...] - alpha * image_ref[...]


def round_kernel(field_ref, top_ref, ends_ref):
    attached = top_ref.shape[0]
    top_ref[...] = field_ref[0, :attached].astype(bf16)
    end = field_ref[0, attached:].astype(bf16)
    ends_ref[...] = jnp.broadcast_to(end[None], ends_ref.shape)


def exchange(blocks, axes):
    return lax.all_to_all(blocks, axes, split_axis=0, concat_axis=0)


def gathered(field):
    return lax.all_gather(field, "dof", axis=0)


def around(sectors):
    onward = [(s, (s + 1) % sectors) for s in range(sectors)]
    return onward, [(b, a) for a, b in onward]


def alpha_of(sums):
    return alpha_from(jnp.sum(sums, axis=0))[0]


def tiled_body(rhs, diagonal, coupling, springs, precond, hub_inverse):
    residual = rhs[0]
    rows, loads = residual.shape
    attached = springs.shape[1]
    quarter = rows - attached
    sectors, parts = lax.axis_size("sector"), lax.axis_size("dof")
    cases = loads // sectors
    height = attached // LANES * cases
    onward, backward = around(sectors)
    full, face = shape(rows, loads), shape(quarter, loads, dtype=bf16)
    top_shape, ends_shape = shape(attached, loads, dtype=bf16), shape(parts, quarter, loads, dtype=bf16)

    stiffness = diagonal[0] + jnp.pad(springs[0], (0, quarter))
    stiffness = jnp.broadcast_to(stiffness[:, None], (rows, loads))
    state = sums = ()

    top, ends = call(round_kernel, (top_shape, ends_shape), (rhs,))
    for step in range(ITERS):
        first, last = step == 0, step == ITERS - 1
        product, load, right, left = call(
            functools.partial(product_kernel, not first),
            (full, shape(sectors, height + SUM_ROWS, LANES), face, face),
            (precond, gathered(top), exchange(ends, "dof"), springs, *sums),
            parted=(0, 1, 2),
            steps=parts,
            flops=2 * precond.size * loads,
        )
        before = lax.ppermute(right, "sector", onward)
        after = lax.ppermute(left, "sector", backward)
        packed = call(
            pack_kernel,
            shape(2 * quarter + height + 4 * SUM_ROWS, loads, dtype=bf16),
            (before, after, exchange(load, "sector")),
            small=True,
        )
        pieces = gathered(packed)
        hub = call(
            functools.partial(hub_kernel, cases),
            shape(sectors, height, LANES),
            (hub_inverse, pieces),
            parted=(0, 1),
            steps=parts,
            scratch=(pltpu.VMEM((cases, attached), f32),),
            flops=2 * hub_inverse.size * cases,
        )
        hubs = exchange(hub, "sector")
        base, ends, factor, *state = call(
            functools.partial(base_kernel, first),
            (full, ends_shape, shape(SUM_ROWS, loads)) + (() if first else (full, full, full)),
            (coupling[0], pieces, product, stiffness, *state),
            parted=(0, 1),
            steps=parts,
            scratch=(pltpu.VMEM((SUM_ROWS, loads), f32),),
            flops=2 * coupling.size * loads,
        )
        residual, precon, *solution = (residual, product) if first else state
        image, top, sums = call(
            image_kernel,
            (
                full,
                top_shape,
                shape(sectors * parts, SUM_ROWS, loads) if last else shape(SUM_ROWS, loads),
            ),
            (base, hubs, springs, factor, residual),
        )
        state = (image, residual, precon, *solution)
        sums = (sums,)
    out = shape(1, rows, loads)
    return call(last_kernel, (out, out), (exchange(*sums, ("sector", "dof")), *state))


def plain_body(rhs, diagonal, coupling, springs, precond, hub_inverse):
    residual = rhs[0]
    spring_rows = springs[0][:, None]
    rows, loads = residual.shape
    quarter = rows // 4
    sectors = lax.axis_size("sector")
    onward, backward = around(sectors)
    solution = jnp.zeros_like(residual)

    def whole(field):
        return gathered(field.astype(bf16)).reshape(-1, loads)

    def copies(cells, axes):
        count = lax.axis_size(axes)
        return exchange(jnp.broadcast_to(cells[None], (count,) + cells.shape), axes)

    precon = jnp.dot(precond, whole(residual), preferred_element_type=f32)
    for step in range(ITERS):
        faces = precon[: 2 * quarter].astype(bf16)
        before = lax.ppermute(faces[quarter:], "sector", onward)
        after = lax.ppermute(faces[:quarter], "sector", backward)
        couple = jnp.dot(
            coupling[0], whole(jnp.concatenate([before, after])), preferred_element_type=f32
        )
        attached = precon[: 3 * quarter]
        load = (spring_rows * attached).T.reshape(sectors, loads // sectors, -1)
        load = jnp.sum(exchange(load, "sector"), axis=0).astype(bf16)
        load = copies(load, "dof").transpose(0, 2, 1).reshape(hub_inverse.shape[1], -1)
        hub = jnp.dot(hub_inverse, load, preferred_element_type=f32)
        hub = copies(hub.T, "sector").reshape(loads, -1).T
        pull = jnp.pad(spring_rows * (attached - hub), ((0, quarter), (0, 0)))
        image = diagonal[0][:, None] * precon + couple + pull
        sums = jnp.stack([jnp.sum(image * residual, axis=0), jnp.sum(image * image, axis=0)])
        alpha = alpha_of(copies(sums, ("sector", "dof")))
        solution = solution + alpha * precon
        residual = residual - alpha * image
        if step < ITERS - 1:
            change = jnp.dot(precond, whole(image), preferred_element_type=f32)
            precon = precon - alpha * change
    return (solution[None], residual[None])


def body(rhs, *rest):
    rows, loads = rhs.shape[1:]
    cases = loads // lax.axis_size("sector")
    tiled = loads == LANES and (rows // 4) % LANES == 0 and cases % 16 == 0
    return (tiled_body if tiled else plain_body)(rhs, *rest)


def solution(mesh):
    placed = (
        P("sector", "dof", None),
        P("sector", "dof"),
        P("sector", "dof", None),
        P("sector", "dof"),
        P("dof", None),
        P("dof", None),
    )
    return jax.shard_map(
        body,
        mesh=mesh,
        in_specs=placed,
        out_specs=(P("sector", "dof", None), P("sector", "dof", None)),
        check_vma=False,
    )
```

```python
import functools

import jax
import jax.numpy as jnp
from jax import lax
from jax.experimental import pallas as pl
from jax.experimental.pallas import tpu as pltpu
from jax.sharding import PartitionSpec as P

ITERS = 3
LANES = 128
MIB = 1024 * 1024
SUM_ROWS = 8
TERM_ROWS = 16
f32 = jnp.float32
bf16 = jnp.bfloat16


def shape(*dims, dtype=f32):
    return jax.ShapeDtypeStruct(dims, dtype)


def call(kernel, outs, operands, parted=(), steps=1, scratch=(), flops=0, small=False):
    specs = []
    for at, operand in enumerate(operands):
        block, dim = list(operand.shape), operand.ndim
        if at not in parted:
            specs.append(pl.BlockSpec(block, lambda k, dim=dim: (0,) * dim))
        elif dim == 2:
            specs.append(pl.BlockSpec([block[0], block[1] // steps], lambda k: (0, k)))
        else:
            specs.append(pl.BlockSpec([1] + block[1:], lambda k: (k, 0, 0)))
    out_specs = jax.tree.map(
        lambda out: pl.BlockSpec(out.shape, lambda k, dim=len(out.shape): (0,) * dim), outs
    )
    return pl.pallas_call(
        kernel,
        grid=(steps,),
        in_specs=specs,
        out_specs=out_specs,
        out_shape=outs,
        scratch_shapes=list(scratch),
        compiler_params=pltpu.CompilerParams(vmem_limit_bytes=(16 if small else 60) * MIB),
        cost_estimate=pl.CostEstimate(
            flops=flops, bytes_accessed=sum(x.size * x.dtype.itemsize for x in operands), transcendentals=0
        ),
    )(*operands)


def add_product(ref, product):
    first = pl.program_id(0) == 0

    @pl.when(first)
    def _():
        ref[...] = product

    @pl.when(jnp.logical_not(first))
    def _():
        ref[...] += product


def at_end(run):
    pl.when(pl.program_id(0) == pl.num_programs(0) - 1)(run)


def in_terms(sums):
    terms = None
    for at in range(3):
        term = sums.astype(bf16).astype(f32)
        sums = sums - term
        terms = term if at == 0 else terms + pltpu.roll(term, 2 * at, 0)
    return jnp.concatenate([terms, jnp.zeros_like(terms)], axis=0)


def from_terms(terms):
    terms = terms[:SUM_ROWS].astype(f32)
    sums = terms + pltpu.roll(terms, SUM_ROWS - 2, 0) + pltpu.roll(terms, SUM_ROWS - 4, 0)
    return jnp.where(lax.broadcasted_iota(jnp.int32, sums.shape, 0) < 2, sums, 0.0)


def product_kernel(summed, matrix_ref, tops_ref, ends_ref, springs_ref, *refs):
    *refs, out_ref, load_ref, right_ref, left_ref = refs
    top = tops_ref.shape[1]
    add_product(
        out_ref,
        jnp.dot(matrix_ref[:, :top], tops_ref[0], preferred_element_type=f32)
        + jnp.dot(matrix_ref[:, top:], ends_ref[0], preferred_element_type=f32),
    )

    @at_end
    def _():
        sectors, height, _ = load_ref.shape
        cases = out_ref.shape[1] // sectors
        quarter = right_ref.shape[0]
        left_ref[...] = out_ref[:quarter].astype(bf16)
        right_ref[...] = out_ref[quarter : 2 * quarter].astype(bf16)
        for at in range((height - TERM_ROWS) // cases):
            rows = slice(at * LANES, (at + 1) * LANES)
            turned = (out_ref[rows].T * springs_ref[:, rows]).astype(load_ref.dtype)
            for s in range(sectors):
                load_ref[s, at * cases : (at + 1) * cases] = turned[s * cases : (s + 1) * cases]
        terms = in_terms(refs[0][...]) if summed else jnp.zeros((TERM_ROWS, LANES), f32)
        for s in range(sectors):
            load_ref[s, height - TERM_ROWS :] = terms.astype(load_ref.dtype)


def pack_kernel(before_ref, after_ref, parts_ref, out_ref):
    quarter = before_ref.shape[0]
    height = parts_ref.shape[1] - TERM_ROWS
    out_ref[:quarter] = before_ref[...]
    out_ref[quarter : 2 * quarter] = after_ref[...]
    total = jnp.sum(parts_ref[...].astype(f32), axis=0)
    out_ref[2 * quarter : 2 * quarter + height] = total[:height].astype(bf16)
    out_ref[2 * quarter + height :] = in_terms(from_terms(total[height:])).astype(bf16)


def alpha_from(sums):
    return sums[0:1] / (sums[1:2] + 1e-06)


def hub_kernel(cases, matrix_ref, pieces_ref, out_ref, total_ref):
    height = out_ref.shape[1]
    chunks = height // cases
    first = pieces_ref.shape[1] - TERM_ROWS - height
    load = jnp.concatenate(
        [pieces_ref[0, first + c * cases : first + (c + 1) * cases] for c in range(chunks)], axis=1
    )
    add_product(
        total_ref,
        lax.dot_general(
            load, matrix_ref[...], (((1,), (1,)), ((), ())), preferred_element_type=f32
        ),
    )

    @at_end
    def _():
        for c in range(chunks):
            block = total_ref[:, c * LANES : (c + 1) * LANES].astype(out_ref.dtype)
            for s in range(out_ref.shape[0]):
                out_ref[s, c * cases : (c + 1) * cases] = block


def base_kernel(first, matrix_ref, pieces_ref, product_ref, stiffness_ref, *refs):
    if first:
        base_ref, ends_ref, factor_ref, sums_ref = refs
    else:
        *refs, base_ref, ends_ref, factor_ref, left_ref, newer_ref, better_ref, sums_ref = refs
        image_ref, residual_ref, precon_ref = refs[:3]
    depth = matrix_ref.shape[1]
    add_product(
        base_ref, jnp.dot(matrix_ref[...], pieces_ref[0, :depth], preferred_element_type=f32)
    )
    add_product(sums_ref, from_terms(pieces_ref[0, pieces_ref.shape[1] - TERM_ROWS :]))

    @at_end
    def _():
        base = base_ref[...] + stiffness_ref[...] * product_ref[...]
        if first:
            factor_ref[...] = jnp.ones_like(factor_ref)
        else:
            alpha = alpha_from(sums_ref[...])
            factor_ref[...] = jnp.broadcast_to(-alpha, factor_ref.shape)
            base = image_ref[...] - alpha * base
            left_ref[...] = residual_ref[...] - alpha * image_ref[...]
            gain = alpha * precon_ref[...]
            better_ref[...] = refs[3][...] + gain if len(refs) > 3 else gain
            newer_ref[...] = precon_ref[...] - alpha * product_ref[...]
        base_ref[...] = base
        end = base[base.shape[0] - ends_ref.shape[1] :].astype(bf16)
        ends_ref[...] = jnp.broadcast_to(end[None], ends_ref.shape)


def image_kernel(base_ref, hubs_ref, springs_ref, factor_ref, residual_ref, image_ref, top_ref, sums_ref):
    sectors, height, _ = hubs_ref.shape
    attached = top_ref.shape[0]
    chunks = attached // LANES
    cases = height // chunks
    factor = factor_ref[0:1]
    for c in range(chunks):
        at = slice(c * LANES, (c + 1) * LANES)
        hub = jnp.concatenate([hubs_ref[s, c * cases : (c + 1) * cases] for s in range(sectors)], axis=0)
        image = base_ref[at] - factor * (hub.astype(f32) * springs_ref[:, at]).T
        image_ref[at] = image
        top_ref[at] = image.astype(bf16)
    image_ref[attached:] = base_ref[attached:]
    image = image_ref[...]
    upper = jnp.sum(image * residual_ref[...], axis=0, keepdims=True)
    lower = jnp.sum(image * image, axis=0, keepdims=True)
    rest = jnp.zeros((SUM_ROWS - 2, image.shape[1]), f32)
    sums = jnp.concatenate([upper, lower, rest], axis=0)
    sums_ref[...] = jnp.broadcast_to(sums, sums_ref.shape)


def last_kernel(sums_ref, image_ref, residual_ref, precon_ref, solution_ref, newer_ref, left_ref):
    alpha = alpha_from(jnp.sum(sums_ref[...], axis=0))
    newer_ref[0] = solution_ref[...] + alpha * precon_ref[...]
    left_ref[0] = residual_ref[...] - alpha * image_ref[...]


def last_update(sums, *state):
    rows, loads = state[0].shape
    height = rows // 4
    block = pl.BlockSpec((height, loads), lambda k: (k, 0))
    out_block = pl.BlockSpec((1, height, loads), lambda k: (0, k, 0))
    out = shape(1, rows, loads)
    return pl.pallas_call(
        last_kernel,
        grid=(4,),
        in_specs=[pl.BlockSpec(sums.shape, lambda k: (0, 0, 0))] + [block] * len(state),
        out_specs=(out_block, out_block),
        out_shape=(out, out),
        compiler_params=pltpu.CompilerParams(vmem_limit_bytes=60 * MIB),
    )(sums, *state)


def round_kernel(field_ref, top_ref, ends_ref):
    attached = top_ref.shape[0]
    top_ref[...] = field_ref[0, :attached].astype(bf16)
    end = field_ref[0, attached:].astype(bf16)
    ends_ref[...] = jnp.broadcast_to(end[None], ends_ref.shape)


def exchange(blocks, axes):
    return lax.all_to_all(blocks, axes, split_axis=0, concat_axis=0)


def gathered(field):
    return lax.all_gather(field, "dof", axis=0)


def around(sectors):
    onward = [(s, (s + 1) % sectors) for s in range(sectors)]
    return onward, [(b, a) for a, b in onward]


def alpha_of(sums):
    return alpha_from(jnp.sum(sums, axis=0))[0]


def tiled_body(rhs, diagonal, coupling, springs, precond, hub_inverse):
    residual = rhs[0]
    rows, loads = residual.shape
    attached = springs.shape[1]
    quarter = rows - attached
    sectors, parts = lax.axis_size("sector"), lax.axis_size("dof")
    cases = loads // sectors
    height = attached // LANES * cases
    onward, backward = around(sectors)
    full, face = shape(rows, loads), shape(quarter, loads, dtype=bf16)
    top_shape, ends_shape = shape(attached, loads, dtype=bf16), shape(parts, quarter, loads, dtype=bf16)

    stiffness = diagonal[0] + jnp.pad(springs[0], (0, quarter))
    stiffness = jnp.broadcast_to(stiffness[:, None], (rows, loads))
    state = sums = ()

    top, ends = call(round_kernel, (top_shape, ends_shape), (rhs,))
    for step in range(ITERS):
        first, last = step == 0, step == ITERS - 1
        sent = f32 if first else bf16
        product, load, right, left = call(
            functools.partial(product_kernel, not first),
            (full, shape(sectors, height + TERM_ROWS, LANES, dtype=sent), face, face),
            (precond, gathered(top), exchange(ends, "dof"), springs, *sums),
            parted=(0, 1, 2),
            steps=parts,
            flops=2 * precond.size * loads,
        )
        before = lax.ppermute(right, "sector", onward)
        after = lax.ppermute(left, "sector", backward)
        packed = call(
            pack_kernel,
            shape(2 * quarter + height + TERM_ROWS, loads, dtype=bf16),
            (before, after, exchange(load, "sector")),
            small=True,
        )
        pieces = gathered(packed)
        hub = call(
            functools.partial(hub_kernel, cases),
            shape(sectors, height, LANES, dtype=sent),
            (hub_inverse, pieces),
            parted=(0, 1),
            steps=parts,
            scratch=(pltpu.VMEM((cases, attached), f32),),
            flops=2 * hub_inverse.size * cases,
        )
        hubs = exchange(hub, "sector")
        base, ends, factor, *state = call(
            functools.partial(base_kernel, first),
            (full, ends_shape, shape(SUM_ROWS, loads)) + (() if first else (full, full, full)),
            (coupling[0], pieces, product, stiffness, *state),
            parted=(0, 1),
            steps=parts,
            scratch=(pltpu.VMEM((SUM_ROWS, loads), f32),),
            flops=2 * coupling.size * loads,
        )
        residual, precon, *solution = (residual, product) if first else state
        image, top, sums = call(
            image_kernel,
            (
                full,
                top_shape,
                shape(sectors * parts, SUM_ROWS, loads) if last else shape(SUM_ROWS, loads),
            ),
            (base, hubs, springs, factor, residual),
        )
        state = (image, residual, precon, *solution)
        sums = (sums,)
    return last_update(exchange(*sums, ("sector", "dof")), *state)


def plain_body(rhs, diagonal, coupling, springs, precond, hub_inverse):
    residual = rhs[0]
    spring_rows = springs[0][:, None]
    rows, loads = residual.shape
    quarter = rows // 4
    sectors = lax.axis_size("sector")
    onward, backward = around(sectors)
    solution = jnp.zeros_like(residual)

    def whole(field):
        return gathered(field.astype(bf16)).reshape(-1, loads)

    def copies(cells, axes):
        count = lax.axis_size(axes)
        return exchange(jnp.broadcast_to(cells[None], (count,) + cells.shape), axes)

    precon = jnp.dot(precond, whole(residual), preferred_element_type=f32)
    for step in range(ITERS):
        faces = precon[: 2 * quarter].astype(bf16)
        before = lax.ppermute(faces[quarter:], "sector", onward)
        after = lax.ppermute(faces[:quarter], "sector", backward)
        couple = jnp.dot(
            coupling[0], whole(jnp.concatenate([before, after])), preferred_element_type=f32
        )
        attached = precon[: 3 * quarter]
        load = (spring_rows * attached).T.reshape(sectors, loads // sectors, -1)
        load = jnp.sum(exchange(load, "sector"), axis=0).astype(bf16)
        load = copies(load, "dof").transpose(0, 2, 1).reshape(hub_inverse.shape[1], -1)
        hub = jnp.dot(hub_inverse, load, preferred_element_type=f32)
        hub = copies(hub.T, "sector").reshape(loads, -1).T
        pull = jnp.pad(spring_rows * (attached - hub), ((0, quarter), (0, 0)))
        image = diagonal[0][:, None] * precon + couple + pull
        sums = jnp.stack([jnp.sum(image * residual, axis=0), jnp.sum(image * image, axis=0)])
        alpha = alpha_of(copies(sums, ("sector", "dof")))
        solution = solution + alpha * precon
        residual = residual - alpha * image
        if step < ITERS - 1:
            change = jnp.dot(precond, whole(image), preferred_element_type=f32)
            precon = precon - alpha * change
    return (solution[None], residual[None])


def body(rhs, *rest):
    rows, loads = rhs.shape[1:]
    cases = loads // lax.axis_size("sector")
    tiled = loads == LANES and (rows // 4) % LANES == 0 and cases % 16 == 0
    return (tiled_body if tiled else plain_body)(rhs, *rest)


def solution(mesh):
    placed = (
        P("sector", "dof", None),
        P("sector", "dof"),
        P("sector", "dof", None),
        P("sector", "dof"),
        P("dof", None),
        P("dof", None),
    )
    return jax.shard_map(
        body,
        mesh=mesh,
        in_specs=placed,
        out_specs=(P("sector", "dof", None), P("sector", "dof", None)),
        check_vma=False,
    )
```

```python
import functools

import jax
import jax.numpy as jnp
from jax import lax
from jax.experimental import pallas as pl
from jax.experimental.pallas import tpu as pltpu
from jax.sharding import PartitionSpec as P

ITERS = 3
LANES = 128
MIB = 1024 * 1024
SUM_ROWS = 8
TERM_ROWS = 16
f32 = jnp.float32
bf16 = jnp.bfloat16


def shape(*dims, dtype=f32):
    return jax.ShapeDtypeStruct(dims, dtype)


def call(kernel, outs, operands, flops=0):
    whole = pl.BlockSpec(memory_space=pltpu.VMEM)
    return pl.pallas_call(
        kernel,
        in_specs=[whole] * len(operands),
        out_specs=jax.tree.map(lambda _: whole, outs),
        out_shape=outs,
        compiler_params=pltpu.CompilerParams(vmem_limit_bytes=20 * MIB),
        cost_estimate=pl.CostEstimate(
            flops=flops, bytes_accessed=sum(x.size * x.dtype.itemsize for x in operands), transcendentals=0
        ),
    )(*operands)


def in_terms(sums):
    terms = None
    for at in range(3):
        term = sums.astype(bf16).astype(f32)
        sums = sums - term
        terms = term if at == 0 else terms + pltpu.roll(term, 2 * at, 0)
    return jnp.concatenate([terms, jnp.zeros_like(terms)], axis=0)


def from_terms(terms):
    terms = terms[:SUM_ROWS].astype(f32)
    sums = terms + pltpu.roll(terms, SUM_ROWS - 2, 0) + pltpu.roll(terms, SUM_ROWS - 4, 0)
    return jnp.where(lax.broadcasted_iota(jnp.int32, sums.shape, 0) < 2, sums, 0.0)


def product_kernel(parts, matrix_ref, springs_ref, tops_ref, *refs):
    *refs, out_ref, load_ref, right_ref, left_ref = refs
    here = lax.axis_index("dof")
    _, top, _ = tops_ref.shape
    for part in range(parts):
        end_ref = refs[part]
        end = end_ref.shape[0]
        start = part * (top + end)
        owner = lax.rem(here + part, parts)
        product = jnp.dot(
            matrix_ref[:, start : start + top], tops_ref[part], preferred_element_type=f32
        ) + jnp.dot(
            matrix_ref[:, pl.ds(pl.multiple_of(owner * (top + end) + top, LANES), end)],
            end_ref[...],
            preferred_element_type=f32,
        )
        if part:
            out_ref[...] += product
        else:
            out_ref[...] = product

    sectors, height, _ = load_ref.shape
    cases = out_ref.shape[1] // sectors
    quarter = right_ref.shape[0]
    left_ref[...] = out_ref[:quarter].astype(bf16)
    right_ref[...] = out_ref[quarter : 2 * quarter].astype(bf16)
    for at in range((height - TERM_ROWS) // cases):
        rows = slice(at * LANES, (at + 1) * LANES)
        turned = (out_ref[rows].T * springs_ref[:, rows]).astype(load_ref.dtype)
        for s in range(sectors):
            load_ref[s, at * cases : (at + 1) * cases] = turned[s * cases : (s + 1) * cases]
    terms = in_terms(refs[parts][...]) if refs[parts:] else jnp.zeros((TERM_ROWS, LANES), f32)
    for s in range(sectors):
        load_ref[s, height - TERM_ROWS :] = terms.astype(load_ref.dtype)


def pack_kernel(before_ref, after_ref, *refs):
    *part_refs, out_ref = refs
    quarter = before_ref.shape[0]
    height = part_refs[0].shape[0] - TERM_ROWS
    out_ref[:quarter] = before_ref[...]
    out_ref[quarter : 2 * quarter] = after_ref[...]
    total = sum(ref[...].astype(f32) for ref in part_refs)
    out_ref[2 * quarter : 2 * quarter + height] = total[:height].astype(bf16)
    out_ref[2 * quarter + height :] = in_terms(from_terms(total[height:])).astype(bf16)


def alpha_from(sums):
    return sums[0:1] / (sums[1:2] + 1e-06)


def hub_kernel(cases, matrix_ref, pieces_ref, out_ref):
    parts = pieces_ref.shape[0]
    height = out_ref.shape[0]
    chunks = height // cases
    depth = chunks * LANES
    first = pieces_ref.shape[1] - TERM_ROWS - height
    total = None
    for part in range(parts):
        load = jnp.concatenate(
            [pieces_ref[part, first + c * cases : first + (c + 1) * cases] for c in range(chunks)], axis=1
        )
        product = lax.dot_general(
            load,
            matrix_ref[:, part * depth : (part + 1) * depth],
            (((1,), (1,)), ((), ())),
            preferred_element_type=f32,
        )
        total = product if total is None else total + product
    for c in range(chunks):
        out_ref[c * cases : (c + 1) * cases] = total[:, c * LANES : (c + 1) * LANES].astype(out_ref.dtype)


def base_kernel(first, matrix_ref, pieces_ref, product_ref, stiffness_ref, *refs):
    if first:
        base_ref, end_ref, factor_ref = refs
    else:
        *refs, base_ref, end_ref, factor_ref, left_ref, newer_ref, better_ref = refs
        image_ref, residual_ref, precon_ref = refs[:3]
    parts, height, _ = pieces_ref.shape
    depth = matrix_ref.shape[1] // parts
    base_ref[...] = stiffness_ref[...] * product_ref[...]
    for part in range(parts):
        base_ref[...] += jnp.dot(
            matrix_ref[:, part * depth : (part + 1) * depth],
            pieces_ref[part, :depth],
            preferred_element_type=f32,
        )
    if first:
        factor_ref[...] = jnp.ones_like(factor_ref)
    else:
        alpha = alpha_from(sum(from_terms(pieces_ref[part, height - TERM_ROWS :]) for part in range(parts)))
        factor_ref[...] = jnp.broadcast_to(-alpha, factor_ref.shape)
        base_ref[...] = image_ref[...] - alpha * base_ref[...]
        left_ref[...] = residual_ref[...] - alpha * image_ref[...]
        gain = alpha * precon_ref[...]
        better_ref[...] = refs[3][...] + gain if len(refs) > 3 else gain
        newer_ref[...] = precon_ref[...] - alpha * product_ref[...]
    end_ref[...] = base_ref[base_ref.shape[0] - end_ref.shape[0] :].astype(bf16)


def image_kernel(sectors, base_ref, springs_ref, factor_ref, residual_ref, *refs):
    *hub_refs, image_ref, top_ref, sums_ref, hubs_ref = refs
    here = lax.axis_index("sector")
    for ahead in range(sectors):
        hubs_ref[lax.rem(here + ahead, sectors)] = hub_refs[ahead][...].astype(f32)
    attached = top_ref.shape[0]
    chunks = attached // LANES
    cases = hubs_ref.shape[1] // chunks
    factor = factor_ref[0:1]
    for c in range(chunks):
        at = slice(c * LANES, (c + 1) * LANES)
        hub = jnp.concatenate([hubs_ref[s, c * cases : (c + 1) * cases] for s in range(sectors)], axis=0)
        image = base_ref[at] - factor * (hub * springs_ref[:, at]).T
        image_ref[at] = image
        top_ref[at] = image.astype(bf16)
    image_ref[attached:] = base_ref[attached:]
    image = image_ref[...]
    upper = jnp.sum(image * residual_ref[...], axis=0, keepdims=True)
    lower = jnp.sum(image * image, axis=0, keepdims=True)
    rest = jnp.zeros((SUM_ROWS - 2, image.shape[1]), f32)
    sums = jnp.concatenate([upper, lower, rest], axis=0)
    sums_ref[...] = jnp.broadcast_to(sums, sums_ref.shape)


def last_kernel(sums_ref, image_ref, residual_ref, precon_ref, solution_ref, newer_ref, left_ref):
    alpha = alpha_from(jnp.sum(sums_ref[...], axis=0))
    newer_ref[0] = solution_ref[...] + alpha * precon_ref[...]
    left_ref[0] = residual_ref[...] - alpha * image_ref[...]


def last_update(sums, *state):
    rows, loads = state[0].shape
    height = rows // 4
    block = pl.BlockSpec((height, loads), lambda k: (k, 0))
    out_block = pl.BlockSpec((1, height, loads), lambda k: (0, k, 0))
    out = shape(1, rows, loads)
    return pl.pallas_call(
        last_kernel,
        grid=(4,),
        in_specs=[pl.BlockSpec(sums.shape, lambda k: (0, 0, 0))] + [block] * len(state),
        out_specs=(out_block, out_block),
        out_shape=(out, out),
        compiler_params=pltpu.CompilerParams(vmem_limit_bytes=60 * MIB),
    )(sums, *state)


def round_kernel(field_ref, top_ref, end_ref):
    attached = top_ref.shape[0]
    top_ref[...] = field_ref[0, :attached].astype(bf16)
    end_ref[...] = field_ref[0, attached:].astype(bf16)


def exchange(blocks, axes):
    return lax.all_to_all(blocks, axes, split_axis=0, concat_axis=0)


def from_ahead(cells, axis, distance):
    count = lax.axis_size(axis)
    return lax.ppermute(cells, axis, [((i + distance) % count, i) for i in range(count)])


def one_from_each(cells, axis):
    return [cells] + [from_ahead(cells, axis, d) for d in range(1, lax.axis_size(axis))]


def mine_from_each(blocks, axis):
    count, here = lax.axis_size(axis), lax.axis_index(axis)
    own = [lax.dynamic_index_in_dim(blocks, (here - d) % count, 0, False) for d in range(count)]
    return own[:1] + [from_ahead(own[d], axis, d) for d in range(1, count)]


def gathered(field):
    return lax.all_gather(field, "dof", axis=0)


def around(sectors):
    onward = [(s, (s + 1) % sectors) for s in range(sectors)]
    return onward, [(b, a) for a, b in onward]


def alpha_of(sums):
    return alpha_from(jnp.sum(sums, axis=0))[0]


def tiled_body(rhs, diagonal, coupling, springs, precond, hub_inverse):
    residual = rhs[0]
    rows, loads = residual.shape
    attached = springs.shape[1]
    quarter = rows - attached
    sectors, parts = lax.axis_size("sector"), lax.axis_size("dof")
    cases = loads // sectors
    height = attached // LANES * cases
    onward, backward = around(sectors)
    full, face = shape(rows, loads), shape(quarter, loads, dtype=bf16)
    top_shape = shape(attached, loads, dtype=bf16)

    stiffness = diagonal[0] + jnp.pad(springs[0], (0, quarter))
    stiffness = jnp.broadcast_to(stiffness[:, None], (rows, loads))
    state = sums = ()

    top, end = call(round_kernel, (top_shape, face), (rhs,))
    for step in range(ITERS):
        first, last = step == 0, step == ITERS - 1
        sent = f32 if first else bf16
        product, load, right, left = call(
            functools.partial(product_kernel, parts),
            (full, shape(sectors, height + TERM_ROWS, LANES, dtype=sent), face, face),
            (precond, springs, gathered(top), *one_from_each(end, "dof"), *sums),
            flops=2 * precond.size * loads,
        )
        before = lax.ppermute(right, "sector", onward)
        after = lax.ppermute(left, "sector", backward)
        packed = call(
            pack_kernel,
            shape(2 * quarter + height + TERM_ROWS, loads, dtype=bf16),
            (before, after, *mine_from_each(load, "sector")),
        )
        pieces = gathered(packed)
        hub = call(
            functools.partial(hub_kernel, cases),
            shape(height, LANES, dtype=sent),
            (hub_inverse, pieces),
            flops=2 * hub_inverse.size * cases,
        )
        hubs = one_from_each(hub, "sector")
        base, end, factor, *state = call(
            functools.partial(base_kernel, first),
            (full, face, shape(SUM_ROWS, loads)) + (() if first else (full, full, full)),
            (coupling[0], pieces, product, stiffness, *state),
            flops=2 * coupling.size * loads,
        )
        residual, precon, *solution = (residual, product) if first else state
        sums_shape = shape(sectors * parts, SUM_ROWS, loads) if last else shape(SUM_ROWS, loads)
        image, top, sums, _ = call(
            functools.partial(image_kernel, sectors),
            (full, top_shape, sums_shape, shape(sectors, height, LANES)),
            (base, springs, factor, residual, *hubs),
        )
        state = (image, residual, precon, *solution)
        sums = (sums,)
    out = shape(1, rows, loads)
    return call(last_kernel, (out, out), (exchange(*sums, ("sector", "dof")), *state))


def plain_body(rhs, diagonal, coupling, springs, precond, hub_inverse):
    residual = rhs[0]
    spring_rows = springs[0][:, None]
    rows, loads = residual.shape
    quarter = rows // 4
    sectors = lax.axis_size("sector")
    onward, backward = around(sectors)
    solution = jnp.zeros_like(residual)

    def whole(field):
        return gathered(field.astype(bf16)).reshape(-1, loads)

    def copies(cells, axes):
        count = lax.axis_size(axes)
        return exchange(jnp.broadcast_to(cells[None], (count,) + cells.shape), axes)

    precon = jnp.dot(precond, whole(residual), preferred_element_type=f32)
    for step in range(ITERS):
        faces = precon[: 2 * quarter].astype(bf16)
        before = lax.ppermute(faces[quarter:], "sector", onward)
        after = lax.ppermute(faces[:quarter], "sector", backward)
        couple = jnp.dot(
            coupling[0], whole(jnp.concatenate([before, after])), preferred_element_type=f32
        )
        attached = precon[: 3 * quarter]
        load = (spring_rows * attached).T.reshape(sectors, loads // sectors, -1)
        load = jnp.sum(exchange(load, "sector"), axis=0).astype(bf16)
        load = copies(load, "dof").transpose(0, 2, 1).reshape(hub_inverse.shape[1], -1)
        hub = jnp.dot(hub_inverse, load, preferred_element_type=f32)
        hub = copies(hub.T, "sector").reshape(loads, -1).T
        pull = jnp.pad(spring_rows * (attached - hub), ((0, quarter), (0, 0)))
        image = diagonal[0][:, None] * precon + couple + pull
        sums = jnp.stack([jnp.sum(image * residual, axis=0), jnp.sum(image * image, axis=0)])
        alpha = alpha_of(copies(sums, ("sector", "dof")))
        solution = solution + alpha * precon
        residual = residual - alpha * image
        if step < ITERS - 1:
            change = jnp.dot(precond, whole(image), preferred_element_type=f32)
            precon = precon - alpha * change
    return (solution[None], residual[None])


def body(rhs, *rest):
    rows, loads = rhs.shape[1:]
    cases = loads // lax.axis_size("sector")
    tiled = loads == LANES and (rows // 4) % LANES == 0 and cases % 16 == 0
    return (tiled_body if tiled else plain_body)(rhs, *rest)


def solution(mesh):
    placed = (
        P("sector", "dof", None),
        P("sector", "dof"),
        P("sector", "dof", None),
        P("sector", "dof"),
        P("dof", None),
        P("dof", None),
    )
    return jax.shard_map(
        body,
        mesh=mesh,
        in_specs=placed,
        out_specs=(P("sector", "dof", None), P("sector", "dof", None)),
        check_vma=False,
    )
```

```python
import functools

import jax
import jax.numpy as jnp
from jax import lax
from jax.experimental import pallas as pl
from jax.experimental.pallas import tpu as pltpu
from jax.sharding import PartitionSpec as P

ITERS = 3
LANES = 128
MIB = 1024 * 1024
SUM_ROWS = 8
TERM_ROWS = 16
f32 = jnp.float32
bf16 = jnp.bfloat16


def shape(*dims, dtype=f32):
    return jax.ShapeDtypeStruct(dims, dtype)


def call(kernel, outs, operands, flops=0):
    whole = pl.BlockSpec(memory_space=pltpu.VMEM)
    return pl.pallas_call(
        kernel,
        in_specs=[whole] * len(operands),
        out_specs=jax.tree.map(lambda _: whole, outs),
        out_shape=outs,
        compiler_params=pltpu.CompilerParams(vmem_limit_bytes=20 * MIB),
        cost_estimate=pl.CostEstimate(
            flops=flops, bytes_accessed=sum(x.size * x.dtype.itemsize for x in operands), transcendentals=0
        ),
    )(*operands)


def in_terms(sums):
    terms = None
    for at in range(3):
        term = sums.astype(bf16).astype(f32)
        sums = sums - term
        terms = term if at == 0 else terms + pltpu.roll(term, 2 * at, 0)
    return jnp.concatenate([terms, jnp.zeros_like(terms)], axis=0)


def from_terms(terms):
    terms = terms[:SUM_ROWS].astype(f32)
    sums = terms + pltpu.roll(terms, SUM_ROWS - 2, 0) + pltpu.roll(terms, SUM_ROWS - 4, 0)
    return jnp.where(lax.broadcasted_iota(jnp.int32, sums.shape, 0) < 2, sums, 0.0)


def product_kernel(parts, matrix_ref, springs_ref, tops_ref, *refs):
    *refs, out_ref, load_ref, right_ref, left_ref = refs
    here = lax.axis_index("dof")
    _, top, _ = tops_ref.shape
    for part in range(parts):
        end_ref = refs[part]
        end = end_ref.shape[0]
        start = part * (top + end)
        owner = lax.rem(here + part, parts)
        product = jnp.dot(
            matrix_ref[:, start : start + top], tops_ref[part], preferred_element_type=f32
        ) + jnp.dot(
            matrix_ref[:, pl.ds(pl.multiple_of(owner * (top + end) + top, LANES), end)],
            end_ref[...],
            preferred_element_type=f32,
        )
        if part:
            out_ref[...] += product
        else:
            out_ref[...] = product

    sectors, height, _ = load_ref.shape
    cases = out_ref.shape[1] // sectors
    quarter = right_ref.shape[0]
    left_ref[...] = out_ref[:quarter].astype(bf16)
    right_ref[...] = out_ref[quarter : 2 * quarter].astype(bf16)
    for at in range((height - TERM_ROWS) // cases):
        rows = slice(at * LANES, (at + 1) * LANES)
        turned = (out_ref[rows].T * springs_ref[:, rows]).astype(load_ref.dtype)
        for s in range(sectors):
            load_ref[s, at * cases : (at + 1) * cases] = turned[s * cases : (s + 1) * cases]
    terms = in_terms(refs[parts][...]) if refs[parts:] else jnp.zeros((TERM_ROWS, LANES), f32)
    for s in range(sectors):
        load_ref[s, height - TERM_ROWS :] = terms.astype(load_ref.dtype)


def join_kernel(before_ref, after_ref, out_ref):
    quarter = before_ref.shape[0]
    out_ref[:quarter] = before_ref[...]
    out_ref[quarter:] = after_ref[...]


def slice_kernel(*refs):
    *part_refs, out_ref = refs
    height = out_ref.shape[0] - TERM_ROWS
    total = sum(ref[...].astype(f32) for ref in part_refs)
    out_ref[:height] = total[:height].astype(bf16)
    out_ref[height:] = in_terms(from_terms(total[height:])).astype(bf16)


def alpha_from(sums):
    return sums[0:1] / (sums[1:2] + 1e-06)


def block_columns(matrix_ref, parts, ahead):
    width = matrix_ref.shape[1] // parts
    owner = lax.rem(lax.axis_index("dof") + ahead, parts)
    return matrix_ref[:, pl.ds(pl.multiple_of(owner * width, LANES), width)]


def hub_kernel(cases, matrix_ref, *refs):
    *load_refs, out_ref = refs
    parts = len(load_refs)
    chunks = out_ref.shape[0] // cases
    total = None
    for part, ref in enumerate(load_refs):
        load = jnp.concatenate([ref[c * cases : (c + 1) * cases] for c in range(chunks)], axis=1)
        product = lax.dot_general(
            load,
            block_columns(matrix_ref, parts, part),
            (((1,), (1,)), ((), ())),
            preferred_element_type=f32,
        )
        total = product if total is None else total + product
    for c in range(chunks):
        out_ref[c * cases : (c + 1) * cases] = total[:, c * LANES : (c + 1) * LANES].astype(out_ref.dtype)


def base_kernel(first, parts, matrix_ref, product_ref, stiffness_ref, *refs):
    face_refs, load_refs, refs = refs[:parts], refs[parts : 2 * parts], refs[2 * parts :]
    if first:
        base_ref, end_ref, factor_ref = refs
    else:
        *refs, base_ref, end_ref, factor_ref, left_ref, newer_ref, better_ref = refs
        image_ref, residual_ref, precon_ref = refs[:3]
    base_ref[...] = stiffness_ref[...] * product_ref[...]
    for part, ref in enumerate(face_refs):
        base_ref[...] += jnp.dot(
            block_columns(matrix_ref, parts, part), ref[...], preferred_element_type=f32
        )
    if first:
        factor_ref[...] = jnp.ones_like(factor_ref)
    else:
        alpha = alpha_from(sum(from_terms(ref[ref.shape[0] - TERM_ROWS :]) for ref in load_refs))
        factor_ref[...] = jnp.broadcast_to(-alpha, factor_ref.shape)
        base_ref[...] = image_ref[...] - alpha * base_ref[...]
        left_ref[...] = residual_ref[...] - alpha * image_ref[...]
        gain = alpha * precon_ref[...]
        better_ref[...] = refs[3][...] + gain if len(refs) > 3 else gain
        newer_ref[...] = precon_ref[...] - alpha * product_ref[...]
    end_ref[...] = base_ref[base_ref.shape[0] - end_ref.shape[0] :].astype(bf16)


def image_kernel(sectors, base_ref, springs_ref, factor_ref, residual_ref, *refs):
    *hub_refs, image_ref, top_ref, sums_ref, hubs_ref = refs
    here = lax.axis_index("sector")
    for ahead in range(sectors):
        hubs_ref[lax.rem(here + ahead, sectors)] = hub_refs[ahead][...].astype(f32)
    attached = top_ref.shape[0]
    chunks = attached // LANES
    cases = hubs_ref.shape[1] // chunks
    factor = factor_ref[0:1]
    for c in range(chunks):
        at = slice(c * LANES, (c + 1) * LANES)
        hub = jnp.concatenate([hubs_ref[s, c * cases : (c + 1) * cases] for s in range(sectors)], axis=0)
        image = base_ref[at] - factor * (hub * springs_ref[:, at]).T
        image_ref[at] = image
        top_ref[at] = image.astype(bf16)
    image_ref[attached:] = base_ref[attached:]
    image = image_ref[...]
    upper = jnp.sum(image * residual_ref[...], axis=0, keepdims=True)
    lower = jnp.sum(image * image, axis=0, keepdims=True)
    rest = jnp.zeros((SUM_ROWS - 2, image.shape[1]), f32)
    sums = jnp.concatenate([upper, lower, rest], axis=0)
    sums_ref[...] = jnp.broadcast_to(sums, sums_ref.shape)


def last_kernel(sums_ref, image_ref, residual_ref, precon_ref, solution_ref, newer_ref, left_ref):
    alpha = alpha_from(jnp.sum(sums_ref[...], axis=0))
    newer_ref[0] = solution_ref[...] + alpha * precon_ref[...]
    left_ref[0] = residual_ref[...] - alpha * image_ref[...]


def last_update(sums, *state):
    rows, loads = state[0].shape
    height = rows // 4
    block = pl.BlockSpec((height, loads), lambda k: (k, 0))
    out_block = pl.BlockSpec((1, height, loads), lambda k: (0, k, 0))
    out = shape(1, rows, loads)
    return pl.pallas_call(
        last_kernel,
        grid=(4,),
        in_specs=[pl.BlockSpec(sums.shape, lambda k: (0, 0, 0))] + [block] * len(state),
        out_specs=(out_block, out_block),
        out_shape=(out, out),
        compiler_params=pltpu.CompilerParams(vmem_limit_bytes=60 * MIB),
    )(sums, *state)


def round_kernel(field_ref, top_ref, end_ref):
    attached = top_ref.shape[0]
    top_ref[...] = field_ref[0, :attached].astype(bf16)
    end_ref[...] = field_ref[0, attached:].astype(bf16)


def exchange(blocks, axes):
    return lax.all_to_all(blocks, axes, split_axis=0, concat_axis=0)


def from_ahead(cells, axis, distance):
    count = lax.axis_size(axis)
    return lax.ppermute(cells, axis, [((i + distance) % count, i) for i in range(count)])


def one_from_each(cells, axis):
    return [cells] + [from_ahead(cells, axis, d) for d in range(1, lax.axis_size(axis))]


def mine_from_each(blocks, axis):
    count, here = lax.axis_size(axis), lax.axis_index(axis)
    own = [lax.dynamic_index_in_dim(blocks, (here - d) % count, 0, False) for d in range(count)]
    return own[:1] + [from_ahead(own[d], axis, d) for d in range(1, count)]


def gathered(field):
    return lax.all_gather(field, "dof", axis=0)


def around(sectors):
    onward = [(s, (s + 1) % sectors) for s in range(sectors)]
    return onward, [(b, a) for a, b in onward]


def alpha_of(sums):
    return alpha_from(jnp.sum(sums, axis=0))[0]


def tiled_body(rhs, diagonal, coupling, springs, precond, hub_inverse):
    residual = rhs[0]
    rows, loads = residual.shape
    attached = springs.shape[1]
    quarter = rows - attached
    sectors, parts = lax.axis_size("sector"), lax.axis_size("dof")
    cases = loads // sectors
    height = attached // LANES * cases
    onward, backward = around(sectors)
    full, face = shape(rows, loads), shape(quarter, loads, dtype=bf16)
    top_shape = shape(attached, loads, dtype=bf16)

    stiffness = diagonal[0] + jnp.pad(springs[0], (0, quarter))
    stiffness = jnp.broadcast_to(stiffness[:, None], (rows, loads))
    state = sums = ()

    top, end = call(round_kernel, (top_shape, face), (rhs,))
    for step in range(ITERS):
        first, last = step == 0, step == ITERS - 1
        sent = f32 if first else bf16
        product, load, right, left = call(
            functools.partial(product_kernel, parts),
            (full, shape(sectors, height + TERM_ROWS, LANES, dtype=sent), face, face),
            (precond, springs, gathered(top), *one_from_each(end, "dof"), *sums),
            flops=2 * precond.size * loads,
        )
        before = lax.ppermute(right, "sector", onward)
        after = lax.ppermute(left, "sector", backward)
        faces = call(join_kernel, shape(2 * quarter, loads, dtype=bf16), (before, after))
        faces = one_from_each(faces, "dof")
        load = call(
            slice_kernel,
            shape(height + TERM_ROWS, loads, dtype=bf16),
            mine_from_each(load, "sector"),
        )
        slices = one_from_each(load, "dof")
        hub = call(
            functools.partial(hub_kernel, cases),
            shape(height, LANES, dtype=sent),
            (hub_inverse, *slices),
            flops=2 * hub_inverse.size * cases,
        )
        hubs = one_from_each(hub, "sector")
        base, end, factor, *state = call(
            functools.partial(base_kernel, first, parts),
            (full, face, shape(SUM_ROWS, loads)) + (() if first else (full, full, full)),
            (coupling[0], product, stiffness, *faces, *slices, *state),
            flops=2 * coupling.size * loads,
        )
        residual, precon, *solution = (residual, product) if first else state
        sums_shape = shape(sectors * parts, SUM_ROWS, loads) if last else shape(SUM_ROWS, loads)
        image, top, sums, _ = call(
            functools.partial(image_kernel, sectors),
            (full, top_shape, sums_shape, shape(sectors, height, LANES)),
            (base, springs, factor, residual, *hubs),
        )
        state = (image, residual, precon, *solution)
        sums = (sums,)
    out = shape(1, rows, loads)
    return call(last_kernel, (out, out), (exchange(*sums, ("sector", "dof")), *state))


def plain_body(rhs, diagonal, coupling, springs, precond, hub_inverse):
    residual = rhs[0]
    spring_rows = springs[0][:, None]
    rows, loads = residual.shape
    quarter = rows // 4
    sectors = lax.axis_size("sector")
    onward, backward = around(sectors)
    solution = jnp.zeros_like(residual)

    def whole(field):
        return gathered(field.astype(bf16)).reshape(-1, loads)

    def copies(cells, axes):
        count = lax.axis_size(axes)
        return exchange(jnp.broadcast_to(cells[None], (count,) + cells.shape), axes)

    precon = jnp.dot(precond, whole(residual), preferred_element_type=f32)
    for step in range(ITERS):
        faces = precon[: 2 * quarter].astype(bf16)
        before = lax.ppermute(faces[quarter:], "sector", onward)
        after = lax.ppermute(faces[:quarter], "sector", backward)
        couple = jnp.dot(
            coupling[0], whole(jnp.concatenate([before, after])), preferred_element_type=f32
        )
        attached = precon[: 3 * quarter]
        load = (spring_rows * attached).T.reshape(sectors, loads // sectors, -1)
        load = jnp.sum(exchange(load, "sector"), axis=0).astype(bf16)
        load = copies(load, "dof").transpose(0, 2, 1).reshape(hub_inverse.shape[1], -1)
        hub = jnp.dot(hub_inverse, load, preferred_element_type=f32)
        hub = copies(hub.T, "sector").reshape(loads, -1).T
        pull = jnp.pad(spring_rows * (attached - hub), ((0, quarter), (0, 0)))
        image = diagonal[0][:, None] * precon + couple + pull
        sums = jnp.stack([jnp.sum(image * residual, axis=0), jnp.sum(image * image, axis=0)])
        alpha = alpha_of(copies(sums, ("sector", "dof")))
        solution = solution + alpha * precon
        residual = residual - alpha * image
        if step < ITERS - 1:
            change = jnp.dot(precond, whole(image), preferred_element_type=f32)
            precon = precon - alpha * change
    return (solution[None], residual[None])


def body(rhs, *rest):
    rows, loads = rhs.shape[1:]
    cases = loads // lax.axis_size("sector")
    tiled = loads == LANES and (rows // 4) % LANES == 0 and cases % 16 == 0
    return (tiled_body if tiled else plain_body)(rhs, *rest)


def solution(mesh):
    placed = (
        P("sector", "dof", None),
        P("sector", "dof"),
        P("sector", "dof", None),
        P("sector", "dof"),
        P("dof", None),
        P("dof", None),
    )
    return jax.shard_map(
        body,
        mesh=mesh,
        in_specs=placed,
        out_specs=(P("sector", "dof", None), P("sector", "dof", None)),
        check_vma=False,
    )
```

```python
import functools

import jax
import jax.numpy as jnp
from jax import lax
from jax.experimental import pallas as pl
from jax.experimental.pallas import tpu as pltpu
from jax.sharding import PartitionSpec as P

ITERS = 3
LANES = 128
MIB = 1024 * 1024
SUM_ROWS = 8
TERM_ROWS = 16
f32 = jnp.float32
bf16 = jnp.bfloat16


def shape(*dims, dtype=f32):
    return jax.ShapeDtypeStruct(dims, dtype)


def call(kernel, outs, operands, flops=0):
    whole = pl.BlockSpec(memory_space=pltpu.VMEM)
    return pl.pallas_call(
        kernel,
        in_specs=[whole] * len(operands),
        out_specs=jax.tree.map(lambda _: whole, outs),
        out_shape=outs,
        compiler_params=pltpu.CompilerParams(vmem_limit_bytes=12 * MIB),
        cost_estimate=pl.CostEstimate(
            flops=flops, bytes_accessed=sum(x.size * x.dtype.itemsize for x in operands), transcendentals=0
        ),
    )(*operands)


def in_terms(sums):
    terms = None
    for at in range(3):
        term = sums.astype(bf16).astype(f32)
        sums = sums - term
        terms = term if at == 0 else terms + pltpu.roll(term, 2 * at, 0)
    return jnp.concatenate([terms, jnp.zeros_like(terms)], axis=0)


def from_terms(terms):
    terms = terms[:SUM_ROWS].astype(f32)
    sums = terms + pltpu.roll(terms, SUM_ROWS - 2, 0) + pltpu.roll(terms, SUM_ROWS - 4, 0)
    return jnp.where(lax.broadcasted_iota(jnp.int32, sums.shape, 0) < 2, sums, 0.0)


def product_kernel(parts, matrix_ref, springs_ref, tops_ref, *refs):
    *refs, out_ref, load_ref, right_ref, left_ref = refs
    here = lax.axis_index("dof")
    _, top, _ = tops_ref.shape
    for part in range(parts):
        end_ref = refs[part]
        end = end_ref.shape[0]
        start = part * (top + end)
        owner = lax.rem(here + part, parts)
        product = jnp.dot(
            matrix_ref[:, start : start + top], tops_ref[part], preferred_element_type=f32
        ) + jnp.dot(
            matrix_ref[:, pl.ds(pl.multiple_of(owner * (top + end) + top, LANES), end)],
            end_ref[...],
            preferred_element_type=f32,
        )
        if part:
            out_ref[...] += product
        else:
            out_ref[...] = product

    sectors, height, _ = load_ref.shape
    cases = out_ref.shape[1] // sectors
    quarter = right_ref.shape[0]
    left_ref[...] = out_ref[:quarter].astype(bf16)
    right_ref[...] = out_ref[quarter : 2 * quarter].astype(bf16)
    for at in range((height - TERM_ROWS) // cases):
        rows = slice(at * LANES, (at + 1) * LANES)
        turned = (out_ref[rows].T * springs_ref[:, rows]).astype(load_ref.dtype)
        for s in range(sectors):
            load_ref[s, at * cases : (at + 1) * cases] = turned[s * cases : (s + 1) * cases]
    terms = in_terms(refs[parts][...]) if refs[parts:] else jnp.zeros((TERM_ROWS, LANES), f32)
    for s in range(sectors):
        load_ref[s, height - TERM_ROWS :] = terms.astype(load_ref.dtype)


def join_kernel(before_ref, after_ref, _, out_ref):
    quarter = before_ref.shape[0]
    out_ref[:quarter] = before_ref[...]
    out_ref[quarter:] = after_ref[...]


def slice_kernel(*refs):
    *part_refs, out_ref = refs
    height = out_ref.shape[0] - TERM_ROWS
    total = sum(ref[...].astype(f32) for ref in part_refs)
    out_ref[:height] = total[:height].astype(bf16)
    out_ref[height:] = in_terms(from_terms(total[height:])).astype(bf16)


def alpha_from(sums):
    return sums[0:1] / (sums[1:2] + 1e-06)


def block_columns(matrix_ref, parts, ahead):
    width = matrix_ref.shape[1] // parts
    owner = lax.rem(lax.axis_index("dof") + ahead, parts)
    return matrix_ref[:, pl.ds(pl.multiple_of(owner * width, LANES), width)]


def hub_kernel(cases, matrix_ref, *refs):
    *load_refs, out_ref = refs
    parts = len(load_refs)
    chunks = out_ref.shape[0] // cases
    total = None
    for part, ref in enumerate(load_refs):
        load = jnp.concatenate([ref[c * cases : (c + 1) * cases] for c in range(chunks)], axis=1)
        product = lax.dot_general(
            load,
            block_columns(matrix_ref, parts, part),
            (((1,), (1,)), ((), ())),
            preferred_element_type=f32,
        )
        total = product if total is None else total + product
    for c in range(chunks):
        out_ref[c * cases : (c + 1) * cases] = total[:, c * LANES : (c + 1) * LANES].astype(out_ref.dtype)


def base_kernel(first, parts, matrix_ref, product_ref, stiffness_ref, *refs):
    face_refs, load_refs, refs = refs[:parts], refs[parts : 2 * parts], refs[2 * parts :]
    if first:
        base_ref, end_ref, factor_ref = refs
    else:
        *refs, base_ref, end_ref, factor_ref, left_ref, newer_ref, better_ref = refs
        image_ref, residual_ref, precon_ref = refs[:3]
    base_ref[...] = stiffness_ref[...] * product_ref[...]
    for part, ref in enumerate(face_refs):
        base_ref[...] += jnp.dot(
            block_columns(matrix_ref, parts, part), ref[...], preferred_element_type=f32
        )
    if first:
        factor_ref[...] = jnp.ones_like(factor_ref)
    else:
        alpha = alpha_from(sum(from_terms(ref[ref.shape[0] - TERM_ROWS :]) for ref in load_refs))
        factor_ref[...] = jnp.broadcast_to(-alpha, factor_ref.shape)
        base_ref[...] = image_ref[...] - alpha * base_ref[...]
        left_ref[...] = residual_ref[...] - alpha * image_ref[...]
        gain = alpha * precon_ref[...]
        better_ref[...] = refs[3][...] + gain if len(refs) > 3 else gain
        newer_ref[...] = precon_ref[...] - alpha * product_ref[...]
    end_ref[...] = base_ref[base_ref.shape[0] - end_ref.shape[0] :].astype(bf16)


def image_kernel(sectors, base_ref, springs_ref, factor_ref, residual_ref, *refs):
    *hub_refs, image_ref, top_ref, sums_ref, hubs_ref = refs
    here = lax.axis_index("sector")
    for ahead in range(sectors):
        hubs_ref[lax.rem(here + ahead, sectors)] = hub_refs[ahead][...].astype(f32)
    attached = top_ref.shape[0]
    chunks = attached // LANES
    cases = hubs_ref.shape[1] // chunks
    factor = factor_ref[0:1]
    for c in range(chunks):
        at = slice(c * LANES, (c + 1) * LANES)
        hub = jnp.concatenate([hubs_ref[s, c * cases : (c + 1) * cases] for s in range(sectors)], axis=0)
        image = base_ref[at] - factor * (hub * springs_ref[:, at]).T
        image_ref[at] = image
        top_ref[at] = image.astype(bf16)
    image_ref[attached:] = base_ref[attached:]
    image = image_ref[...]
    upper = jnp.sum(image * residual_ref[...], axis=0, keepdims=True)
    lower = jnp.sum(image * image, axis=0, keepdims=True)
    rest = jnp.zeros((SUM_ROWS - 2, image.shape[1]), f32)
    sums = jnp.concatenate([upper, lower, rest], axis=0)
    sums_ref[...] = jnp.broadcast_to(sums, sums_ref.shape)


def last_kernel(sums_ref, image_ref, residual_ref, precon_ref, solution_ref, newer_ref, left_ref):
    alpha = alpha_from(jnp.sum(sums_ref[...], axis=0))
    newer_ref[0] = solution_ref[...] + alpha * precon_ref[...]
    left_ref[0] = residual_ref[...] - alpha * image_ref[...]


def last_update(sums, *state):
    rows, loads = state[0].shape
    height = rows // 4
    block = pl.BlockSpec((height, loads), lambda k: (k, 0))
    out_block = pl.BlockSpec((1, height, loads), lambda k: (0, k, 0))
    out = shape(1, rows, loads)
    return pl.pallas_call(
        last_kernel,
        grid=(4,),
        in_specs=[pl.BlockSpec(sums.shape, lambda k: (0, 0, 0))] + [block] * len(state),
        out_specs=(out_block, out_block),
        out_shape=(out, out),
        compiler_params=pltpu.CompilerParams(vmem_limit_bytes=60 * MIB),
    )(sums, *state)


def round_kernel(field_ref, top_ref, end_ref):
    attached = top_ref.shape[0]
    top_ref[...] = field_ref[0, :attached].astype(bf16)
    end_ref[...] = field_ref[0, attached:].astype(bf16)


def exchange(blocks, axes):
    return lax.all_to_all(blocks, axes, split_axis=0, concat_axis=0)


def from_ahead(cells, axis, distance):
    count = lax.axis_size(axis)
    return lax.ppermute(cells, axis, [((i + distance) % count, i) for i in range(count)])


def one_from_each(cells, axis):
    return [cells] + [from_ahead(cells, axis, d) for d in range(1, lax.axis_size(axis))]


def mine_from_each(blocks, axis):
    count, here = lax.axis_size(axis), lax.axis_index(axis)
    own = [lax.dynamic_index_in_dim(blocks, (here - d) % count, 0, False) for d in range(count)]
    return own[:1] + [from_ahead(own[d], axis, d) for d in range(1, count)]


def gathered(field):
    return lax.all_gather(field, "dof", axis=0)


def around(sectors):
    onward = [(s, (s + 1) % sectors) for s in range(sectors)]
    return onward, [(b, a) for a, b in onward]


def alpha_of(sums):
    return alpha_from(jnp.sum(sums, axis=0))[0]


def tiled_body(rhs, diagonal, coupling, springs, precond, hub_inverse):
    residual = rhs[0]
    rows, loads = residual.shape
    attached = springs.shape[1]
    quarter = rows - attached
    sectors, parts = lax.axis_size("sector"), lax.axis_size("dof")
    cases = loads // sectors
    height = attached // LANES * cases
    onward, backward = around(sectors)
    full, face = shape(rows, loads), shape(quarter, loads, dtype=bf16)
    top_shape = shape(attached, loads, dtype=bf16)

    stiffness = diagonal[0] + jnp.pad(springs[0], (0, quarter))
    stiffness = jnp.broadcast_to(stiffness[:, None], (rows, loads))
    state = sums = ()

    top, end = call(round_kernel, (top_shape, face), (rhs,))
    for step in range(ITERS):
        first, last = step == 0, step == ITERS - 1
        sent = f32 if first else bf16
        product, load, right, left = call(
            functools.partial(product_kernel, parts),
            (full, shape(sectors, height + TERM_ROWS, LANES, dtype=sent), face, face),
            (precond, springs, gathered(top), *one_from_each(end, "dof"), *sums),
            flops=2 * precond.size * loads,
        )
        before = lax.ppermute(right, "sector", onward)
        after = lax.ppermute(left, "sector", backward)
        load = call(
            slice_kernel,
            shape(height + TERM_ROWS, loads, dtype=bf16),
            mine_from_each(load, "sector"),
        )
        slices = one_from_each(load, "dof")
        faces = call(join_kernel, shape(2 * quarter, loads, dtype=bf16), (before, after, slices[-1]))
        faces = one_from_each(faces, "dof")
        hub = call(
            functools.partial(hub_kernel, cases),
            shape(height, LANES, dtype=sent),
            (hub_inverse, *slices),
            flops=2 * hub_inverse.size * cases,
        )
        hubs = one_from_each(hub, "sector")
        base, end, factor, *state = call(
            functools.partial(base_kernel, first, parts),
            (full, face, shape(SUM_ROWS, loads)) + (() if first else (full, full, full)),
            (coupling[0], product, stiffness, *faces, *slices, *state),
            flops=2 * coupling.size * loads,
        )
        residual, precon, *solution = (residual, product) if first else state
        sums_shape = shape(sectors * parts, SUM_ROWS, loads) if last else shape(SUM_ROWS, loads)
        image, top, sums, _ = call(
            functools.partial(image_kernel, sectors),
            (full, top_shape, sums_shape, shape(sectors, height, LANES)),
            (base, springs, factor, residual, *hubs),
        )
        state = (image, residual, precon, *solution)
        sums = (sums,)
    out = shape(1, rows, loads)
    return call(last_kernel, (out, out), (exchange(*sums, ("sector", "dof")), *state))


def plain_body(rhs, diagonal, coupling, springs, precond, hub_inverse):
    residual = rhs[0]
    spring_rows = springs[0][:, None]
    rows, loads = residual.shape
    quarter = rows // 4
    sectors = lax.axis_size("sector")
    onward, backward = around(sectors)
    solution = jnp.zeros_like(residual)

    def whole(field):
        return gathered(field.astype(bf16)).reshape(-1, loads)

    def copies(cells, axes):
        count = lax.axis_size(axes)
        return exchange(jnp.broadcast_to(cells[None], (count,) + cells.shape), axes)

    precon = jnp.dot(precond, whole(residual), preferred_element_type=f32)
    for step in range(ITERS):
        faces = precon[: 2 * quarter].astype(bf16)
        before = lax.ppermute(faces[quarter:], "sector", onward)
        after = lax.ppermute(faces[:quarter], "sector", backward)
        couple = jnp.dot(
            coupling[0], whole(jnp.concatenate([before, after])), preferred_element_type=f32
        )
        attached = precon[: 3 * quarter]
        load = (spring_rows * attached).T.reshape(sectors, loads // sectors, -1)
        load = jnp.sum(exchange(load, "sector"), axis=0).astype(bf16)
        load = copies(load, "dof").transpose(0, 2, 1).reshape(hub_inverse.shape[1], -1)
        hub = jnp.dot(hub_inverse, load, preferred_element_type=f32)
        hub = copies(hub.T, "sector").reshape(loads, -1).T
        pull = jnp.pad(spring_rows * (attached - hub), ((0, quarter), (0, 0)))
        image = diagonal[0][:, None] * precon + couple + pull
        sums = jnp.stack([jnp.sum(image * residual, axis=0), jnp.sum(image * image, axis=0)])
        alpha = alpha_of(copies(sums, ("sector", "dof")))
        solution = solution + alpha * precon
        residual = residual - alpha * image
        if step < ITERS - 1:
            change = jnp.dot(precond, whole(image), preferred_element_type=f32)
            precon = precon - alpha * change
    return (solution[None], residual[None])


def body(rhs, *rest):
    rows, loads = rhs.shape[1:]
    cases = loads // lax.axis_size("sector")
    tiled = loads == LANES and (rows // 4) % LANES == 0 and cases % 16 == 0
    return (tiled_body if tiled else plain_body)(rhs, *rest)


def solution(mesh):
    placed = (
        P("sector", "dof", None),
        P("sector", "dof"),
        P("sector", "dof", None),
        P("sector", "dof"),
        P("dof", None),
        P("dof", None),
    )
    return jax.shard_map(
        body,
        mesh=mesh,
        in_specs=placed,
        out_specs=(P("sector", "dof", None), P("sector", "dof", None)),
        check_vma=False,
    )
```

```python
import functools

import jax
import jax.numpy as jnp
from jax import lax
from jax.experimental import pallas as pl
from jax.experimental.pallas import tpu as pltpu
from jax.sharding import PartitionSpec as P

ITERS = 3
LANES = 128
MIB = 1024 * 1024
SUM_ROWS = 8
TERM_ROWS = 16
f32 = jnp.float32
bf16 = jnp.bfloat16


def shape(*dims, dtype=f32):
    return jax.ShapeDtypeStruct(dims, dtype)


def call(kernel, outs, operands, flops=0):
    whole = pl.BlockSpec(memory_space=pltpu.VMEM)
    return pl.pallas_call(
        kernel,
        in_specs=[whole] * len(operands),
        out_specs=jax.tree.map(lambda _: whole, outs),
        out_shape=outs,
        compiler_params=pltpu.CompilerParams(vmem_limit_bytes=20 * MIB),
        cost_estimate=pl.CostEstimate(
            flops=flops, bytes_accessed=sum(x.size * x.dtype.itemsize for x in operands), transcendentals=0
        ),
    )(*operands)


def in_terms(sums):
    terms = None
    for at in range(3):
        term = sums.astype(bf16).astype(f32)
        sums = sums - term
        terms = term if at == 0 else terms + pltpu.roll(term, 2 * at, 0)
    return jnp.concatenate([terms, jnp.zeros_like(terms)], axis=0)


def from_terms(terms):
    terms = terms[:SUM_ROWS].astype(f32)
    sums = terms + pltpu.roll(terms, SUM_ROWS - 2, 0) + pltpu.roll(terms, SUM_ROWS - 4, 0)
    return jnp.where(lax.broadcasted_iota(jnp.int32, sums.shape, 0) < 2, sums, 0.0)


def product_kernel(parts, matrix_ref, springs_ref, tops_ref, *refs):
    *refs, out_ref, load_ref, right_ref, left_ref = refs
    here = lax.axis_index("dof")
    _, top, _ = tops_ref.shape
    for part in range(parts):
        end_ref = refs[part]
        end = end_ref.shape[0]
        start = part * (top + end)
        owner = lax.rem(here + part, parts)
        product = jnp.dot(
            matrix_ref[:, start : start + top], tops_ref[part], preferred_element_type=f32
        ) + jnp.dot(
            matrix_ref[:, pl.ds(pl.multiple_of(owner * (top + end) + top, LANES), end)],
            end_ref[...],
            preferred_element_type=f32,
        )
        if part:
            out_ref[...] += product
        else:
            out_ref[...] = product

    sectors, height, _ = load_ref.shape
    cases = out_ref.shape[1] // sectors
    quarter = right_ref.shape[0]
    left_ref[...] = out_ref[:quarter].astype(bf16)
    right_ref[...] = out_ref[quarter : 2 * quarter].astype(bf16)
    for at in range((height - TERM_ROWS) // cases):
        rows = slice(at * LANES, (at + 1) * LANES)
        turned = (out_ref[rows].T * springs_ref[:, rows]).astype(load_ref.dtype)
        for s in range(sectors):
            load_ref[s, at * cases : (at + 1) * cases] = turned[s * cases : (s + 1) * cases]
    terms = in_terms(refs[parts][...]) if refs[parts:] else jnp.zeros((TERM_ROWS, LANES), f32)
    for s in range(sectors):
        load_ref[s, height - TERM_ROWS :] = terms.astype(load_ref.dtype)


def join_kernel(before_ref, after_ref, *refs):
    out_ref = refs[-1]
    quarter = before_ref.shape[0]
    out_ref[:quarter] = before_ref[...]
    out_ref[quarter:] = after_ref[...]


def slice_kernel(*refs):
    *part_refs, out_ref = refs
    height = out_ref.shape[0] - TERM_ROWS
    total = sum(ref[...].astype(f32) for ref in part_refs)
    out_ref[:height] = total[:height].astype(bf16)
    out_ref[height:] = in_terms(from_terms(total[height:])).astype(bf16)


def alpha_from(sums):
    return sums[0:1] / (sums[1:2] + 1e-06)


def block_columns(matrix_ref, parts, ahead):
    width = matrix_ref.shape[1] // parts
    owner = lax.rem(lax.axis_index("dof") + ahead, parts)
    return matrix_ref[:, pl.ds(pl.multiple_of(owner * width, LANES), width)]


def hub_kernel(cases, matrix_ref, *refs):
    *load_refs, out_ref = refs
    parts = len(load_refs)
    chunks = out_ref.shape[0] // cases
    total = None
    for part, ref in enumerate(load_refs):
        load = jnp.concatenate([ref[c * cases : (c + 1) * cases] for c in range(chunks)], axis=1)
        product = lax.dot_general(
            load,
            block_columns(matrix_ref, parts, part),
            (((1,), (1,)), ((), ())),
            preferred_element_type=f32,
        )
        total = product if total is None else total + product
    for c in range(chunks):
        out_ref[c * cases : (c + 1) * cases] = total[:, c * LANES : (c + 1) * LANES].astype(out_ref.dtype)


def base_kernel(first, parts, matrix_ref, product_ref, stiffness_ref, *refs):
    face_refs, load_refs, refs = refs[:parts], refs[parts : 2 * parts], refs[2 * parts :]
    if first:
        base_ref, end_ref, factor_ref = refs
    else:
        *refs, base_ref, end_ref, factor_ref, left_ref, newer_ref, better_ref = refs
        image_ref, residual_ref, precon_ref = refs[:3]
    base_ref[...] = stiffness_ref[...] * product_ref[...]
    for part, ref in enumerate(face_refs):
        base_ref[...] += jnp.dot(
            block_columns(matrix_ref, parts, part), ref[...], preferred_element_type=f32
        )
    if first:
        factor_ref[...] = jnp.ones_like(factor_ref)
    else:
        alpha = alpha_from(sum(from_terms(ref[ref.shape[0] - TERM_ROWS :]) for ref in load_refs))
        factor_ref[...] = jnp.broadcast_to(-alpha, factor_ref.shape)
        base_ref[...] = image_ref[...] - alpha * base_ref[...]
        left_ref[...] = residual_ref[...] - alpha * image_ref[...]
        gain = alpha * precon_ref[...]
        better_ref[...] = refs[3][...] + gain if len(refs) > 3 else gain
        newer_ref[...] = precon_ref[...] - alpha * product_ref[...]
    end_ref[...] = base_ref[base_ref.shape[0] - end_ref.shape[0] :].astype(bf16)


def image_kernel(sectors, base_ref, springs_ref, factor_ref, residual_ref, *refs):
    *hub_refs, image_ref, top_ref, sums_ref, hubs_ref = refs
    here = lax.axis_index("sector")
    for ahead in range(sectors):
        hubs_ref[lax.rem(here + ahead, sectors)] = hub_refs[ahead][...].astype(f32)
    attached = top_ref.shape[0]
    chunks = attached // LANES
    cases = hubs_ref.shape[1] // chunks
    factor = factor_ref[0:1]
    for c in range(chunks):
        at = slice(c * LANES, (c + 1) * LANES)
        hub = jnp.concatenate([hubs_ref[s, c * cases : (c + 1) * cases] for s in range(sectors)], axis=0)
        image = base_ref[at] - factor * (hub * springs_ref[:, at]).T
        image_ref[at] = image
        top_ref[at] = image.astype(bf16)
    image_ref[attached:] = base_ref[attached:]
    image = image_ref[...]
    upper = jnp.sum(image * residual_ref[...], axis=0, keepdims=True)
    lower = jnp.sum(image * image, axis=0, keepdims=True)
    rest = jnp.zeros((SUM_ROWS - 2, image.shape[1]), f32)
    sums = jnp.concatenate([upper, lower, rest], axis=0)
    sums_ref[...] = jnp.broadcast_to(sums, sums_ref.shape)


def last_kernel(sums_ref, image_ref, residual_ref, precon_ref, solution_ref, newer_ref, left_ref):
    alpha = alpha_from(jnp.sum(sums_ref[...], axis=0))
    newer_ref[0] = solution_ref[...] + alpha * precon_ref[...]
    left_ref[0] = residual_ref[...] - alpha * image_ref[...]


def last_update(sums, *state):
    rows, loads = state[0].shape
    height = rows // 4
    block = pl.BlockSpec((height, loads), lambda k: (k, 0))
    out_block = pl.BlockSpec((1, height, loads), lambda k: (0, k, 0))
    out = shape(1, rows, loads)
    return pl.pallas_call(
        last_kernel,
        grid=(4,),
        in_specs=[pl.BlockSpec(sums.shape, lambda k: (0, 0, 0))] + [block] * len(state),
        out_specs=(out_block, out_block),
        out_shape=(out, out),
        compiler_params=pltpu.CompilerParams(vmem_limit_bytes=60 * MIB),
    )(sums, *state)


def round_kernel(field_ref, top_ref, end_ref):
    attached = top_ref.shape[0]
    top_ref[...] = field_ref[0, :attached].astype(bf16)
    end_ref[...] = field_ref[0, attached:].astype(bf16)


def exchange(blocks, axes):
    return lax.all_to_all(blocks, axes, split_axis=0, concat_axis=0)


def from_ahead(cells, axis, distance):
    count = lax.axis_size(axis)
    return lax.ppermute(cells, axis, [((i + distance) % count, i) for i in range(count)])


def one_from_each(cells, axis):
    return [cells] + [from_ahead(cells, axis, d) for d in range(1, lax.axis_size(axis))]


def mine_from_each(blocks, axis):
    count, here = lax.axis_size(axis), lax.axis_index(axis)
    own = [lax.dynamic_index_in_dim(blocks, (here - d) % count, 0, False) for d in range(count)]
    return own[:1] + [from_ahead(own[d], axis, d) for d in range(1, count)]


def gathered(field):
    return lax.all_gather(field, "dof", axis=0)


def around(sectors):
    onward = [(s, (s + 1) % sectors) for s in range(sectors)]
    return onward, [(b, a) for a, b in onward]


def alpha_of(sums):
    return alpha_from(jnp.sum(sums, axis=0))[0]


def tiled_body(rhs, diagonal, coupling, springs, precond, hub_inverse):
    residual = rhs[0]
    rows, loads = residual.shape
    attached = springs.shape[1]
    quarter = rows - attached
    sectors, parts = lax.axis_size("sector"), lax.axis_size("dof")
    cases = loads // sectors
    height = attached // LANES * cases
    onward, backward = around(sectors)
    full, face = shape(rows, loads), shape(quarter, loads, dtype=bf16)
    top_shape = shape(attached, loads, dtype=bf16)

    stiffness = diagonal[0] + jnp.pad(springs[0], (0, quarter))
    stiffness = jnp.broadcast_to(stiffness[:, None], (rows, loads))
    state = sums = ()

    top, end = call(round_kernel, (top_shape, face), (rhs,))
    for step in range(ITERS):
        first, last = step == 0, step == ITERS - 1
        sent = f32 if first else bf16
        product, load, right, left = call(
            functools.partial(product_kernel, parts),
            (full, shape(sectors, height + TERM_ROWS, LANES, dtype=sent), face, face),
            (precond, springs, gathered(top), *one_from_each(end, "dof"), *sums),
            flops=2 * precond.size * loads,
        )
        before = lax.ppermute(right, "sector", onward)
        after = lax.ppermute(left, "sector", backward)
        load = call(
            slice_kernel,
            shape(height + TERM_ROWS, loads, dtype=bf16),
            mine_from_each(load, "sector"),
        )
        slices = one_from_each(load, "dof")
        faces = call(join_kernel, shape(2 * quarter, loads, dtype=bf16), (before, after, *slices[1:]))
        faces = one_from_each(faces, "dof")
        hub = call(
            functools.partial(hub_kernel, cases),
            shape(height, LANES, dtype=sent),
            (hub_inverse, *slices),
            flops=2 * hub_inverse.size * cases,
        )
        hubs = one_from_each(hub, "sector")
        base, end, factor, *state = call(
            functools.partial(base_kernel, first, parts),
            (full, face, shape(SUM_ROWS, loads)) + (() if first else (full, full, full)),
            (coupling[0], product, stiffness, *faces, *slices, *state),
            flops=2 * coupling.size * loads,
        )
        residual, precon, *solution = (residual, product) if first else state
        sums_shape = shape(sectors * parts, SUM_ROWS, loads) if last else shape(SUM_ROWS, loads)
        image, top, sums, _ = call(
            functools.partial(image_kernel, sectors),
            (full, top_shape, sums_shape, shape(sectors, height, LANES)),
            (base, springs, factor, residual, *hubs),
        )
        state = (image, residual, precon, *solution)
        sums = (sums,)
    out = shape(1, rows, loads)
    return call(last_kernel, (out, out), (exchange(*sums, ("sector", "dof")), *state))


def plain_body(rhs, diagonal, coupling, springs, precond, hub_inverse):
    residual = rhs[0]
    spring_rows = springs[0][:, None]
    rows, loads = residual.shape
    quarter = rows // 4
    sectors = lax.axis_size("sector")
    onward, backward = around(sectors)
    solution = jnp.zeros_like(residual)

    def whole(field):
        return gathered(field.astype(bf16)).reshape(-1, loads)

    def copies(cells, axes):
        count = lax.axis_size(axes)
        return exchange(jnp.broadcast_to(cells[None], (count,) + cells.shape), axes)

    precon = jnp.dot(precond, whole(residual), preferred_element_type=f32)
    for step in range(ITERS):
        faces = precon[: 2 * quarter].astype(bf16)
        before = lax.ppermute(faces[quarter:], "sector", onward)
        after = lax.ppermute(faces[:quarter], "sector", backward)
        couple = jnp.dot(
            coupling[0], whole(jnp.concatenate([before, after])), preferred_element_type=f32
        )
        attached = precon[: 3 * quarter]
        load = (spring_rows * attached).T.reshape(sectors, loads // sectors, -1)
        load = jnp.sum(exchange(load, "sector"), axis=0).astype(bf16)
        load = copies(load, "dof").transpose(0, 2, 1).reshape(hub_inverse.shape[1], -1)
        hub = jnp.dot(hub_inverse, load, preferred_element_type=f32)
        hub = copies(hub.T, "sector").reshape(loads, -1).T
        pull = jnp.pad(spring_rows * (attached - hub), ((0, quarter), (0, 0)))
        image = diagonal[0][:, None] * precon + couple + pull
        sums = jnp.stack([jnp.sum(image * residual, axis=0), jnp.sum(image * image, axis=0)])
        alpha = alpha_of(copies(sums, ("sector", "dof")))
        solution = solution + alpha * precon
        residual = residual - alpha * image
        if step < ITERS - 1:
            change = jnp.dot(precond, whole(image), preferred_element_type=f32)
            precon = precon - alpha * change
    return (solution[None], residual[None])


def body(rhs, *rest):
    rows, loads = rhs.shape[1:]
    cases = loads // lax.axis_size("sector")
    tiled = loads == LANES and (rows // 4) % LANES == 0 and cases % 16 == 0
    return (tiled_body if tiled else plain_body)(rhs, *rest)


def solution(mesh):
    placed = (
        P("sector", "dof", None),
        P("sector", "dof"),
        P("sector", "dof", None),
        P("sector", "dof"),
        P("dof", None),
        P("dof", None),
    )
    return jax.shard_map(
        body,
        mesh=mesh,
        in_specs=placed,
        out_specs=(P("sector", "dof", None), P("sector", "dof", None)),
        check_vma=False,
    )
```

```python
import functools

import jax
import jax.numpy as jnp
from jax import lax
from jax.experimental import pallas as pl
from jax.experimental.pallas import tpu as pltpu
from jax.sharding import PartitionSpec as P

ITERS = 3
LANES = 128
MIB = 1024 * 1024
SUM_ROWS = 8
TERM_ROWS = 16
f32 = jnp.float32
bf16 = jnp.bfloat16


def shape(*dims, dtype=f32):
    return jax.ShapeDtypeStruct(dims, dtype)


def call(kernel, outs, operands, flops=0):
    whole = pl.BlockSpec(memory_space=pltpu.VMEM)
    return pl.pallas_call(
        kernel,
        in_specs=[whole] * len(operands),
        out_specs=jax.tree.map(lambda _: whole, outs),
        out_shape=outs,
        compiler_params=pltpu.CompilerParams(vmem_limit_bytes=20 * MIB),
        cost_estimate=pl.CostEstimate(
            flops=flops, bytes_accessed=sum(x.size * x.dtype.itemsize for x in operands), transcendentals=0
        ),
    )(*operands)


def in_terms(sums):
    terms = None
    for at in range(3):
        term = sums.astype(bf16).astype(f32)
        sums = sums - term
        terms = term if at == 0 else terms + pltpu.roll(term, 2 * at, 0)
    return jnp.concatenate([terms, jnp.zeros_like(terms)], axis=0)


def from_terms(terms):
    terms = terms[:SUM_ROWS].astype(f32)
    sums = terms + pltpu.roll(terms, SUM_ROWS - 2, 0) + pltpu.roll(terms, SUM_ROWS - 4, 0)
    return jnp.where(lax.broadcasted_iota(jnp.int32, sums.shape, 0) < 2, sums, 0.0)


def product_kernel(parts, matrix_ref, springs_ref, tops_ref, *refs):
    *refs, out_ref, load_ref, right_ref, left_ref = refs
    here = lax.axis_index("dof")
    _, top, _ = tops_ref.shape
    for part in range(parts):
        end_ref = refs[part]
        end = end_ref.shape[0]
        start = part * (top + end)
        owner = lax.rem(here + part, parts)
        product = jnp.dot(
            matrix_ref[:, start : start + top], tops_ref[part], preferred_element_type=f32
        ) + jnp.dot(
            matrix_ref[:, pl.ds(pl.multiple_of(owner * (top + end) + top, LANES), end)],
            end_ref[...],
            preferred_element_type=f32,
        )
        if part:
            out_ref[...] += product
        else:
            out_ref[...] = product

    sectors, height, _ = load_ref.shape
    cases = out_ref.shape[1] // sectors
    quarter = right_ref.shape[0]
    left_ref[...] = out_ref[:quarter].astype(bf16)
    right_ref[...] = out_ref[quarter : 2 * quarter].astype(bf16)
    for at in range((height - TERM_ROWS) // cases):
        rows = slice(at * LANES, (at + 1) * LANES)
        turned = (out_ref[rows].T * springs_ref[:, rows]).astype(load_ref.dtype)
        for s in range(sectors):
            load_ref[s, at * cases : (at + 1) * cases] = turned[s * cases : (s + 1) * cases]
    terms = in_terms(refs[parts][...]) if refs[parts:] else jnp.zeros((TERM_ROWS, LANES), f32)
    for s in range(sectors):
        load_ref[s, height - TERM_ROWS :] = terms.astype(load_ref.dtype)


def join_kernel(before_ref, after_ref, *refs):
    out_ref = refs[-1]
    quarter = before_ref.shape[0]
    out_ref[:quarter] = before_ref[...]
    out_ref[quarter:] = after_ref[...]


def slice_kernel(*refs):
    *part_refs, out_ref = refs
    height = out_ref.shape[0] - TERM_ROWS
    total = sum(ref[...].astype(f32) for ref in part_refs)
    out_ref[:height] = total[:height].astype(bf16)
    out_ref[height:] = in_terms(from_terms(total[height:])).astype(bf16)


def alpha_from(sums):
    return sums[0:1] / (sums[1:2] + 1e-06)


def block_columns(matrix_ref, parts, ahead):
    width = matrix_ref.shape[1] // parts
    owner = lax.rem(lax.axis_index("dof") + ahead, parts)
    return matrix_ref[:, pl.ds(pl.multiple_of(owner * width, LANES), width)]


def hub_kernel(cases, matrix_ref, *refs):
    *load_refs, out_ref = refs
    parts = len(load_refs)
    chunks = out_ref.shape[0] // cases
    total = None
    for part, ref in enumerate(load_refs):
        load = jnp.concatenate([ref[c * cases : (c + 1) * cases] for c in range(chunks)], axis=1)
        product = lax.dot_general(
            load,
            block_columns(matrix_ref, parts, part),
            (((1,), (1,)), ((), ())),
            preferred_element_type=f32,
        )
        total = product if total is None else total + product
    for c in range(chunks):
        out_ref[c * cases : (c + 1) * cases] = total[:, c * LANES : (c + 1) * LANES].astype(out_ref.dtype)


def base_kernel(first, parts, matrix_ref, product_ref, stiffness_ref, *refs):
    face_refs, load_refs, refs = refs[:parts], refs[parts : 2 * parts], refs[2 * parts :]
    if first:
        base_ref, end_ref, factor_ref = refs
    else:
        *refs, base_ref, end_ref, factor_ref, left_ref, newer_ref, better_ref = refs
        image_ref, residual_ref, precon_ref = refs[:3]
    base_ref[...] = stiffness_ref[...] * product_ref[...]
    for part, ref in enumerate(face_refs):
        base_ref[...] += jnp.dot(
            block_columns(matrix_ref, parts, part), ref[...], preferred_element_type=f32
        )
    if first:
        factor_ref[...] = jnp.ones_like(factor_ref)
    else:
        alpha = alpha_from(sum(from_terms(ref[ref.shape[0] - TERM_ROWS :]) for ref in load_refs))
        factor_ref[...] = jnp.broadcast_to(-alpha, factor_ref.shape)
        base_ref[...] = image_ref[...] - alpha * base_ref[...]
        left_ref[...] = residual_ref[...] - alpha * image_ref[...]
        gain = alpha * precon_ref[...]
        better_ref[...] = refs[3][...] + gain if len(refs) > 3 else gain
        newer_ref[...] = precon_ref[...] - alpha * product_ref[...]
    end_ref[...] = base_ref[base_ref.shape[0] - end_ref.shape[0] :].astype(bf16)


def image_kernel(sectors, base_ref, springs_ref, factor_ref, residual_ref, *refs):
    *hub_refs, image_ref, top_ref, sums_ref, hubs_ref = refs
    here = lax.axis_index("sector")
    for ahead in range(sectors):
        hubs_ref[lax.rem(here + ahead, sectors)] = hub_refs[ahead][...].astype(f32)
    attached = top_ref.shape[0]
    chunks = attached // LANES
    cases = hubs_ref.shape[1] // chunks
    factor = factor_ref[0:1]
    for c in range(chunks):
        at = slice(c * LANES, (c + 1) * LANES)
        hub = jnp.concatenate([hubs_ref[s, c * cases : (c + 1) * cases] for s in range(sectors)], axis=0)
        image = base_ref[at] - factor * (hub * springs_ref[:, at]).T
        image_ref[at] = image
        top_ref[at] = image.astype(bf16)
    image_ref[attached:] = base_ref[attached:]
    image = image_ref[...]
    upper = jnp.sum(image * residual_ref[...], axis=0, keepdims=True)
    lower = jnp.sum(image * image, axis=0, keepdims=True)
    rest = jnp.zeros((SUM_ROWS - 2, image.shape[1]), f32)
    sums = jnp.concatenate([upper, lower, rest], axis=0)
    sums_ref[...] = jnp.broadcast_to(sums, sums_ref.shape)


def last_kernel(sums_ref, image_ref, residual_ref, precon_ref, solution_ref, newer_ref, left_ref):
    alpha = alpha_from(jnp.sum(sums_ref[...], axis=0))
    newer_ref[0] = solution_ref[...] + alpha * precon_ref[...]
    left_ref[0] = residual_ref[...] - alpha * image_ref[...]


def last_update(sums, *state):
    rows, loads = state[0].shape
    height = rows // 4
    block = pl.BlockSpec((height, loads), lambda k: (k, 0))
    out_block = pl.BlockSpec((1, height, loads), lambda k: (0, k, 0))
    out = shape(1, rows, loads)
    return pl.pallas_call(
        last_kernel,
        grid=(4,),
        in_specs=[pl.BlockSpec(sums.shape, lambda k: (0, 0, 0))] + [block] * len(state),
        out_specs=(out_block, out_block),
        out_shape=(out, out),
        compiler_params=pltpu.CompilerParams(vmem_limit_bytes=60 * MIB),
    )(sums, *state)


def round_kernel(field_ref, diagonal_ref, springs_ref, top_ref, end_ref, stiffness_ref):
    attached = top_ref.shape[0]
    top_ref[...] = field_ref[0, :attached].astype(bf16)
    end_ref[...] = field_ref[0, attached:].astype(bf16)
    for start in range(0, stiffness_ref.shape[0], LANES):
        rows = slice(start, start + LANES)
        row = diagonal_ref[:, rows]
        if start < attached:
            row = row + springs_ref[:, rows]
        stiffness_ref[rows] = jnp.broadcast_to(row, (LANES, LANES)).T


def exchange(blocks, axes):
    return lax.all_to_all(blocks, axes, split_axis=0, concat_axis=0)


def from_ahead(cells, axis, distance):
    count = lax.axis_size(axis)
    return lax.ppermute(cells, axis, [((i + distance) % count, i) for i in range(count)])


def one_from_each(cells, axis):
    return [cells] + [from_ahead(cells, axis, d) for d in range(1, lax.axis_size(axis))]


def mine_from_each(blocks, axis):
    count, here = lax.axis_size(axis), lax.axis_index(axis)
    own = [lax.dynamic_index_in_dim(blocks, (here - d) % count, 0, False) for d in range(count)]
    return own[:1] + [from_ahead(own[d], axis, d) for d in range(1, count)]


def gathered(field):
    return lax.all_gather(field, "dof", axis=0)


def around(sectors):
    onward = [(s, (s + 1) % sectors) for s in range(sectors)]
    return onward, [(b, a) for a, b in onward]


def alpha_of(sums):
    return alpha_from(jnp.sum(sums, axis=0))[0]


def tiled_body(rhs, diagonal, coupling, springs, precond, hub_inverse):
    residual = rhs[0]
    rows, loads = residual.shape
    attached = springs.shape[1]
    quarter = rows - attached
    sectors, parts = lax.axis_size("sector"), lax.axis_size("dof")
    cases = loads // sectors
    height = attached // LANES * cases
    onward, backward = around(sectors)
    full, face = shape(rows, loads), shape(quarter, loads, dtype=bf16)
    top_shape = shape(attached, loads, dtype=bf16)

    state = sums = ()

    top, end, stiffness = call(round_kernel, (top_shape, face, full), (rhs, diagonal, springs))
    for step in range(ITERS):
        first, last = step == 0, step == ITERS - 1
        sent = f32 if first else bf16
        product, load, right, left = call(
            functools.partial(product_kernel, parts),
            (full, shape(sectors, height + TERM_ROWS, LANES, dtype=sent), face, face),
            (precond, springs, gathered(top), *one_from_each(end, "dof"), *sums),
            flops=2 * precond.size * loads,
        )
        before = lax.ppermute(right, "sector", onward)
        after = lax.ppermute(left, "sector", backward)
        load = call(
            slice_kernel,
            shape(height + TERM_ROWS, loads, dtype=bf16),
            mine_from_each(load, "sector"),
        )
        slices = one_from_each(load, "dof")
        faces = call(join_kernel, shape(2 * quarter, loads, dtype=bf16), (before, after, *slices[1:]))
        faces = one_from_each(faces, "dof")
        hub = call(
            functools.partial(hub_kernel, cases),
            shape(height, LANES, dtype=sent),
            (hub_inverse, *slices),
            flops=2 * hub_inverse.size * cases,
        )
        hubs = one_from_each(hub, "sector")
        base, end, factor, *state = call(
            functools.partial(base_kernel, first, parts),
            (full, face, shape(SUM_ROWS, loads)) + (() if first else (full, full, full)),
            (coupling[0], product, stiffness, *faces, *slices, *state),
            flops=2 * coupling.size * loads,
        )
        residual, precon, *solution = (residual, product) if first else state
        sums_shape = shape(sectors * parts, SUM_ROWS, loads) if last else shape(SUM_ROWS, loads)
        image, top, sums, _ = call(
            functools.partial(image_kernel, sectors),
            (full, top_shape, sums_shape, shape(sectors, height, LANES)),
            (base, springs, factor, residual, *hubs),
        )
        state = (image, residual, precon, *solution)
        sums = (sums,)
    out = shape(1, rows, loads)
    return call(last_kernel, (out, out), (exchange(*sums, ("sector", "dof")), *state))


def plain_body(rhs, diagonal, coupling, springs, precond, hub_inverse):
    residual = rhs[0]
    spring_rows = springs[0][:, None]
    rows, loads = residual.shape
    quarter = rows // 4
    sectors = lax.axis_size("sector")
    onward, backward = around(sectors)
    solution = jnp.zeros_like(residual)

    def whole(field):
        return gathered(field.astype(bf16)).reshape(-1, loads)

    def copies(cells, axes):
        count = lax.axis_size(axes)
        return exchange(jnp.broadcast_to(cells[None], (count,) + cells.shape), axes)

    precon = jnp.dot(precond, whole(residual), preferred_element_type=f32)
    for step in range(ITERS):
        faces = precon[: 2 * quarter].astype(bf16)
        before = lax.ppermute(faces[quarter:], "sector", onward)
        after = lax.ppermute(faces[:quarter], "sector", backward)
        couple = jnp.dot(
            coupling[0], whole(jnp.concatenate([before, after])), preferred_element_type=f32
        )
        attached = precon[: 3 * quarter]
        load = (spring_rows * attached).T.reshape(sectors, loads // sectors, -1)
        load = jnp.sum(exchange(load, "sector"), axis=0).astype(bf16)
        load = copies(load, "dof").transpose(0, 2, 1).reshape(hub_inverse.shape[1], -1)
        hub = jnp.dot(hub_inverse, load, preferred_element_type=f32)
        hub = copies(hub.T, "sector").reshape(loads, -1).T
        pull = jnp.pad(spring_rows * (attached - hub), ((0, quarter), (0, 0)))
        image = diagonal[0][:, None] * precon + couple + pull
        sums = jnp.stack([jnp.sum(image * residual, axis=0), jnp.sum(image * image, axis=0)])
        alpha = alpha_of(copies(sums, ("sector", "dof")))
        solution = solution + alpha * precon
        residual = residual - alpha * image
        if step < ITERS - 1:
            change = jnp.dot(precond, whole(image), preferred_element_type=f32)
            precon = precon - alpha * change
    return (solution[None], residual[None])


def body(rhs, *rest):
    rows, loads = rhs.shape[1:]
    cases = loads // lax.axis_size("sector")
    tiled = loads == LANES and (rows // 4) % LANES == 0 and cases % 16 == 0
    return (tiled_body if tiled else plain_body)(rhs, *rest)


def solution(mesh):
    placed = (
        P("sector", "dof", None),
        P("sector", "dof"),
        P("sector", "dof", None),
        P("sector", "dof"),
        P("dof", None),
        P("dof", None),
    )
    return jax.shard_map(
        body,
        mesh=mesh,
        in_specs=placed,
        out_specs=(P("sector", "dof", None), P("sector", "dof", None)),
        check_vma=False,
    )
```

```python
import functools

import jax
import jax.numpy as jnp
from jax import lax
from jax.experimental import pallas as pl
from jax.experimental.pallas import tpu as pltpu
from jax.sharding import PartitionSpec as P

ITERS = 3
LANES = 128
MIB = 1024 * 1024
SUM_ROWS = 8
TERM_ROWS = 16
f32 = jnp.float32
bf16 = jnp.bfloat16


def shape(*dims, dtype=f32):
    return jax.ShapeDtypeStruct(dims, dtype)


def call(kernel, outs, operands, flops=0):
    whole = pl.BlockSpec(memory_space=pltpu.VMEM)
    return pl.pallas_call(
        kernel,
        in_specs=[whole] * len(operands),
        out_specs=jax.tree.map(lambda _: whole, outs),
        out_shape=outs,
        compiler_params=pltpu.CompilerParams(vmem_limit_bytes=20 * MIB),
        cost_estimate=pl.CostEstimate(
            flops=flops, bytes_accessed=sum(x.size * x.dtype.itemsize for x in operands), transcendentals=0
        ),
    )(*operands)


def in_terms(sums):
    terms = None
    for at in range(3):
        term = sums.astype(bf16).astype(f32)
        sums = sums - term
        terms = term if at == 0 else terms + pltpu.roll(term, 2 * at, 0)
    return jnp.concatenate([terms, jnp.zeros_like(terms)], axis=0)


def from_terms(terms):
    terms = terms[:SUM_ROWS].astype(f32)
    sums = terms + pltpu.roll(terms, SUM_ROWS - 2, 0) + pltpu.roll(terms, SUM_ROWS - 4, 0)
    return jnp.where(lax.broadcasted_iota(jnp.int32, sums.shape, 0) < 2, sums, 0.0)


def product_kernel(parts, matrix_ref, springs_ref, tops_ref, *refs):
    *refs, out_ref, load_ref, right_ref, left_ref = refs
    here = lax.axis_index("dof")
    _, top, _ = tops_ref.shape
    for part in range(parts):
        end_ref = refs[part]
        end = end_ref.shape[0]
        start = part * (top + end)
        owner = lax.rem(here + part, parts)
        product = jnp.dot(
            matrix_ref[:, start : start + top], tops_ref[part], preferred_element_type=f32
        ) + jnp.dot(
            matrix_ref[:, pl.ds(pl.multiple_of(owner * (top + end) + top, LANES), end)],
            end_ref[...],
            preferred_element_type=f32,
        )
        if part:
            out_ref[...] += product
        else:
            out_ref[...] = product

    sectors, height, _ = load_ref.shape
    cases = out_ref.shape[1] // sectors
    quarter = right_ref.shape[0]
    left_ref[...] = out_ref[:quarter].astype(bf16)
    right_ref[...] = out_ref[quarter : 2 * quarter].astype(bf16)
    for at in range((height - TERM_ROWS) // cases):
        rows = slice(at * LANES, (at + 1) * LANES)
        turned = (out_ref[rows].T * springs_ref[:, rows]).astype(load_ref.dtype)
        for s in range(sectors):
            load_ref[s, at * cases : (at + 1) * cases] = turned[s * cases : (s + 1) * cases]
    terms = in_terms(refs[parts][...]) if refs[parts:] else jnp.zeros((TERM_ROWS, LANES), f32)
    for s in range(sectors):
        load_ref[s, height - TERM_ROWS :] = terms.astype(load_ref.dtype)


def join_kernel(before_ref, after_ref, *refs):
    out_ref = refs[-1]
    quarter = before_ref.shape[0]
    out_ref[:quarter] = before_ref[...]
    out_ref[quarter:] = after_ref[...]


def slice_kernel(*refs):
    *part_refs, out_ref = refs
    height = out_ref.shape[0] - TERM_ROWS
    total = sum(ref[...].astype(f32) for ref in part_refs)
    out_ref[:height] = total[:height].astype(bf16)
    out_ref[height:] = in_terms(from_terms(total[height:])).astype(bf16)


def alpha_from(sums):
    return sums[0:1] / (sums[1:2] + 1e-06)


def block_columns(matrix_ref, parts, ahead):
    width = matrix_ref.shape[1] // parts
    owner = lax.rem(lax.axis_index("dof") + ahead, parts)
    return matrix_ref[:, pl.ds(pl.multiple_of(owner * width, LANES), width)]


def hub_kernel(cases, matrix_ref, *refs):
    *load_refs, out_ref = refs
    parts = len(load_refs)
    chunks = out_ref.shape[0] // cases
    total = None
    for part, ref in enumerate(load_refs):
        load = jnp.concatenate([ref[c * cases : (c + 1) * cases] for c in range(chunks)], axis=1)
        product = lax.dot_general(
            load,
            block_columns(matrix_ref, parts, part),
            (((1,), (1,)), ((), ())),
            preferred_element_type=f32,
        )
        total = product if total is None else total + product
    for c in range(chunks):
        out_ref[c * cases : (c + 1) * cases] = total[:, c * LANES : (c + 1) * LANES].astype(out_ref.dtype)


def base_kernel(first, parts, matrix_ref, product_ref, stiffness_ref, *refs):
    face_refs, load_refs, refs = refs[:parts], refs[parts : 2 * parts], refs[2 * parts :]
    if first:
        base_ref, end_ref, factor_ref = refs
    else:
        *refs, base_ref, end_ref, factor_ref, left_ref, newer_ref, better_ref = refs
        image_ref, residual_ref, precon_ref = refs[:3]
    base_ref[...] = stiffness_ref[...] * product_ref[...]
    for part, ref in enumerate(face_refs):
        base_ref[...] += jnp.dot(
            block_columns(matrix_ref, parts, part), ref[...], preferred_element_type=f32
        )
    if first:
        factor_ref[...] = jnp.ones_like(factor_ref)
    else:
        alpha = alpha_from(sum(from_terms(ref[ref.shape[0] - TERM_ROWS :]) for ref in load_refs))
        factor_ref[...] = jnp.broadcast_to(-alpha, factor_ref.shape)
        base_ref[...] = image_ref[...] - alpha * base_ref[...]
        left_ref[...] = residual_ref[...] - alpha * image_ref[...]
        gain = alpha * precon_ref[...]
        better_ref[...] = refs[3][...] + gain if len(refs) > 3 else gain
        newer_ref[...] = precon_ref[...] - alpha * product_ref[...]
    end_ref[...] = base_ref[base_ref.shape[0] - end_ref.shape[0] :].astype(bf16)


def image_kernel(sectors, base_ref, springs_ref, factor_ref, residual_ref, *refs):
    *hub_refs, image_ref, top_ref, sums_ref, hubs_ref = refs
    here = lax.axis_index("sector")
    for ahead in range(sectors):
        hubs_ref[lax.rem(here + ahead, sectors)] = hub_refs[ahead][...].astype(f32)
    attached = top_ref.shape[0]
    chunks = attached // LANES
    cases = hubs_ref.shape[1] // chunks
    factor = factor_ref[0:1]
    for c in range(chunks):
        at = slice(c * LANES, (c + 1) * LANES)
        hub = jnp.concatenate([hubs_ref[s, c * cases : (c + 1) * cases] for s in range(sectors)], axis=0)
        image = base_ref[at] - factor * (hub * springs_ref[:, at]).T
        image_ref[at] = image
        top_ref[at] = image.astype(bf16)
    image_ref[attached:] = base_ref[attached:]
    image = image_ref[...]
    upper = jnp.sum(image * residual_ref[...], axis=0, keepdims=True)
    lower = jnp.sum(image * image, axis=0, keepdims=True)
    rest = jnp.zeros((SUM_ROWS - 2, image.shape[1]), f32)
    sums = jnp.concatenate([upper, lower, rest], axis=0)
    sums_ref[...] = jnp.broadcast_to(sums[: sums_ref.shape[-2]], sums_ref.shape)


def last_kernel(sums_ref, image_ref, residual_ref, precon_ref, solution_ref, newer_ref, left_ref):
    alpha = alpha_from(jnp.sum(sums_ref[...], axis=0))
    newer_ref[0] = solution_ref[...] + alpha * precon_ref[...]
    left_ref[0] = residual_ref[...] - alpha * image_ref[...]


def last_update(sums, *state):
    rows, loads = state[0].shape
    height = rows // 4
    block = pl.BlockSpec((height, loads), lambda k: (k, 0))
    out_block = pl.BlockSpec((1, height, loads), lambda k: (0, k, 0))
    out = shape(1, rows, loads)
    return pl.pallas_call(
        last_kernel,
        grid=(4,),
        in_specs=[pl.BlockSpec(sums.shape, lambda k: (0, 0, 0))] + [block] * len(state),
        out_specs=(out_block, out_block),
        out_shape=(out, out),
        compiler_params=pltpu.CompilerParams(vmem_limit_bytes=60 * MIB),
    )(sums, *state)


def round_kernel(field_ref, top_ref, end_ref):
    attached = top_ref.shape[0]
    top_ref[...] = field_ref[0, :attached].astype(bf16)
    end_ref[...] = field_ref[0, attached:].astype(bf16)


def stiffness_kernel(diagonal_ref, springs_ref, out_ref):
    for start in range(0, out_ref.shape[0], LANES):
        rows = slice(start, start + LANES)
        row = diagonal_ref[:, rows]
        if start < springs_ref.shape[1]:
            row = row + springs_ref[:, rows]
        out_ref[rows] = jnp.broadcast_to(row, (LANES, LANES)).T


def exchange(blocks, axes):
    return lax.all_to_all(blocks, axes, split_axis=0, concat_axis=0)


def from_ahead(cells, axis, distance):
    count = lax.axis_size(axis)
    return lax.ppermute(cells, axis, [((i + distance) % count, i) for i in range(count)])


def one_from_each(cells, axis):
    return [cells] + [from_ahead(cells, axis, d) for d in range(1, lax.axis_size(axis))]


def mine_from_each(blocks, axis):
    count, here = lax.axis_size(axis), lax.axis_index(axis)
    own = [lax.dynamic_index_in_dim(blocks, (here - d) % count, 0, False) for d in range(count)]
    return own[:1] + [from_ahead(own[d], axis, d) for d in range(1, count)]


def gathered(field):
    return lax.all_gather(field, "dof", axis=0)


def around(sectors):
    onward = [(s, (s + 1) % sectors) for s in range(sectors)]
    return onward, [(b, a) for a, b in onward]


def alpha_of(sums):
    return alpha_from(jnp.sum(sums, axis=0))[0]


def tiled_body(rhs, diagonal, coupling, springs, precond, hub_inverse):
    residual = rhs[0]
    rows, loads = residual.shape
    attached = springs.shape[1]
    quarter = rows - attached
    sectors, parts = lax.axis_size("sector"), lax.axis_size("dof")
    cases = loads // sectors
    height = attached // LANES * cases
    onward, backward = around(sectors)
    full, face = shape(rows, loads), shape(quarter, loads, dtype=bf16)
    top_shape = shape(attached, loads, dtype=bf16)

    state = sums = ()

    top, end = call(round_kernel, (top_shape, face), (rhs,))
    stiffness = call(stiffness_kernel, full, (diagonal, springs))
    for step in range(ITERS):
        first, last = step == 0, step == ITERS - 1
        sent = f32 if first else bf16
        product, load, right, left = call(
            functools.partial(product_kernel, parts),
            (full, shape(sectors, height + TERM_ROWS, LANES, dtype=sent), face, face),
            (precond, springs, gathered(top), *one_from_each(end, "dof"), *sums),
            flops=2 * precond.size * loads,
        )
        before = lax.ppermute(right, "sector", onward)
        after = lax.ppermute(left, "sector", backward)
        load = call(
            slice_kernel,
            shape(height + TERM_ROWS, loads, dtype=bf16),
            mine_from_each(load, "sector"),
        )
        slices = one_from_each(load, "dof")
        faces = call(join_kernel, shape(2 * quarter, loads, dtype=bf16), (before, after, *slices[1:]))
        faces = one_from_each(faces, "dof")
        hub = call(
            functools.partial(hub_kernel, cases),
            shape(height, LANES, dtype=sent),
            (hub_inverse, *slices),
            flops=2 * hub_inverse.size * cases,
        )
        hubs = one_from_each(hub, "sector")
        base, end, factor, *state = call(
            functools.partial(base_kernel, first, parts),
            (full, face, shape(SUM_ROWS, loads)) + (() if first else (full, full, full)),
            (coupling[0], product, stiffness, *faces, *slices, *state),
            flops=2 * coupling.size * loads,
        )
        residual, precon, *solution = (residual, product) if first else state
        sums_shape = shape(sectors * parts, 2, loads) if last else shape(SUM_ROWS, loads)
        image, top, sums, _ = call(
            functools.partial(image_kernel, sectors),
            (full, top_shape, sums_shape, shape(sectors, height, LANES)),
            (base, springs, factor, residual, *hubs),
        )
        state = (image, residual, precon, *solution)
        sums = (sums,)
    out = shape(1, rows, loads)
    return call(last_kernel, (out, out), (exchange(*sums, ("sector", "dof")), *state))


def plain_body(rhs, diagonal, coupling, springs, precond, hub_inverse):
    residual = rhs[0]
    spring_rows = springs[0][:, None]
    rows, loads = residual.shape
    quarter = rows // 4
    sectors = lax.axis_size("sector")
    onward, backward = around(sectors)
    solution = jnp.zeros_like(residual)

    def whole(field):
        return gathered(field.astype(bf16)).reshape(-1, loads)

    def copies(cells, axes):
        count = lax.axis_size(axes)
        return exchange(jnp.broadcast_to(cells[None], (count,) + cells.shape), axes)

    precon = jnp.dot(precond, whole(residual), preferred_element_type=f32)
    for step in range(ITERS):
        faces = precon[: 2 * quarter].astype(bf16)
        before = lax.ppermute(faces[quarter:], "sector", onward)
        after = lax.ppermute(faces[:quarter], "sector", backward)
        couple = jnp.dot(
            coupling[0], whole(jnp.concatenate([before, after])), preferred_element_type=f32
        )
        attached = precon[: 3 * quarter]
        load = (spring_rows * attached).T.reshape(sectors, loads // sectors, -1)
        load = jnp.sum(exchange(load, "sector"), axis=0).astype(bf16)
        load = copies(load, "dof").transpose(0, 2, 1).reshape(hub_inverse.shape[1], -1)
        hub = jnp.dot(hub_inverse, load, preferred_element_type=f32)
        hub = copies(hub.T, "sector").reshape(loads, -1).T
        pull = jnp.pad(spring_rows * (attached - hub), ((0, quarter), (0, 0)))
        image = diagonal[0][:, None] * precon + couple + pull
        sums = jnp.stack([jnp.sum(image * residual, axis=0), jnp.sum(image * image, axis=0)])
        alpha = alpha_of(copies(sums, ("sector", "dof")))
        solution = solution + alpha * precon
        residual = residual - alpha * image
        if step < ITERS - 1:
            change = jnp.dot(precond, whole(image), preferred_element_type=f32)
            precon = precon - alpha * change
    return (solution[None], residual[None])


def body(rhs, *rest):
    rows, loads = rhs.shape[1:]
    cases = loads // lax.axis_size("sector")
    tiled = loads == LANES and (rows // 4) % LANES == 0 and cases % 16 == 0
    return (tiled_body if tiled else plain_body)(rhs, *rest)


def solution(mesh):
    placed = (
        P("sector", "dof", None),
        P("sector", "dof"),
        P("sector", "dof", None),
        P("sector", "dof"),
        P("dof", None),
        P("dof", None),
    )
    return jax.shard_map(
        body,
        mesh=mesh,
        in_specs=placed,
        out_specs=(P("sector", "dof", None), P("sector", "dof", None)),
        check_vma=False,
    )
```

```python
import functools

import jax
import jax.numpy as jnp
from jax import lax
from jax.experimental import pallas as pl
from jax.experimental.pallas import tpu as pltpu
from jax.sharding import PartitionSpec as P

ITERS = 3
LANES = 128
MIB = 1024 * 1024
SUM_ROWS = 8
TERM_ROWS = 16
f32 = jnp.float32
bf16 = jnp.bfloat16


def shape(*dims, dtype=f32):
    return jax.ShapeDtypeStruct(dims, dtype)


def call(kernel, outs, operands, flops=0):
    whole = pl.BlockSpec(memory_space=pltpu.VMEM)
    return pl.pallas_call(
        kernel,
        in_specs=[whole] * len(operands),
        out_specs=jax.tree.map(lambda _: whole, outs),
        out_shape=outs,
        compiler_params=pltpu.CompilerParams(vmem_limit_bytes=20 * MIB),
        cost_estimate=pl.CostEstimate(
            flops=flops, bytes_accessed=sum(x.size * x.dtype.itemsize for x in operands), transcendentals=0
        ),
    )(*operands)


def in_terms(sums):
    terms = None
    for at in range(3):
        term = sums.astype(bf16).astype(f32)
        sums = sums - term
        terms = term if at == 0 else terms + pltpu.roll(term, 2 * at, 0)
    return jnp.concatenate([terms, jnp.zeros_like(terms)], axis=0)


def from_terms(terms):
    terms = terms[:SUM_ROWS].astype(f32)
    sums = terms + pltpu.roll(terms, SUM_ROWS - 2, 0) + pltpu.roll(terms, SUM_ROWS - 4, 0)
    return jnp.where(lax.broadcasted_iota(jnp.int32, sums.shape, 0) < 2, sums, 0.0)


def product_kernel(parts, matrix_ref, springs_ref, tops_ref, *refs):
    *refs, out_ref, load_ref, right_ref, left_ref = refs
    here = lax.axis_index("dof")
    _, top, _ = tops_ref.shape
    for part in range(parts):
        end_ref = refs[part]
        end = end_ref.shape[0]
        start = part * (top + end)
        owner = lax.rem(here + part, parts)
        product = jnp.dot(
            matrix_ref[:, start : start + top], tops_ref[part], preferred_element_type=f32
        ) + jnp.dot(
            matrix_ref[:, pl.ds(pl.multiple_of(owner * (top + end) + top, LANES), end)],
            end_ref[...],
            preferred_element_type=f32,
        )
        if part:
            out_ref[...] += product
        else:
            out_ref[...] = product

    sectors, height, _ = load_ref.shape
    cases = out_ref.shape[1] // sectors
    quarter = right_ref.shape[0]
    left_ref[...] = out_ref[:quarter].astype(bf16)
    right_ref[...] = out_ref[quarter : 2 * quarter].astype(bf16)
    for at in range((height - TERM_ROWS) // cases):
        rows = slice(at * LANES, (at + 1) * LANES)
        turned = (out_ref[rows].T * springs_ref[:, rows]).astype(load_ref.dtype)
        for s in range(sectors):
            load_ref[s, at * cases : (at + 1) * cases] = turned[s * cases : (s + 1) * cases]
    terms = in_terms(refs[parts][...]) if refs[parts:] else jnp.zeros((TERM_ROWS, LANES), f32)
    for s in range(sectors):
        load_ref[s, height - TERM_ROWS :] = terms.astype(load_ref.dtype)


def join_kernel(before_ref, after_ref, *refs):
    out_ref = refs[-1]
    quarter = before_ref.shape[0]
    out_ref[:quarter] = before_ref[...]
    out_ref[quarter:] = after_ref[...]


def slice_kernel(right_ref, left_ref, *refs):
    *part_refs, out_ref, right_out, left_out = refs
    right_out[...] = right_ref[...]
    left_out[...] = left_ref[...]
    height = out_ref.shape[0] - TERM_ROWS
    total = sum(ref[...].astype(f32) for ref in part_refs)
    out_ref[:height] = total[:height].astype(bf16)
    out_ref[height:] = in_terms(from_terms(total[height:])).astype(bf16)


def alpha_from(sums):
    return sums[0:1] / (sums[1:2] + 1e-06)


def block_columns(matrix_ref, parts, ahead):
    width = matrix_ref.shape[1] // parts
    owner = lax.rem(lax.axis_index("dof") + ahead, parts)
    return matrix_ref[:, pl.ds(pl.multiple_of(owner * width, LANES), width)]


def hub_kernel(cases, matrix_ref, *refs):
    *load_refs, out_ref = refs
    parts = len(load_refs)
    chunks = out_ref.shape[0] // cases
    total = None
    for part, ref in enumerate(load_refs):
        load = jnp.concatenate([ref[c * cases : (c + 1) * cases] for c in range(chunks)], axis=1)
        product = lax.dot_general(
            load,
            block_columns(matrix_ref, parts, part),
            (((1,), (1,)), ((), ())),
            preferred_element_type=f32,
        )
        total = product if total is None else total + product
    for c in range(chunks):
        out_ref[c * cases : (c + 1) * cases] = total[:, c * LANES : (c + 1) * LANES].astype(out_ref.dtype)


def base_kernel(first, parts, matrix_ref, product_ref, stiffness_ref, *refs):
    face_refs, load_refs, refs = refs[:parts], refs[parts : 2 * parts], refs[2 * parts :]
    if first:
        base_ref, end_ref, factor_ref = refs
    else:
        *refs, base_ref, end_ref, factor_ref, left_ref, newer_ref, better_ref = refs
        image_ref, residual_ref, precon_ref = refs[:3]
    base_ref[...] = stiffness_ref[...] * product_ref[...]
    for part, ref in enumerate(face_refs):
        base_ref[...] += jnp.dot(
            block_columns(matrix_ref, parts, part), ref[...], preferred_element_type=f32
        )
    if first:
        factor_ref[...] = jnp.ones_like(factor_ref)
    else:
        alpha = alpha_from(sum(from_terms(ref[ref.shape[0] - TERM_ROWS :]) for ref in load_refs))
        factor_ref[...] = jnp.broadcast_to(-alpha, factor_ref.shape)
        base_ref[...] = image_ref[...] - alpha * base_ref[...]
        left_ref[...] = residual_ref[...] - alpha * image_ref[...]
        gain = alpha * precon_ref[...]
        better_ref[...] = refs[3][...] + gain if len(refs) > 3 else gain
        newer_ref[...] = precon_ref[...] - alpha * product_ref[...]
    end_ref[...] = base_ref[base_ref.shape[0] - end_ref.shape[0] :].astype(bf16)


def image_kernel(sectors, base_ref, springs_ref, factor_ref, residual_ref, *refs):
    *hub_refs, image_ref, top_ref, sums_ref, hubs_ref = refs
    here = lax.axis_index("sector")
    for ahead in range(sectors):
        hubs_ref[lax.rem(here + ahead, sectors)] = hub_refs[ahead][...].astype(f32)
    attached = top_ref.shape[0]
    chunks = attached // LANES
    cases = hubs_ref.shape[1] // chunks
    factor = factor_ref[0:1]
    for c in range(chunks):
        at = slice(c * LANES, (c + 1) * LANES)
        hub = jnp.concatenate([hubs_ref[s, c * cases : (c + 1) * cases] for s in range(sectors)], axis=0)
        image = base_ref[at] - factor * (hub * springs_ref[:, at]).T
        image_ref[at] = image
        top_ref[at] = image.astype(bf16)
    image_ref[attached:] = base_ref[attached:]
    image = image_ref[...]
    upper = jnp.sum(image * residual_ref[...], axis=0, keepdims=True)
    lower = jnp.sum(image * image, axis=0, keepdims=True)
    rest = jnp.zeros((SUM_ROWS - 2, image.shape[1]), f32)
    sums = jnp.concatenate([upper, lower, rest], axis=0)
    sums_ref[...] = jnp.broadcast_to(sums[: sums_ref.shape[-2]], sums_ref.shape)


def last_kernel(sums_ref, image_ref, residual_ref, precon_ref, solution_ref, newer_ref, left_ref):
    alpha = alpha_from(jnp.sum(sums_ref[...], axis=0))
    newer_ref[0] = solution_ref[...] + alpha * precon_ref[...]
    left_ref[0] = residual_ref[...] - alpha * image_ref[...]


def last_update(sums, *state):
    rows, loads = state[0].shape
    height = rows // 4
    block = pl.BlockSpec((height, loads), lambda k: (k, 0))
    out_block = pl.BlockSpec((1, height, loads), lambda k: (0, k, 0))
    out = shape(1, rows, loads)
    return pl.pallas_call(
        last_kernel,
        grid=(4,),
        in_specs=[pl.BlockSpec(sums.shape, lambda k: (0, 0, 0))] + [block] * len(state),
        out_specs=(out_block, out_block),
        out_shape=(out, out),
        compiler_params=pltpu.CompilerParams(vmem_limit_bytes=60 * MIB),
    )(sums, *state)


def round_kernel(field_ref, top_ref, end_ref):
    attached = top_ref.shape[0]
    top_ref[...] = field_ref[0, :attached].astype(bf16)
    end_ref[...] = field_ref[0, attached:].astype(bf16)


def stiffness_kernel(diagonal_ref, springs_ref, out_ref):
    for start in range(0, out_ref.shape[0], LANES):
        rows = slice(start, start + LANES)
        row = diagonal_ref[:, rows]
        if start < springs_ref.shape[1]:
            row = row + springs_ref[:, rows]
        out_ref[rows] = jnp.broadcast_to(row, (LANES, LANES)).T


def exchange(blocks, axes):
    return lax.all_to_all(blocks, axes, split_axis=0, concat_axis=0)


def from_ahead(cells, axis, distance):
    count = lax.axis_size(axis)
    return lax.ppermute(cells, axis, [((i + distance) % count, i) for i in range(count)])


def one_from_each(cells, axis):
    return [cells] + [from_ahead(cells, axis, d) for d in range(1, lax.axis_size(axis))]


def mine_from_each(blocks, axis):
    count, here = lax.axis_size(axis), lax.axis_index(axis)
    own = [lax.dynamic_index_in_dim(blocks, (here - d) % count, 0, False) for d in range(count)]
    return own[:1] + [from_ahead(own[d], axis, d) for d in range(1, count)]


def gathered(field):
    return lax.all_gather(field, "dof", axis=0)


def around(sectors):
    onward = [(s, (s + 1) % sectors) for s in range(sectors)]
    return onward, [(b, a) for a, b in onward]


def alpha_of(sums):
    return alpha_from(jnp.sum(sums, axis=0))[0]


def tiled_body(rhs, diagonal, coupling, springs, precond, hub_inverse):
    residual = rhs[0]
    rows, loads = residual.shape
    attached = springs.shape[1]
    quarter = rows - attached
    sectors, parts = lax.axis_size("sector"), lax.axis_size("dof")
    cases = loads // sectors
    height = attached // LANES * cases
    onward, backward = around(sectors)
    full, face = shape(rows, loads), shape(quarter, loads, dtype=bf16)
    top_shape = shape(attached, loads, dtype=bf16)

    state = sums = ()

    top, end = call(round_kernel, (top_shape, face), (rhs,))
    stiffness = call(stiffness_kernel, full, (diagonal, springs))
    for step in range(ITERS):
        first, last = step == 0, step == ITERS - 1
        sent = f32 if first else bf16
        product, load, right, left = call(
            functools.partial(product_kernel, parts),
            (full, shape(sectors, height + TERM_ROWS, LANES, dtype=sent), face, face),
            (precond, springs, gathered(top), *one_from_each(end, "dof"), *sums),
            flops=2 * precond.size * loads,
        )
        load, right, left = call(
            slice_kernel,
            (shape(height + TERM_ROWS, loads, dtype=bf16), face, face),
            (right, left, *mine_from_each(load, "sector")),
        )
        before = lax.ppermute(right, "sector", onward)
        after = lax.ppermute(left, "sector", backward)
        slices = one_from_each(load, "dof")
        faces = call(join_kernel, shape(2 * quarter, loads, dtype=bf16), (before, after, *slices[1:]))
        faces = one_from_each(faces, "dof")
        hub = call(
            functools.partial(hub_kernel, cases),
            shape(height, LANES, dtype=sent),
            (hub_inverse, *slices),
            flops=2 * hub_inverse.size * cases,
        )
        hubs = one_from_each(hub, "sector")
        base, end, factor, *state = call(
            functools.partial(base_kernel, first, parts),
            (full, face, shape(SUM_ROWS, loads)) + (() if first else (full, full, full)),
            (coupling[0], product, stiffness, *faces, *slices, *state),
            flops=2 * coupling.size * loads,
        )
        residual, precon, *solution = (residual, product) if first else state
        sums_shape = shape(sectors * parts, 2, loads) if last else shape(SUM_ROWS, loads)
        image, top, sums, _ = call(
            functools.partial(image_kernel, sectors),
            (full, top_shape, sums_shape, shape(sectors, height, LANES)),
            (base, springs, factor, residual, *hubs),
        )
        state = (image, residual, precon, *solution)
        sums = (sums,)
    out = shape(1, rows, loads)
    return call(last_kernel, (out, out), (exchange(*sums, ("sector", "dof")), *state))


def plain_body(rhs, diagonal, coupling, springs, precond, hub_inverse):
    residual = rhs[0]
    spring_rows = springs[0][:, None]
    rows, loads = residual.shape
    quarter = rows // 4
    sectors = lax.axis_size("sector")
    onward, backward = around(sectors)
    solution = jnp.zeros_like(residual)

    def whole(field):
        return gathered(field.astype(bf16)).reshape(-1, loads)

    def copies(cells, axes):
        count = lax.axis_size(axes)
        return exchange(jnp.broadcast_to(cells[None], (count,) + cells.shape), axes)

    precon = jnp.dot(precond, whole(residual), preferred_element_type=f32)
    for step in range(ITERS):
        faces = precon[: 2 * quarter].astype(bf16)
        before = lax.ppermute(faces[quarter:], "sector", onward)
        after = lax.ppermute(faces[:quarter], "sector", backward)
        couple = jnp.dot(
            coupling[0], whole(jnp.concatenate([before, after])), preferred_element_type=f32
        )
        attached = precon[: 3 * quarter]
        load = (spring_rows * attached).T.reshape(sectors, loads // sectors, -1)
        load = jnp.sum(exchange(load, "sector"), axis=0).astype(bf16)
        load = copies(load, "dof").transpose(0, 2, 1).reshape(hub_inverse.shape[1], -1)
        hub = jnp.dot(hub_inverse, load, preferred_element_type=f32)
        hub = copies(hub.T, "sector").reshape(loads, -1).T
        pull = jnp.pad(spring_rows * (attached - hub), ((0, quarter), (0, 0)))
        image = diagonal[0][:, None] * precon + couple + pull
        sums = jnp.stack([jnp.sum(image * residual, axis=0), jnp.sum(image * image, axis=0)])
        alpha = alpha_of(copies(sums, ("sector", "dof")))
        solution = solution + alpha * precon
        residual = residual - alpha * image
        if step < ITERS - 1:
            change = jnp.dot(precond, whole(image), preferred_element_type=f32)
            precon = precon - alpha * change
    return (solution[None], residual[None])


def body(rhs, *rest):
    rows, loads = rhs.shape[1:]
    cases = loads // lax.axis_size("sector")
    tiled = loads == LANES and (rows // 4) % LANES == 0 and cases % 16 == 0
    return (tiled_body if tiled else plain_body)(rhs, *rest)


def solution(mesh):
    placed = (
        P("sector", "dof", None),
        P("sector", "dof"),
        P("sector", "dof", None),
        P("sector", "dof"),
        P("dof", None),
        P("dof", None),
    )
    return jax.shard_map(
        body,
        mesh=mesh,
        in_specs=placed,
        out_specs=(P("sector", "dof", None), P("sector", "dof", None)),
        check_vma=False,
    )
```
